32 devices in a mesh: section: 2 (over y), dp: 16 (over z, x, core).
Axes of the slice: x: 2, y: 2, z: 4, core: 2. Of those that a mesh axis runs over, the one named last changes fastest.
Arguments:
- tokens: bfloat16 [8192, 768], P('dp'), may hold values from -6 to 6
- images: bfloat16 [64, 576, 768], P('dp'), may hold values from -6 to 6
- segments: int32 [128, 64], P('dp'), may hold values from 0 to 2, never falling along the last dimension, each value on 1 to 40 neighbouring positions
- image_ids: int32 [128, 3], P('dp'), may hold values from 0 to 1
- cotangent: bfloat16 [2, 8192, 768], P('section', 'dp'), may hold values from -6 to 6
- norm_gain: float32 [2, 2, 768], P('section', None, 'dp'), may hold values from 0.5 to 1.5
- norm_bias: float32 [2, 2, 768], P('section', None, 'dp'), may hold values from -2 to 2
- qkv_weight: float32 [2, 768, 2304], P('section', 'dp'), may hold values from -0.21875 to 0.21875
- out_weight: float32 [2, 768, 768], P('section', 'dp'), may hold values from -0.625 to 0.625
- up_weight: float32 [2, 768, 3072], P('section', 'dp'), may hold values from -0.21875 to 0.21875
- down_weight: float32 [2, 3072, 768], P('section', 'dp'), may hold values from -0.109375 to 0.109375
- cross_gain: float32 [768], P(('section', 'dp')), may hold values from 0.5 to 1.5
- cross_bias: float32 [768], P(('section', 'dp')), may hold values from -2 to 2
- cross_query: float32 [768, 768], P(('section', 'dp')), may hold values from -0.21875 to 0.21875
- cross_kv: float32 [768, 1536], P(('section', 'dp')), may hold values from -0.21875 to 0.21875
- cross_out: float32 [768, 768], P(('section', 'dp')), may hold values from -1.75 to 1.75
Outputs:
- layer_out: bfloat16 [2, 8192, 768], P('section', 'dp')
- input_grad: float32 [2, 8192, 768], P('section', 'dp')
- image_grad: float32 [64, 576, 768], P('dp', None, 'section')
- norm_gain_grad: float32 [2, 2, 768], P('section', None, 'dp')
- norm_bias_grad: float32 [2, 2, 768], P('section', None, 'dp')
- qkv_weight_grad: float32 [2, 768, 2304], P('section', 'dp')
- out_weight_grad: float32 [2, 768, 768], P('section', 'dp')
- up_weight_grad: float32 [2, 768, 3072], P('section', 'dp')
- down_weight_grad: float32 [2, 3072, 768], P('section', 'dp')
- cross_gain_grad: float32 [768], P(('section', 'dp'))
- cross_bias_grad: float32 [768], P(('section', 'dp'))
- cross_query_grad: float32 [768, 768], P(('section', 'dp'))
- cross_kv_grad: float32 [768, 1536], P(('section', 'dp'))
- cross_out_grad: float32 [768, 768], P(('section', 'dp'))
The draws below stay inside these ranges and needn't reach their ends.
Inputs may be any that keep to these rules, and one draw needn't show every extreme that they name: `segments`: within a row the caption numbers never fall; each of the 3 captions has 1 to 40 tokens. `image_ids`: the image of caption s of a row, counted among the 2 images of that row's block: rows k * 4 to (k + 1) * 4 - 1 use images k * 2 onward.
All inputs are finite; a program needn't handle non-finite values.
Results may differ from the reference program's by a relative error of at most 0.025.
Values may be sent and summed in bfloat16 or wider, within the bound.
No kernel may reach another device: no remote copies, remote signals or barrier semaphores. Data moves between devices by JAX's collectives and lax.ppermute only.
A program may use at most 256 MiB of HBM per device.

```python
import math
from functools import partial
import jax
import jax.numpy as jnp
import numpy as np
from jax import lax

HEADS = 12
HEAD_DIM = 64
FF = 3072
PATCHES = 576
ROW_LEN = 64
SEGS = 3
SEG_MOST = 40
IMG_MB = 2
ROWS_MB = 4
D = 768
ROWS = 128
TOKENS = 8192
IMAGES = 64


def place_ends(values, key, least, high):
    dims = values.shape
    place = [jax.random.randint(jax.random.fold_in(key, axis), (), 0, dims[axis]) for axis in range(len(dims))]
    values = values.at[tuple(place)].set(least)
    longest = dims.index(max(dims))
    place[longest] = (place[longest] + 1) % dims[longest]
    return values.at[tuple(place)].set(high)


def levels(rng, shape, cuts, smallest, high):
    loudness = 1.0
    for dim, shards_of in cuts:
        heights = jax.random.uniform(jax.random.fold_in(jax.random.fold_in(rng, 6), dim), (shards_of,), jnp.float32, smallest / len(cuts), high / len(cuts))
        loudness = loudness * jnp.repeat(jnp.exp(heights), shape[dim] // shards_of).reshape((-1,) + (1,) * (len(shape) - 1 - dim))
    return loudness


def profile(number_of, total, most, skew):
    weights = [(1 << 20) // math.isqrt(standing ** skew) + 1 for standing in range(2, number_of + 1)]
    surplus, counts = total - most - (number_of - 1), [1] * (number_of - 1)
    while surplus > 0:
        candidates = [i for i in range(number_of - 1) if counts[i] < most]
        mass, remaining = sum([weights[i] for i in candidates]), surplus
        for i in candidates:
            extra = min(most - counts[i], max(1, remaining * weights[i] // mass), surplus)
            counts[i] = counts[i] + extra
            surplus = surplus - extra
    return np.array([most] + counts)


def uneven_parts(rng, amount, total, bound, slope):
    if amount == 2:
        one = jax.random.randint(rng, (), max(1, total - bound), min(bound, total - 1) + 1)
        return jnp.stack([one, total - one])
    lengths = jnp.asarray(profile(amount, total, bound, slope), jnp.int32)
    pairs = (amount - 1) // 2
    source_of, sink = lengths[1:1 + 2 * pairs:2], lengths[2:2 + 2 * pairs:2]
    slack = jnp.minimum(source_of - 1, bound - sink)
    shifted = jax.random.randint(jax.random.fold_in(rng, 1), (pairs,), 0, 1 << 20) % (slack + 1)
    lengths = lengths.at[1:1 + 2 * pairs:2].set(source_of - shifted).at[2:2 + 2 * pairs:2].set(sink + shifted)
    return lengths[jax.random.permutation(jax.random.fold_in(rng, 2), amount)]


def scatter_about(key, shape, scale, bound, cuts=(), dtype=jnp.bfloat16):
    drawn = scale * jax.random.normal(key, shape, jnp.float32)
    if cuts:
        drawn = drawn * levels(key, shape, cuts, -0.22, 0.18)
    return jnp.clip(drawn, -bound, bound).astype(dtype)


def setup_inputs(seed: int = 0) -> dict:
    arg_keys = jax.random.split(jax.random.key(seed), 17)
    return {
        "tokens": scatter_about(arg_keys[0], (TOKENS, D), 1.0, 6.0, ((0, 16),)),
        "images": scatter_about(arg_keys[1], (IMAGES, PATCHES, D), 1.0, 6.0, ((0, 16),)),
        "segments": jax.vmap(lambda own: jnp.searchsorted(jnp.cumsum(uneven_parts(own, SEGS, ROW_LEN, SEG_MOST, 1)), jnp.arange(ROW_LEN), side="right"))(jax.random.split(arg_keys[2], ROWS)).reshape((ROWS, ROW_LEN)).astype(jnp.int32),
        "image_ids": place_ends(jax.random.randint(arg_keys[3], (ROWS, SEGS), 0, IMG_MB), jax.random.fold_in(arg_keys[3], 1), 0, IMG_MB - 1).astype(jnp.int32),
        "cotangent": scatter_about(arg_keys[4], (2, TOKENS, D), 1.0, 6.0, ((0, 2), (1, 16))),
        "norm_gain": jnp.clip(1.0 + 0.1 * jax.random.normal(arg_keys[5], (2, 2, D), jnp.float32), 0.5, 1.5),
        "norm_bias": scatter_about(arg_keys[6], (2, 2, D), 0.3, 2.0, ((0, 2), (2, 16)), jnp.float32),
        "qkv_weight": scatter_about(arg_keys[7], (2, D, 3 * D), D ** -0.5, 0.21875, ((0, 2), (1, 16)), jnp.float32),
        "out_weight": scatter_about(arg_keys[8], (2, D, D), (D // 8) ** -0.5, 0.625, ((0, 2), (1, 16)), jnp.float32),
        "up_weight": scatter_about(arg_keys[9], (2, D, FF), D ** -0.5, 0.21875, ((0, 2), (1, 16)), jnp.float32),
        "down_weight": scatter_about(arg_keys[10], (2, FF, D), FF ** -0.5, 0.109375, ((0, 2), (1, 16)), jnp.float32),
        "cross_gain": jnp.clip(1.0 + 0.1 * jax.random.normal(arg_keys[11], (D,), jnp.float32), 0.5, 1.5),
        "cross_bias": scatter_about(arg_keys[12], (D,), 0.3, 2.0, ((0, 32),), jnp.float32),
        "cross_query": scatter_about(arg_keys[13], (D, D), D ** -0.5, 0.21875, ((0, 32),), jnp.float32),
        "cross_kv": scatter_about(arg_keys[14], (D, 2 * D), D ** -0.5, 0.21875, ((0, 32),), jnp.float32),
        "cross_out": scatter_about(arg_keys[15], (D, D), (D // 64) ** -0.5, 1.75, ((0, 32),), jnp.float32),
    }


MASKED_SCORE = -1000000000.0
NORM_EPS = 1e-05

@jax.custom_vjp
def low(v):
    return lax.optimization_barrier(v.astype(jnp.bfloat16)).astype(jnp.float32)

@jax.custom_vjp
def low_back(v):
    return v

def low_keep(v):
    return (low(v), None)

def low_pass(kept, grad):
    return (grad,)

def back_keep(v):
    return (v, None)

def back_low(kept, grad):
    return (low(grad),)
low.defvjp(low_keep, low_pass)
low_back.defvjp(back_keep, back_low)

def matmul(left, right):
    return jnp.dot(left, right, precision=lax.Precision.HIGHEST)

def layer_norm(residual, gain_vec, bias_vec):
    average = lax.optimization_barrier(jnp.mean(residual, axis=-1, keepdims=True))
    centred = residual - average
    inv_scale = lax.rsqrt(lax.optimization_barrier(jnp.mean(centred * centred, axis=-1, keepdims=True)) + NORM_EPS)
    return centred * inv_scale * gain_vec + bias_vec

def attend_core(queries, key_heads, value_heads, allowed):
    scores = jnp.einsum('bqhd,bkhd->bhqk', queries, key_heads, precision=lax.Precision.HIGHEST) * HEAD_DIM ** (-0.5)
    scores = low_back(jnp.where(allowed, scores, MASKED_SCORE))
    row_max = lax.optimization_barrier(jnp.max(scores, axis=-1, keepdims=True))
    exponent = jnp.exp(scores - row_max)
    attn_probs = low(exponent / lax.optimization_barrier(jnp.sum(exponent, axis=-1, keepdims=True)))
    return jnp.einsum('bhqk,bkhd->bqhd', attn_probs, value_heads, precision=lax.Precision.HIGHEST)

def self_block(residual, gain_vec, bias_vec, qkv_mat, out_mat, same_doc):
    row_count = same_doc.shape[0]
    hidden = low(layer_norm(residual, gain_vec, bias_vec))
    qkv_heads = low(low_back(matmul(hidden, qkv_mat))).reshape(row_count, ROW_LEN, 3, HEADS, HEAD_DIM)
    mixed_heads = attend_core(qkv_heads[:, :, 0], qkv_heads[:, :, 1], qkv_heads[:, :, 2], same_doc[:, None])
    mixed_flat = low(low_back(mixed_heads.reshape(residual.shape[0], D)))
    return residual + low_back(matmul(mixed_flat, out_mat))

def cross_block(residual, image_block, tied_image, cross_set):
    gain_vec, bias_vec, query_mat, kv_mat, out_mat = cross_set
    hidden = low(layer_norm(residual, gain_vec, bias_vec))
    queries = low(low_back(matmul(hidden, query_mat))).reshape(1, -1, HEADS, HEAD_DIM)
    image_kv = low(low_back(matmul(low(image_block), kv_mat)))
    key_heads = image_kv[:, :D].reshape(1, -1, HEADS, HEAD_DIM)
    value_heads = image_kv[:, D:].reshape(1, -1, HEADS, HEAD_DIM)
    mixed_heads = attend_core(queries, key_heads, value_heads, tied_image[None, None])
    mixed_flat = low(low_back(mixed_heads.reshape(residual.shape[0], D)))
    return residual + low_back(matmul(mixed_flat, out_mat))

def feed_block(residual, gain_vec, bias_vec, up_mat, down_mat):
    hidden = low(layer_norm(residual, gain_vec, bias_vec))
    upward = low_back(matmul(hidden, up_mat))
    activated = low(jax.nn.gelu(upward, approximate=False))
    return residual + low_back(matmul(activated, down_mat))

def block_masks(seg_rows, id_rows):
    position = lax.broadcasted_iota(jnp.int32, (ROW_LEN, ROW_LEN), 0)
    earlier = lax.broadcasted_iota(jnp.int32, (ROW_LEN, ROW_LEN), 1) <= position
    same_doc = (seg_rows[:, :, None] == seg_rows[:, None, :]) & earlier[None]
    slots = lax.broadcasted_iota(jnp.int32, (1, 1, SEGS), 2)
    token_image = lax.optimization_barrier(jnp.sum(jnp.where(seg_rows[:, :, None] == slots, id_rows[:, None, :], 0), axis=-1)).reshape(-1)
    key_image = lax.broadcasted_iota(jnp.int32, (1, IMG_MB * PATCHES), 1) // PATCHES
    tied_image = token_image[:, None] == key_image
    return (same_doc, tied_image)

def block_forward(weights, inputs):
    norm_gain, norm_bias, qkv_weight, out_weight, up_weight, down_weight = weights[:6]
    cross_set = weights[6:]
    token_block, between, image_block, seg_rows, id_rows = inputs
    same_doc, tied_image = block_masks(seg_rows, id_rows)
    first = self_block(token_block, norm_gain[0, 0], norm_bias[0, 0], qkv_weight[0], out_weight[0], same_doc)
    first = feed_block(first, norm_gain[0, 1], norm_bias[0, 1], up_weight[0], down_weight[0])
    second = low(low_back(first)) + between
    second = self_block(second, norm_gain[1, 0], norm_bias[1, 0], qkv_weight[1], out_weight[1], same_doc)
    second = cross_block(second, image_block, tied_image, cross_set)
    second = feed_block(second, norm_gain[1, 1], norm_bias[1, 1], up_weight[1], down_weight[1])
    return (first, second)

def reference(tokens, images, segments, image_ids, cotangent, norm_gain, norm_bias, qkv_weight, out_weight, up_weight, down_weight, cross_gain, cross_bias, cross_query, cross_kv, cross_out):
    block_tokens = ROWS_MB * ROW_LEN
    block_count = TOKENS // block_tokens
    masters = tuple((weight.astype(jnp.float32) for weight in (norm_gain, norm_bias, qkv_weight, out_weight, up_weight, down_weight, cross_gain, cross_bias, cross_query, cross_kv, cross_out)))
    token_blocks = tokens.astype(jnp.float32).reshape(block_count, block_tokens, D)
    image_blocks = images.astype(jnp.float32).reshape(block_count, IMG_MB * PATCHES, D)
    seg_blocks = segments.reshape(block_count, ROWS_MB, ROW_LEN)
    id_blocks = image_ids.reshape(block_count, ROWS_MB, SEGS)
    between = jnp.zeros_like(token_blocks)

    def whole(token_part, between_part, image_part, master_set):
        lowered = tuple((low(weight) for weight in master_set))
        layer_fn = jax.checkpoint(partial(block_forward, lowered))

        def step_block(carry, inputs):
            return (carry, layer_fn(inputs))
        carry, outputs = lax.scan(step_block, jnp.zeros((), jnp.float32), (token_part, between_part, image_part, seg_blocks, id_blocks))
        return outputs
    outputs, pullback = jax.vjp(whole, token_blocks, between, image_blocks, masters)
    cot_blocks = cotangent.astype(jnp.float32).reshape(2, block_count, block_tokens, D)
    grad_tokens, grad_between, grad_images, grad_masters = pullback((cot_blocks[0], cot_blocks[1]))
    layer_out = jnp.stack([outputs[0], outputs[1]]).reshape(2, TOKENS, D).astype(jnp.bfloat16)
    input_grad = jnp.stack([grad_tokens, grad_between]).reshape(2, TOKENS, D)
    image_grad = grad_images.reshape(IMAGES, PATCHES, D)
    return (layer_out, input_grad, image_grad, grad_masters[0], grad_masters[1], grad_masters[2], grad_masters[3], grad_masters[4], grad_masters[5], grad_masters[6], grad_masters[7], grad_masters[8], grad_masters[9], grad_masters[10])
```

```python
from functools import partial

import jax
import jax.numpy as jnp
import numpy as np
from jax import lax
from jax.experimental import pallas as pl
from jax.experimental.pallas import tpu as pltpu
from jax.sharding import PartitionSpec as P

HEADS = 12
HEAD_DIM = 64
PATCHES = 576
ROW_LEN = 64
SEGS = 3
IMG_MB = 2
ROWS_MB = 4
BLOCK = ROWS_MB * ROW_LEN
PAIR = 2 * HEAD_DIM
PAIRS = HEADS // 2
TILE = 2 * ROW_LEN
MASKED_SCORE = -1000000000.0
NORM_EPS = 1e-05
SCALE = HEAD_DIM ** (-0.5)
VMEM_LIMIT = 56 * 1024 * 1024

F32 = jnp.float32
BF16 = jnp.bfloat16


def dot(a, b):
    return lax.dot_general(a, b, (((1,), (0,)), ((), ())), preferred_element_type=F32)


def dot_nt(a, b):
    return lax.dot_general(a, b, (((1,), (1,)), ((), ())), preferred_element_type=F32)


def dot_tn(a, b):
    return lax.dot_general(a, b, (((0,), (0,)), ((), ())), preferred_element_type=F32)


def norm_parts(x):
    mean = jnp.mean(x, axis=-1, keepdims=True)
    centred = x - mean
    inv = lax.rsqrt(jnp.mean(centred * centred, axis=-1, keepdims=True) + NORM_EPS)
    return centred * inv, inv


def norm_back(d_out, normed, inv, gain):
    d_normed = d_out * gain
    d_input = inv * (
        d_normed
        - jnp.mean(d_normed, axis=-1, keepdims=True)
        - normed * jnp.mean(d_normed * normed, axis=-1, keepdims=True)
    )
    sums = jnp.concatenate(
        [
            jnp.sum(d_out * normed, axis=0, keepdims=True),
            jnp.sum(d_out, axis=0, keepdims=True),
            jnp.zeros((6, d_out.shape[1]), F32),
        ],
        axis=0,
    )
    return d_input, sums


def lane_masks(dtype):
    lane = lax.broadcasted_iota(jnp.int32, (1, PAIR), 1)
    even = (lane < HEAD_DIM).astype(F32)
    return even.astype(dtype), (1.0 - even).astype(dtype)


def softmax(scores):
    top = jnp.max(scores, axis=-1, keepdims=True)
    e = jnp.exp(scores - top)
    return (e * (1.0 / jnp.sum(e, axis=-1, keepdims=True))).astype(BF16)


def stack_heads(part, even, odd):
    return jnp.concatenate([part * even, part * odd], axis=0)


def self_fwd_kernel(x_ref, vec_ref, code_ref, code_row_ref, w_ref, x1_ref, h_ref, qkv_ref, p_ref, o_ref):
    d = x_ref.shape[1]
    x = x_ref[...].astype(F32)
    normed, _ = norm_parts(x)
    h = (normed * vec_ref[0:1, :] + vec_ref[1:2, :]).astype(BF16)
    h_ref[...] = h
    qkv_ref[...] = dot(h, w_ref[:, : 3 * d]).astype(BF16)
    even, odd = lane_masks(BF16)
    for t in range(BLOCK // TILE):
        rows = slice(t * TILE, (t + 1) * TILE)
        causal = lax.broadcasted_iota(jnp.int32, (TILE, TILE), 1) <= lax.broadcasted_iota(
            jnp.int32, (TILE, TILE), 0
        )
        allowed = (code_ref[rows, :] == code_row_ref[0, :, rows]) & causal
        for p in range(PAIRS):
            lanes = slice(p * PAIR, (p + 1) * PAIR)
            q = qkv_ref[rows, lanes] * jnp.asarray(SCALE, BF16)
            k2 = stack_heads(qkv_ref[rows, d + p * PAIR : d + (p + 1) * PAIR], even, odd)
            v2 = stack_heads(qkv_ref[rows, 2 * d + p * PAIR : 2 * d + (p + 1) * PAIR], even, odd)
            s = dot_nt(q, k2)
            probs = jnp.concatenate(
                [
                    softmax(jnp.where(allowed, s[:, :TILE], MASKED_SCORE)),
                    softmax(jnp.where(allowed, s[:, TILE:], MASKED_SCORE)),
                ],
                axis=1,
            )
            p_ref[rows, 2 * p * TILE : 2 * (p + 1) * TILE] = probs
            o_ref[rows, lanes] = dot(probs, v2).astype(BF16)
    x1_ref[...] = x + dot(o_ref[...], w_ref[:, 3 * d :])


def self_bwd_kernel(x_ref, dy_ref, vec_ref, qkv_ref, p_ref, w_ref, dx_ref, dyb_ref, dqkv_ref, sums_ref):
    d = x_ref.shape[1]
    dy = dy_ref[...]
    dyb = dy.astype(BF16)
    dyb_ref[...] = dyb
    d_mixed = dot_nt(dyb, w_ref[:, 3 * d :]).astype(BF16)
    even, odd = lane_masks(BF16)
    for t in range(BLOCK // TILE):
        rows = slice(t * TILE, (t + 1) * TILE)
        for p in range(PAIRS):
            lanes = slice(p * PAIR, (p + 1) * PAIR)
            q2 = stack_heads(qkv_ref[rows, lanes] * jnp.asarray(SCALE, BF16), even, odd)
            k2 = stack_heads(qkv_ref[rows, d + p * PAIR : d + (p + 1) * PAIR], even, odd)
            v2 = stack_heads(qkv_ref[rows, 2 * d + p * PAIR : 2 * d + (p + 1) * PAIR], even, odd)
            do = d_mixed[rows, lanes]
            do2 = stack_heads(do, even, odd)
            dp = dot_nt(do, v2)
            probs_e = p_ref[rows, 2 * p * TILE : (2 * p + 1) * TILE]
            probs_o = p_ref[rows, (2 * p + 1) * TILE : (2 * p + 2) * TILE]
            ds = []
            for probs, part in ((probs_e, dp[:, :TILE]), (probs_o, dp[:, TILE:])):
                pf = probs.astype(F32)
                term = pf * part
                ds.append((term - pf * jnp.sum(term, axis=-1, keepdims=True)).astype(BF16))
            dq = dot(jnp.concatenate(ds, axis=1), k2) * SCALE
            dk = dot_tn(jnp.concatenate(ds, axis=0), q2)
            dv = dot_tn(jnp.concatenate([probs_e, probs_o], axis=0), do2)
            dqkv_ref[rows, lanes] = dq.astype(BF16)
            dqkv_ref[rows, d + p * PAIR : d + (p + 1) * PAIR] = dk.astype(BF16)
            dqkv_ref[rows, 2 * d + p * PAIR : 2 * d + (p + 1) * PAIR] = dv.astype(BF16)
    dh = dot_nt(dqkv_ref[...], w_ref[:, : 3 * d])
    normed, inv = norm_parts(x_ref[...].astype(F32))
    d_input, sums = norm_back(dh, normed, inv, vec_ref[0:1, :])
    dx_ref[...] = dy + d_input
    sums_ref[0] = sums


def gelu_parts(u):
    phi = 0.5 + 0.5 * lax.erf(u * (0.5**0.5))
    slope = phi + u * (jnp.exp(-0.5 * (u * u)) * ((2.0 * np.pi) ** -0.5))
    return u * phi, slope


def ffn_fwd_kernel(x_ref, vec_ref, up_ref, down_ref, y_ref, m_ref, g_ref, slope_ref):
    d = x_ref.shape[1]
    ff = up_ref.shape[1]
    x = x_ref[...]
    normed, _ = norm_parts(x)
    m = (normed * vec_ref[0:1, :] + vec_ref[1:2, :]).astype(BF16)
    m_ref[...] = m
    acc = x
    for j in range(ff // d):
        cols = slice(j * d, (j + 1) * d)
        g, slope = gelu_parts(dot(m, up_ref[:, cols]))
        g = g.astype(BF16)
        g_ref[:, cols] = g
        slope_ref[:, cols] = slope.astype(BF16)
        acc = acc + dot(g, down_ref[cols, :])
    y_ref[...] = acc.astype(y_ref.dtype)


def ffn_bwd_kernel(x_ref, dy_ref, vec_ref, slope_ref, up_ref, down_ref, dx_ref, dyb_ref, du_ref, sums_ref):
    d = x_ref.shape[1]
    ff = up_ref.shape[1]
    dy = dy_ref[...].astype(F32)
    dyb = dy.astype(BF16)
    dyb_ref[...] = dyb
    acc = None
    for j in range(ff // d):
        cols = slice(j * d, (j + 1) * d)
        du = (dot_nt(dyb, down_ref[cols, :]) * slope_ref[:, cols].astype(F32)).astype(BF16)
        du_ref[:, cols] = du
        part = dot_nt(du, up_ref[:, cols])
        acc = part if acc is None else acc + part
    normed, inv = norm_parts(x_ref[...])
    d_input, sums = norm_back(acc, normed, inv, vec_ref[0:1, :])
    dx_ref[...] = dy + d_input
    sums_ref[0] = sums


def tied(part, first, second):
    return jnp.concatenate([part * first, part * second], axis=1)


def cross_fwd_kernel(x_ref, vec_ref, image_ref, kv_ref, w_ref, x2_ref, h_ref, q_ref, p_ref, o_ref):
    d = x_ref.shape[1]
    n = PATCHES
    x = x_ref[...]
    normed, _ = norm_parts(x)
    h = (normed * vec_ref[0:1, :] + vec_ref[1:2, :]).astype(BF16)
    h_ref[...] = h
    q_ref[...] = dot(h, w_ref[:, :d]).astype(BF16)
    even, odd = lane_masks(BF16)
    image = image_ref[...]
    second = image.astype(BF16)
    first = (1.0 - image).astype(BF16)
    lane_even = lax.broadcasted_iota(jnp.int32, (BLOCK, PAIR), 1) < HEAD_DIM
    is_first = jnp.broadcast_to(image, (BLOCK, PAIR)) < 0.5
    for p in range(PAIRS):
        lanes = slice(p * PAIR, (p + 1) * PAIR)
        vlanes = slice(d + p * PAIR, d + (p + 1) * PAIR)
        k2 = jnp.concatenate([kv_ref[:n, lanes], kv_ref[n:, lanes]], axis=1)
        v2 = jnp.concatenate([kv_ref[:n, vlanes], kv_ref[n:, vlanes]], axis=1)
        q = q_ref[:, lanes] * jnp.asarray(SCALE, BF16)
        out = []
        for half, mask in enumerate((even, odd)):
            probs = softmax(dot_nt(tied(q * mask, first, second), k2))
            p_ref[2 * p + half] = probs
            both = dot(probs, v2)
            out.append(jnp.where(is_first, both[:, :PAIR], both[:, PAIR:]))
        o_ref[:, lanes] = jnp.where(lane_even, out[0], out[1]).astype(BF16)
    x2_ref[...] = x + dot(o_ref[...], w_ref[:, 3 * d : 4 * d])


def cross_bwd_kernel(
    x_ref, dy_ref, vec_ref, image_ref, q_ref, p_ref, kv_ref, w_ref, dx_ref, dyb_ref, dq_ref, dkv_ref, sums_ref
):
    d = x_ref.shape[1]
    n = PATCHES
    dy = dy_ref[...]
    dyb = dy.astype(BF16)
    dyb_ref[...] = dyb
    d_mixed = dot_nt(dyb, w_ref[:, 3 * d : 4 * d]).astype(BF16)
    even, odd = lane_masks(BF16)
    image = image_ref[...]
    second = image.astype(BF16)
    first = (1.0 - image).astype(BF16)
    lane_even = lax.broadcasted_iota(jnp.int32, (BLOCK, PAIR), 1) < HEAD_DIM
    is_first = jnp.broadcast_to(image, (BLOCK, PAIR)) < 0.5
    for p in range(PAIRS):
        lanes = slice(p * PAIR, (p + 1) * PAIR)
        vlanes = slice(d + p * PAIR, d + (p + 1) * PAIR)
        k2 = jnp.concatenate([kv_ref[:n, lanes], kv_ref[n:, lanes]], axis=1)
        v2 = jnp.concatenate([kv_ref[:n, vlanes], kv_ref[n:, vlanes]], axis=1)
        q = q_ref[:, lanes] * jnp.asarray(SCALE, BF16)
        do = d_mixed[:, lanes]
        ds, qq, dd, dq = [], [], [], []
        for half, mask in enumerate((even, odd)):
            qq.append(tied(q * mask, first, second))
            dd.append(tied(do * mask, first, second))
            dp = dot_nt(dd[half], v2)
            pf = p_ref[2 * p + half].astype(F32)
            term = pf * dp
            ds.append((term - pf * jnp.sum(term, axis=-1, keepdims=True)).astype(BF16))
            both = dot(ds[half], k2)
            dq.append(jnp.where(is_first, both[:, :PAIR], both[:, PAIR:]))
        dq_ref[:, lanes] = (jnp.where(lane_even, dq[0], dq[1]) * SCALE).astype(BF16)
        dk = dot_tn(jnp.concatenate(ds, axis=0), jnp.concatenate(qq, axis=0)).astype(BF16)
        dv = dot_tn(
            jnp.concatenate([p_ref[2 * p], p_ref[2 * p + 1]], axis=0), jnp.concatenate(dd, axis=0)
        ).astype(BF16)
        dkv_ref[:n, lanes] = dk[:, :PAIR]
        dkv_ref[n:, lanes] = dk[:, PAIR:]
        dkv_ref[:n, vlanes] = dv[:, :PAIR]
        dkv_ref[n:, vlanes] = dv[:, PAIR:]
    dh = dot_nt(dq_ref[...], w_ref[:, :d])
    normed, inv = norm_parts(x_ref[...])
    d_input, sums = norm_back(dh, normed, inv, vec_ref[0:1, :])
    dx_ref[...] = dy + d_input
    sums_ref[0] = sums


def rows_spec(rows, cols):
    return pl.BlockSpec((rows, cols), lambda i: (i, 0))


def whole_spec(shape):
    return pl.BlockSpec(shape, lambda i: (0,) * len(shape), pipeline_mode=pl.Buffered(1))


def call(kernel, blocks, in_specs, out_specs, out_shape, flops, moved, trans=0):
    return pl.pallas_call(
        kernel,
        grid=(blocks,),
        in_specs=in_specs,
        out_specs=out_specs,
        out_shape=out_shape,
        compiler_params=pltpu.CompilerParams(vmem_limit_bytes=VMEM_LIMIT),
        cost_estimate=pl.CostEstimate(flops=flops, bytes_accessed=moved, transcendentals=trans),
    )


def sds(shape, dtype):
    return jax.ShapeDtypeStruct(shape, dtype)


def sums_spec(d):
    return pl.BlockSpec((1, 8, d), lambda i: (i, 0, 0))


def self_fwd(x, vec, code, code_row, w):
    t, d = x.shape
    nb = t // BLOCK
    return call(
        self_fwd_kernel,
        nb,
        [
            rows_spec(BLOCK, d),
            whole_spec((8, d)),
            rows_spec(BLOCK, 1),
            pl.BlockSpec((1, 1, BLOCK), lambda i: (i, 0, 0)),
            whole_spec((d, 4 * d)),
        ],
        [
            rows_spec(BLOCK, d),
            rows_spec(BLOCK, d),
            rows_spec(BLOCK, 3 * d),
            rows_spec(BLOCK, HEADS * TILE),
            rows_spec(BLOCK, d),
        ],
        [
            sds((t, d), F32),
            sds((t, d), BF16),
            sds((t, 3 * d), BF16),
            sds((t, HEADS * TILE), BF16),
            sds((t, d), BF16),
        ],
        t * d * 8 * d + t * HEADS * TILE * 512,
        d * d * 8 + t * d * 24,
    )(x, vec, code, code_row, w)


def self_bwd(x, dy, vec, qkv, probs, w):
    t, d = x.shape
    nb = t // BLOCK
    return call(
        self_bwd_kernel,
        nb,
        [
            rows_spec(BLOCK, d),
            rows_spec(BLOCK, d),
            whole_spec((8, d)),
            rows_spec(BLOCK, 3 * d),
            rows_spec(BLOCK, HEADS * TILE),
            whole_spec((d, 4 * d)),
        ],
        [rows_spec(BLOCK, d), rows_spec(BLOCK, d), rows_spec(BLOCK, 3 * d), sums_spec(d)],
        [sds((t, d), F32), sds((t, d), BF16), sds((t, 3 * d), BF16), sds((nb, 8, d), F32)],
        t * d * 8 * d + t * HEADS * TILE * 1024,
        d * d * 8 + t * d * 30,
    )(x, dy, vec, qkv, probs, w)


def ffn_fwd(x, vec, up, down, out_dtype):
    t, d = x.shape
    ff = up.shape[1]
    nb = t // BLOCK
    return call(
        ffn_fwd_kernel,
        nb,
        [rows_spec(BLOCK, d), whole_spec((8, d)), whole_spec((d, ff)), whole_spec((ff, d))],
        [rows_spec(BLOCK, d), rows_spec(BLOCK, d), rows_spec(BLOCK, ff), rows_spec(BLOCK, ff)],
        [sds((t, d), out_dtype), sds((t, d), BF16), sds((t, ff), BF16), sds((t, ff), BF16)],
        t * d * 4 * ff,
        d * ff * 4 + t * (d * 8 + ff * 4),
        2 * t * ff,
    )(x, vec, up, down)


def ffn_bwd(x, dy, vec, slope, up, down):
    t, d = x.shape
    ff = up.shape[1]
    nb = t // BLOCK
    return call(
        ffn_bwd_kernel,
        nb,
        [
            rows_spec(BLOCK, d),
            rows_spec(BLOCK, d),
            whole_spec((8, d)),
            rows_spec(BLOCK, ff),
            whole_spec((d, ff)),
            whole_spec((ff, d)),
        ],
        [rows_spec(BLOCK, d), rows_spec(BLOCK, d), rows_spec(BLOCK, ff), sums_spec(d)],
        [sds((t, d), F32), sds((t, d), BF16), sds((t, ff), BF16), sds((nb, 8, d), F32)],
        t * d * 4 * ff,
        d * ff * 4 + t * (d * 14 + ff * 4),
    )(x, dy, vec, slope, up, down)


def cross_fwd(x, vec, image, kv, w):
    t, d = x.shape
    nb = t // BLOCK
    wide = w.shape[1]
    return call(
        cross_fwd_kernel,
        nb,
        [
            rows_spec(BLOCK, d),
            whole_spec((8, d)),
            rows_spec(BLOCK, 1),
            rows_spec(IMG_MB * PATCHES, 2 * d),
            whole_spec((d, wide)),
        ],
        [
            rows_spec(BLOCK, d),
            rows_spec(BLOCK, d),
            rows_spec(BLOCK, d),
            pl.BlockSpec((HEADS, BLOCK, PATCHES), lambda i: (i, 0, 0)),
            rows_spec(BLOCK, d),
        ],
        [
            sds((t, d), F32),
            sds((t, d), BF16),
            sds((t, d), BF16),
            sds((nb * HEADS, BLOCK, PATCHES), BF16),
            sds((t, d), BF16),
        ],
        t * d * 4 * d + 4 * t * HEADS * PATCHES * 256,
        d * d * 8 + t * d * 16 + nb * PATCHES * d * 8 + t * HEADS * PATCHES * 2,
        t * HEADS * PATCHES,
    )(x, vec, image, kv, w)


def cross_bwd(x, dy, vec, image, q, probs, kv, w):
    t, d = x.shape
    nb = t // BLOCK
    wide = w.shape[1]
    return call(
        cross_bwd_kernel,
        nb,
        [
            rows_spec(BLOCK, d),
            rows_spec(BLOCK, d),
            whole_spec((8, d)),
            rows_spec(BLOCK, 1),
            rows_spec(BLOCK, d),
            pl.BlockSpec((HEADS, BLOCK, PATCHES), lambda i: (i, 0, 0)),
            rows_spec(IMG_MB * PATCHES, 2 * d),
            whole_spec((d, wide)),
        ],
        [
            rows_spec(BLOCK, d),
            rows_spec(BLOCK, d),
            rows_spec(BLOCK, d),
            rows_spec(IMG_MB * PATCHES, 2 * d),
            sums_spec(d),
        ],
        [
            sds((t, d), F32),
            sds((t, d), BF16),
            sds((t, d), BF16),
            sds((nb * IMG_MB * PATCHES, 2 * d), BF16),
            sds((nb, 8, d), F32),
        ],
        t * d * 4 * d + 8 * t * HEADS * PATCHES * 256,
        d * d * 8 + t * d * 16 + nb * PATCHES * d * 16 + t * HEADS * PATCHES * 2,
    )(x, dy, vec, image, q, probs, kv, w)


CORES = 2
RING = 8


def ring_tables():
    half = RING // 2
    chip_at = [2 * z for z in range(half)] + [2 * z + 1 for z in range(half - 1, -1, -1)]
    pos_of = [chip_at.index(chip) for chip in range(RING)]
    return chip_at, pos_of


CHIP_AT, POS_OF = ring_tables()


def flat(section, chip, core):
    return section * RING * CORES + chip * CORES + core


def ring_pairs(sections, step):
    return [
        (flat(s, CHIP_AT[i], c), flat(s, CHIP_AT[(i + step) % RING], c))
        for s in sections
        for i in range(RING)
        for c in range(CORES)
    ]


def core_pairs(sections):
    return [
        (flat(s, chip, c), flat(s, chip, 1 - c))
        for s in sections
        for chip in range(RING)
        for c in range(CORES)
    ]


def send(x, pairs):
    return lax.ppermute(x, ("section", "dp"), pairs)


def tie(x, deps):
    if not deps:
        return x
    return lax.optimization_barrier((x, *deps))[0]


def place(chip_count):
    return lax.axis_index("dp") // CORES, lax.axis_index("dp") % CORES


def chip_by_offset(offset):
    pos = jnp.asarray(POS_OF, jnp.int32)[lax.axis_index("dp") // CORES]
    return jnp.asarray(CHIP_AT, jnp.int32)[(pos + offset + RING) % RING]


def ring_gather(chunk, sections, long_way, deps, by_core):
    core = lax.axis_index("dp") % CORES
    first, second = (CORES, RING) if by_core else (RING, CORES)
    whole = jnp.zeros((first, second) + chunk.shape, chunk.dtype)

    def put(whole, piece, offset, piece_core):
        chip = chip_by_offset(offset)
        start = (piece_core, chip) if by_core else (chip, piece_core)
        return lax.dynamic_update_slice(whole, piece[None, None], start + (0,) * chunk.ndim)

    def keep(whole, piece, offset):
        whole = put(whole, piece, offset, core)
        return put(whole, send(piece, core_pairs(sections)), offset, 1 - core)

    chunk = tie(chunk, deps)
    arrivals = {1: [], -1: []}
    for step in range(1, RING // 2 + 1):
        for way in (1, -1):
            if step == RING // 2 and way != long_way:
                continue
            held = arrivals[way][-1] if arrivals[way] else chunk
            arrivals[way].append(send(held, ring_pairs(sections, way)))
    whole = keep(whole, chunk, 0)
    for step in range(1, RING // 2 + 1):
        for way in (1, -1):
            if step <= len(arrivals[way]):
                whole = keep(whole, arrivals[way][step - 1], -way * step)
    return whole.reshape((RING * CORES * chunk.shape[0],) + chunk.shape[1:]), arrivals


def ring_scatter(partial_sums, sections, long_way, by_core):
    core = lax.axis_index("dp") % CORES
    rows = partial_sums.shape[0] // (RING * CORES)
    first, second = (CORES, RING) if by_core else (RING, CORES)
    axis = 0 if by_core else 1
    split = partial_sums.reshape((first, second, rows) + partial_sums.shape[1:])
    theirs = lax.dynamic_index_in_dim(split, 1 - core, axis, keepdims=False)
    mine = lax.dynamic_index_in_dim(split, core, axis, keepdims=False)
    joined = (mine.astype(F32) + send(theirs, core_pairs(sections)).astype(F32)).astype(BF16)

    def own(offset):
        return lax.dynamic_index_in_dim(joined, chip_by_offset(offset), 0, keepdims=False)

    total = own(0).astype(F32)
    for way in (1, -1):
        hops = RING // 2 if way == long_way else RING // 2 - 1
        moving = None
        for step in range(hops):
            piece = own(way * (hops - step))
            if moving is not None:
                piece = (piece.astype(F32) + moving.astype(F32)).astype(BF16)
            moving = send(piece, ring_pairs(sections, way))
        total = total + moving.astype(F32)
    return total


def vec_rows(gain, bias):
    rows = jnp.stack([gain, bias]).astype(F32)
    return jnp.concatenate([rows, jnp.zeros((6, rows.shape[1]), F32)], axis=0)


def lanes_of(vectors, width):
    table = jnp.stack(vectors, axis=1)
    return jnp.pad(table, ((0, 0), (0, width - table.shape[1])))


def local(
    tokens,
    images,
    segments,
    image_ids,
    cotangent,
    norm_gain,
    norm_bias,
    qkv_weight,
    out_weight,
    up_weight,
    down_weight,
    cross_gain,
    cross_bias,
    cross_query,
    cross_kv,
    cross_out,
):
    section = lax.axis_index("section")
    multimodal = section == 1
    d = tokens.shape[1]
    t = tokens.shape[0]
    nb = t // BLOCK
    members = lax.axis_size("dp")
    ringed = members == RING * CORES and lax.axis_size("section") == 2

    attn_piece = jnp.concatenate(
        [
            qkv_weight[0],
            out_weight[0],
            lanes_of([norm_gain[0, 0], norm_bias[0, 0], norm_gain[0, 1], norm_bias[0, 1]], PAIR),
        ],
        axis=1,
    ).astype(BF16)
    up_piece = up_weight[0].astype(BF16)
    down_piece = down_weight[0].astype(BF16)
    cross_piece = jnp.concatenate(
        [cross_query, cross_kv, cross_out, lanes_of([cross_gain, cross_bias], PAIR)], axis=1
    ).astype(BF16)

    if ringed:
        core = lax.axis_index("dp") % CORES
        both = (0, 1)
        one = send(
            cross_piece,
            [(flat(0, k, 0), flat(1, k, 0)) for k in range(RING)]
            + [(flat(1, k, 0), flat(1, k, 1)) for k in range(RING)],
        )
        two = send(cross_piece, [(flat(0, k, 1), flat(1, k, 0)) for k in range(RING)])
        cross_chunk = jnp.concatenate([one, jnp.where(core == 0, two, cross_piece)], axis=0)
        w_attn, seen = ring_gather(attn_piece, both, 1, (), False)
        w_cross, seen_cross = ring_gather(cross_chunk, (1,), -1, (seen[1][1],), True)
        w_up, seen_up = ring_gather(up_piece, both, -1, (seen[1][1], seen[-1][1]), False)
        w_down, _ = ring_gather(down_piece, both, 1, (seen_up[1][1], seen_up[-1][1]), False)
    else:
        w_attn = lax.all_gather(attn_piece, "dp", axis=0, tiled=True)
        w_up = lax.all_gather(up_piece, "dp", axis=0, tiled=True)
        w_down = lax.all_gather(down_piece, "dp", axis=0, tiled=True)
        w_cross = lax.all_gather(cross_piece, ("section", "dp"), axis=0, tiled=True)

    vec_table = w_attn[:, 4 * d : 4 * d + 4].T
    vec_attn = vec_rows(vec_table[0], vec_table[1])
    vec_ffn = vec_rows(vec_table[2], vec_table[3])
    cross_table = w_cross[:, 4 * d : 4 * d + 2].T
    vec_cross = vec_rows(cross_table[0], cross_table[1])

    row_in_tile = lax.broadcasted_iota(jnp.int32, segments.shape, 0) % (TILE // ROW_LEN)
    code = (row_in_tile * (SEGS + 1) + segments).reshape(-1)
    code_col = code[:, None]
    code_row = code.reshape(nb, 1, BLOCK)
    slots = lax.broadcasted_iota(jnp.int32, (1, 1, SEGS), 2)
    token_image = jnp.sum(
        jnp.where(segments[:, :, None] == slots, image_ids[:, None, :], 0), axis=-1
    )
    image_col = token_image.reshape(-1, 1).astype(F32)
    patches = images.reshape(-1, d)

    kv = dot(patches, w_cross[:, d : 3 * d]).astype(BF16)

    a_x1, a_h, a_qkv, a_p, a_o = self_fwd(tokens, vec_attn, code_col, code_row, w_attn)
    a_y, a_m, a_g, a_slope = [], [], [], []
    for b in range(nb):
        rows = slice(b * BLOCK, (b + 1) * BLOCK)
        for got, part in zip(
            (a_y, a_m, a_g, a_slope), ffn_fwd(a_x1[rows], vec_ffn, w_up, w_down, BF16)
        ):
            got.append(part)
    arriving = jnp.concatenate([lax.ppermute(y, "section", [(0, 1)]) for y in a_y])
    a_y, a_m, a_g, a_slope = (jnp.concatenate(parts) for parts in (a_y, a_m, a_g, a_slope))

    b_x1, b_h, b_qkv, b_p, b_o = self_fwd(arriving, vec_attn, code_col, code_row, w_attn)
    b_x2, c_h, c_q, c_p, c_o = cross_fwd(b_x1, vec_cross, image_col, kv, w_cross)
    b_y, b_m, b_g, b_slope = ffn_fwd(b_x2, vec_ffn, w_up, w_down, BF16)
    b_dx2, b_dy, b_du, b_fsum = ffn_bwd(b_x2, cotangent[0], vec_ffn, b_slope, w_up, w_down)
    b_dx1, c_dy, c_dq, c_dkv, c_sum = cross_bwd(
        b_x1, b_dx2, vec_cross, image_col, c_q, c_p, kv, w_cross
    )
    b_dx0, b_dy1, b_dqkv, b_asum = self_bwd(arriving, b_dx1, vec_attn, b_qkv, b_p, w_attn)
    returning = lax.ppermute(b_dx0.astype(BF16), "section", [(1, 0)])

    def low_tn(left, right):
        return dot_tn(left, right).astype(BF16)

    def attn_grads(h, dqkv, o, dyb, asum, fsum):
        sums = jnp.concatenate([jnp.sum(asum, axis=0)[:2], jnp.sum(fsum, axis=0)[:2]])
        columns = jnp.pad(sums.T, ((0, 0), (0, PAIR - 4))).astype(BF16)
        return jnp.concatenate([low_tn(h, dqkv), low_tn(o, dyb), columns], axis=1)

    def cross_grads():
        columns = jnp.pad(jnp.sum(c_sum, axis=0)[:2].T, ((0, 0), (0, PAIR - 2))).astype(BF16)
        return jnp.concatenate(
            [low_tn(c_h, c_dq), low_tn(patches, c_dkv), low_tn(c_o, c_dy), columns], axis=1
        )

    w_kv = w_cross[:, d : 3 * d]
    half = d // 2
    image_theirs = dot_nt(c_dkv, w_kv[:half]).astype(BF16)
    image_mine = dot_nt(c_dkv, w_kv[half:])
    image_shard = jnp.where(
        multimodal,
        image_mine,
        lax.ppermute(image_theirs, "section", [(1, 0)]).astype(F32),
    )

    a_dy_in = cotangent[0].astype(F32) + returning.astype(F32)
    a_dx1, a_dy, a_du, a_fsum = ffn_bwd(a_x1, a_dy_in, vec_ffn, a_slope, w_up, w_down)
    a_dx0, a_dy1, a_dqkv, a_asum = self_bwd(tokens, a_dx1, vec_attn, a_qkv, a_p, w_attn)

    b_down, b_up = low_tn(b_g, b_dy), low_tn(b_m, b_du)
    b_attn = attn_grads(b_h, b_dqkv, b_o, b_dy1, b_asum, b_fsum)
    b_cross = cross_grads()
    a_down, a_up = low_tn(a_g, a_dy), low_tn(a_m, a_du)
    a_attn = attn_grads(a_h, a_dqkv, a_o, a_dy1, a_asum, a_fsum)

    if ringed:
        s1, s0 = (1,), (0,)
        b_shards = [
            ring_scatter(b_down, s1, 1, False),
            ring_scatter(b_up, s1, -1, False),
            ring_scatter(b_attn, s1, -1, False),
        ]
        cross_sum = ring_scatter(b_cross, s1, 1, True)
        a_shards = [
            ring_scatter(a_down, s0, 1, False),
            ring_scatter(a_up, s0, -1, False),
            ring_scatter(a_attn, s0, 1, False),
        ]
        down_g, up_g, attn_g = (
            jnp.where(multimodal, second, first) for first, second in zip(a_shards, b_shards)
        )
        part = cross_sum.shape[0] // 2
        one = send(
            cross_sum[:part],
            [(flat(1, k, 0), flat(0, k, 0)) for k in range(RING)]
            + [(flat(1, k, 1), flat(1, k, 0)) for k in range(RING)],
        )
        two = send(cross_sum[part:], [(flat(1, k, 0), flat(0, k, 1)) for k in range(RING)])
        cross_g = jnp.where(
            core == 0, one, jnp.where(multimodal, cross_sum[part:], two)
        )
    else:
        def summed(first, second):
            return lax.psum_scatter(
                jnp.where(multimodal, second, first).astype(F32), "dp", scatter_dimension=0, tiled=True
            )

        down_g, up_g, attn_g = summed(a_down, b_down), summed(a_up, b_up), summed(a_attn, b_attn)
        cross_g = lax.psum_scatter(
            jnp.where(multimodal, b_cross, 0.0).astype(F32),
            ("section", "dp"),
            scatter_dimension=0,
            tiled=True,
        )

    vec_g = attn_g[:, 4 * d : 4 * d + 4].T
    return (
        jnp.where(multimodal, b_y, a_y)[None],
        jnp.where(multimodal, b_dx0, a_dx0)[None],
        image_shard.reshape(images.shape[0], images.shape[1], half),
        jnp.stack([vec_g[0], vec_g[2]])[None],
        jnp.stack([vec_g[1], vec_g[3]])[None],
        attn_g[None, :, : 3 * d],
        attn_g[None, :, 3 * d : 4 * d],
        up_g[None],
        down_g[None],
        cross_g[:, 4 * d],
        cross_g[:, 4 * d + 1],
        cross_g[:, :d],
        cross_g[:, d : 3 * d],
        cross_g[:, 3 * d : 4 * d],
    )


def solution(mesh):
    in_specs = (
        P("dp", None),
        P("dp", None, None),
        P("dp", None),
        P("dp", None),
        P("section", "dp", None),
        P("section", None, "dp"),
        P("section", None, "dp"),
        P("section", "dp", None),
        P("section", "dp", None),
        P("section", "dp", None),
        P("section", "dp", None),
        P(("section", "dp")),
        P(("section", "dp")),
        P(("section", "dp"), None),
        P(("section", "dp"), None),
        P(("section", "dp"), None),
    )
    out_specs = (
        P("section", "dp", None),
        P("section", "dp", None),
        P("dp", None, "section"),
        P("section", None, "dp"),
        P("section", None, "dp"),
        P("section", "dp", None),
        P("section", "dp", None),
        P("section", "dp", None),
        P("section", "dp", None),
        P(("section", "dp")),
        P(("section", "dp")),
        P(("section", "dp"), None),
        P(("section", "dp"), None),
        P(("section", "dp"), None),
    )
    return jax.shard_map(local, mesh=mesh, in_specs=in_specs, out_specs=out_specs, check_vma=False)
```

```python
from functools import partial
from typing import Any, NamedTuple

import jax
import jax.numpy as jnp
import numpy as np
from jax import lax
from jax.experimental import pallas as pl
from jax.experimental.pallas import tpu as pltpu
from jax.sharding import PartitionSpec as P

HEADS = 12
HEAD_DIM = 64
PATCHES = 576
ROW_LEN = 64
SEGS = 3
IMG_MB = 2
ROWS_MB = 4
CORES = 2
RING = 8
BLOCK = ROWS_MB * ROW_LEN
PAIR = 2 * HEAD_DIM
PAIRS = HEADS // 2
TILE = 2 * ROW_LEN
MASKED_SCORE = -1000000000.0
NORM_EPS = 1e-05
SCALE = HEAD_DIM ** (-0.5)
VMEM_LIMIT = 56 * 1024 * 1024
SMALL_LIMIT = 12 * 1024 * 1024

F32 = jnp.float32
BF16 = jnp.bfloat16


def dot(a, b):
    return lax.dot_general(a, b, (((1,), (0,)), ((), ())), preferred_element_type=F32)


def dot_nt(a, b):
    return lax.dot_general(a, b, (((1,), (1,)), ((), ())), preferred_element_type=F32)


def dot_tn(a, b):
    return lax.dot_general(a, b, (((0,), (0,)), ((), ())), preferred_element_type=F32)


def norm_parts(x):
    mean = jnp.mean(x, axis=-1, keepdims=True)
    centred = x - mean
    inv = lax.rsqrt(jnp.mean(centred * centred, axis=-1, keepdims=True) + NORM_EPS)
    return centred * inv, inv


def norm_back(d_out, normed, inv, gain):
    d_normed = d_out * gain
    d_input = inv * (
        d_normed
        - jnp.mean(d_normed, axis=-1, keepdims=True)
        - normed * jnp.mean(d_normed * normed, axis=-1, keepdims=True)
    )
    sums = jnp.concatenate(
        [
            jnp.sum(d_out * normed, axis=0, keepdims=True),
            jnp.sum(d_out, axis=0, keepdims=True),
            jnp.zeros((6, d_out.shape[1]), F32),
        ],
        axis=0,
    )
    return d_input, sums


def lane_masks(dtype):
    lane = lax.broadcasted_iota(jnp.int32, (1, PAIR), 1)
    even = (lane < HEAD_DIM).astype(F32)
    return even.astype(dtype), (1.0 - even).astype(dtype)


def softmax(scores):
    top = jnp.max(scores, axis=-1, keepdims=True)
    e = jnp.exp(scores - top)
    return (e * (1.0 / jnp.sum(e, axis=-1, keepdims=True))).astype(BF16)


def stack_heads(part, even, odd):
    return jnp.concatenate([part * even, part * odd], axis=0)


def self_fwd_kernel(x_ref, vec_ref, code_ref, code_row_ref, w_ref, x1_ref, h_ref, qkv_ref, p_ref, o_ref):
    d = x_ref.shape[1]
    x = x_ref[...].astype(F32)
    normed, _ = norm_parts(x)
    h = (normed * vec_ref[0:1, :] + vec_ref[1:2, :]).astype(BF16)
    h_ref[...] = h
    qkv_ref[...] = dot(h, w_ref[:, : 3 * d]).astype(BF16)
    even, odd = lane_masks(BF16)
    for t in range(BLOCK // TILE):
        rows = slice(t * TILE, (t + 1) * TILE)
        causal = lax.broadcasted_iota(jnp.int32, (TILE, TILE), 1) <= lax.broadcasted_iota(
            jnp.int32, (TILE, TILE), 0
        )
        allowed = (code_ref[rows, :] == code_row_ref[0, :, rows]) & causal
        for p in range(PAIRS):
            lanes = slice(p * PAIR, (p + 1) * PAIR)
            q = qkv_ref[rows, lanes] * jnp.asarray(SCALE, BF16)
            k2 = stack_heads(qkv_ref[rows, d + p * PAIR : d + (p + 1) * PAIR], even, odd)
            v2 = stack_heads(qkv_ref[rows, 2 * d + p * PAIR : 2 * d + (p + 1) * PAIR], even, odd)
            s = dot_nt(q, k2)
            probs = jnp.concatenate(
                [
                    softmax(jnp.where(allowed, s[:, :TILE], MASKED_SCORE)),
                    softmax(jnp.where(allowed, s[:, TILE:], MASKED_SCORE)),
                ],
                axis=1,
            )
            p_ref[rows, 2 * p * TILE : 2 * (p + 1) * TILE] = probs
            o_ref[rows, lanes] = dot(probs, v2).astype(BF16)
    x1_ref[...] = x + dot(o_ref[...], w_ref[:, 3 * d : 4 * d])


def self_bwd_kernel(x_ref, dy_ref, vec_ref, qkv_ref, p_ref, w_ref, dxb_ref, dx_ref, dyb_ref, dqkv_ref, sums_ref):
    d = x_ref.shape[1]
    dy = dy_ref[...]
    dyb = dy.astype(BF16)
    dyb_ref[...] = dyb
    d_mixed = dot_nt(dyb, w_ref[:, 3 * d : 4 * d]).astype(BF16)
    even, odd = lane_masks(BF16)
    for t in range(BLOCK // TILE):
        rows = slice(t * TILE, (t + 1) * TILE)
        for p in range(PAIRS):
            lanes = slice(p * PAIR, (p + 1) * PAIR)
            q2 = stack_heads(qkv_ref[rows, lanes] * jnp.asarray(SCALE, BF16), even, odd)
            k2 = stack_heads(qkv_ref[rows, d + p * PAIR : d + (p + 1) * PAIR], even, odd)
            v2 = stack_heads(qkv_ref[rows, 2 * d + p * PAIR : 2 * d + (p + 1) * PAIR], even, odd)
            do = d_mixed[rows, lanes]
            do2 = stack_heads(do, even, odd)
            dp = dot_nt(do, v2)
            probs_e = p_ref[rows, 2 * p * TILE : (2 * p + 1) * TILE]
            probs_o = p_ref[rows, (2 * p + 1) * TILE : (2 * p + 2) * TILE]
            ds = []
            for probs, part in ((probs_e, dp[:, :TILE]), (probs_o, dp[:, TILE:])):
                pf = probs.astype(F32)
                term = pf * part
                ds.append((term - pf * jnp.sum(term, axis=-1, keepdims=True)).astype(BF16))
            dq = dot(jnp.concatenate(ds, axis=1), k2) * SCALE
            dk = dot_tn(jnp.concatenate(ds, axis=0), q2)
            dv = dot_tn(jnp.concatenate([probs_e, probs_o], axis=0), do2)
            dqkv_ref[rows, lanes] = dq.astype(BF16)
            dqkv_ref[rows, d + p * PAIR : d + (p + 1) * PAIR] = dk.astype(BF16)
            dqkv_ref[rows, 2 * d + p * PAIR : 2 * d + (p + 1) * PAIR] = dv.astype(BF16)
    dh = dot_nt(dqkv_ref[...], w_ref[:, : 3 * d])
    normed, inv = norm_parts(x_ref[...].astype(F32))
    d_input, sums = norm_back(dh, normed, inv, vec_ref[0:1, :])
    dx = dy + d_input
    dx_ref[...] = dx
    dxb_ref[...] = dx.astype(BF16)
    sums_ref[0] = sums


def gelu_parts(u):
    phi = 0.5 + 0.5 * lax.erf(u * (0.5**0.5))
    slope = phi + u * (jnp.exp(-0.5 * (u * u)) * ((2.0 * np.pi) ** -0.5))
    return u * phi, slope


def ffn_fwd_kernel(x_ref, vec_ref, up_ref, down_ref, y_ref, m_ref, g_ref, slope_ref):
    d = x_ref.shape[1]
    x = x_ref[...]
    normed, _ = norm_parts(x)
    m = (normed * vec_ref[0:1, :] + vec_ref[1:2, :]).astype(BF16)
    m_ref[...] = m
    acc = x
    for j in range(up_ref.shape[0]):
        cols = slice(j * d, (j + 1) * d)
        g, slope = gelu_parts(dot(m, up_ref[j]))
        g = g.astype(BF16)
        g_ref[:, cols] = g
        slope_ref[:, cols] = slope.astype(BF16)
        acc = acc + dot(g, down_ref[cols, :])
    y_ref[...] = acc.astype(y_ref.dtype)


def ffn_bwd_kernel(x_ref, dy_ref, more_ref, vec_ref, slope_ref, up_ref, down_ref, dx_ref, dyb_ref, du_ref, sums_ref):
    d = x_ref.shape[1]
    dy = dy_ref[...].astype(F32)
    if more_ref is not None:
        dy = dy + more_ref[...].astype(F32)
    dyb = dy.astype(BF16)
    dyb_ref[...] = dyb
    acc = None
    for j in range(up_ref.shape[0]):
        cols = slice(j * d, (j + 1) * d)
        du = (dot_nt(dyb, down_ref[cols, :]) * slope_ref[:, cols].astype(F32)).astype(BF16)
        du_ref[:, cols] = du
        part = dot_nt(du, up_ref[j])
        acc = part if acc is None else acc + part
    normed, inv = norm_parts(x_ref[...])
    d_input, sums = norm_back(acc, normed, inv, vec_ref[0:1, :])
    dx_ref[...] = dy + d_input
    sums_ref[0] = sums


def tied(part, first, second):
    return jnp.concatenate([part * first, part * second], axis=1)


def cross_fwd_kernel(x_ref, vec_ref, image_ref, kv_ref, w_ref, x2_ref, h_ref, q_ref, p_ref, o_ref):
    d = x_ref.shape[1]
    n = PATCHES
    x = x_ref[...]
    normed, _ = norm_parts(x)
    h = (normed * vec_ref[0:1, :] + vec_ref[1:2, :]).astype(BF16)
    h_ref[...] = h
    q_ref[...] = dot(h, w_ref[:, :d]).astype(BF16)
    even, odd = lane_masks(BF16)
    image = image_ref[...]
    second = image.astype(BF16)
    first = (1.0 - image).astype(BF16)
    lane_even = lax.broadcasted_iota(jnp.int32, (BLOCK, PAIR), 1) < HEAD_DIM
    is_first = jnp.broadcast_to(image, (BLOCK, PAIR)) < 0.5
    for p in range(PAIRS):
        lanes = slice(p * PAIR, (p + 1) * PAIR)
        vlanes = slice(d + p * PAIR, d + (p + 1) * PAIR)
        k2 = jnp.concatenate([kv_ref[:n, lanes], kv_ref[n:, lanes]], axis=1)
        v2 = jnp.concatenate([kv_ref[:n, vlanes], kv_ref[n:, vlanes]], axis=1)
        q = q_ref[:, lanes] * jnp.asarray(SCALE, BF16)
        out = []
        for half, mask in enumerate((even, odd)):
            probs = softmax(dot_nt(tied(q * mask, first, second), k2))
            p_ref[2 * p + half] = probs
            both = dot(probs, v2)
            out.append(jnp.where(is_first, both[:, :PAIR], both[:, PAIR:]))
        o_ref[:, lanes] = jnp.where(lane_even, out[0], out[1]).astype(BF16)
    x2_ref[...] = x + dot(o_ref[...], w_ref[:, 3 * d : 4 * d])


def cross_bwd_kernel(
    x_ref, dy_ref, vec_ref, image_ref, q_ref, p_ref, kv_ref, w_ref, dx_ref, dyb_ref, dq_ref, dkv_ref, sums_ref
):
    d = x_ref.shape[1]
    n = PATCHES
    dy = dy_ref[...]
    dyb = dy.astype(BF16)
    dyb_ref[...] = dyb
    d_mixed = dot_nt(dyb, w_ref[:, 3 * d : 4 * d]).astype(BF16)
    even, odd = lane_masks(BF16)
    image = image_ref[...]
    second = image.astype(BF16)
    first = (1.0 - image).astype(BF16)
    lane_even = lax.broadcasted_iota(jnp.int32, (BLOCK, PAIR), 1) < HEAD_DIM
    is_first = jnp.broadcast_to(image, (BLOCK, PAIR)) < 0.5
    for p in range(PAIRS):
        lanes = slice(p * PAIR, (p + 1) * PAIR)
        vlanes = slice(d + p * PAIR, d + (p + 1) * PAIR)
        k2 = jnp.concatenate([kv_ref[:n, lanes], kv_ref[n:, lanes]], axis=1)
        v2 = jnp.concatenate([kv_ref[:n, vlanes], kv_ref[n:, vlanes]], axis=1)
        q = q_ref[:, lanes] * jnp.asarray(SCALE, BF16)
        do = d_mixed[:, lanes]
        ds, qq, dd, dq = [], [], [], []
        for half, mask in enumerate((even, odd)):
            qq.append(tied(q * mask, first, second))
            dd.append(tied(do * mask, first, second))
            dp = dot_nt(dd[half], v2)
            pf = p_ref[2 * p + half].astype(F32)
            term = pf * dp
            ds.append((term - pf * jnp.sum(term, axis=-1, keepdims=True)).astype(BF16))
            both = dot(ds[half], k2)
            dq.append(jnp.where(is_first, both[:, :PAIR], both[:, PAIR:]))
        dq_ref[:, lanes] = (jnp.where(lane_even, dq[0], dq[1]) * SCALE).astype(BF16)
        dk = dot_tn(jnp.concatenate(ds, axis=0), jnp.concatenate(qq, axis=0)).astype(BF16)
        dv = dot_tn(
            jnp.concatenate([p_ref[2 * p], p_ref[2 * p + 1]], axis=0), jnp.concatenate(dd, axis=0)
        ).astype(BF16)
        dkv_ref[:n, lanes] = dk[:, :PAIR]
        dkv_ref[n:, lanes] = dk[:, PAIR:]
        dkv_ref[:n, vlanes] = dv[:, :PAIR]
        dkv_ref[n:, vlanes] = dv[:, PAIR:]
    dh = dot_nt(dq_ref[...], w_ref[:, :d])
    normed, inv = norm_parts(x_ref[...])
    d_input, sums = norm_back(dh, normed, inv, vec_ref[0:1, :])
    dx_ref[...] = dy + d_input
    sums_ref[0] = sums


def kv_kernel(x_ref, w_ref, out_ref):
    out_ref[...] = dot(x_ref[...], w_ref[...]).astype(BF16)


def image_back_kernel(dkv_ref, w_ref, theirs_ref, mine_ref):
    half = theirs_ref.shape[1]
    both = dot_nt(dkv_ref[...], w_ref[...])
    theirs_ref[...] = both[:, :half].astype(BF16)
    mine_ref[...] = both[:, half:]


def vec_columns(sums, width):
    rows = sums.shape[0]
    full = jnp.concatenate([sums, jnp.zeros((width - rows, sums.shape[1]), F32)], axis=0)
    return full.T.astype(BF16)


def by_section(tab_ref, first, second, kernel):
    @pl.when(tab_ref[0] == 0)
    def _():
        kernel(*first)

    @pl.when(tab_ref[0] == 1)
    def _():
        kernel(*second)


def store_halves(tab_ref, mine_ref, theirs_ref, rows, cols, value):
    chips = mine_ref.shape[0]
    count = value.shape[0] // (2 * chips)
    pairs = value.reshape(chips, 2, count, value.shape[1])
    here = tab_ref[1] == 0
    mine_ref[:, rows, cols] = jnp.where(here, pairs[:, 0], pairs[:, 1]).astype(BF16)
    theirs_ref[:, rows, cols] = jnp.where(here, pairs[:, 1], pairs[:, 0]).astype(BF16)


def ffn_grads_kernel(tab_ref, *refs):
    mine_ref, theirs_ref = refs[8:]
    d = mine_ref.shape[2]

    def grads(m_ref, du_ref, g_ref, dyb_ref):
        blocks = du_ref.shape[1] // d
        up_rows = m_ref.shape[1] // (2 * mine_ref.shape[0])
        store = partial(store_halves, tab_ref, mine_ref, theirs_ref)
        m = m_ref[...]
        for j in range(blocks):
            part = dot_tn(m, du_ref[:, j * d : (j + 1) * d]).astype(BF16)
            store(slice(j * up_rows, (j + 1) * up_rows), slice(None), part)
        down = dot_tn(g_ref[...], dyb_ref[...]).astype(BF16)
        store(slice(blocks * up_rows, None), slice(None), down)

    by_section(tab_ref, refs[:4], refs[4:8], grads)


def attn_grads_kernel(tab_ref, *refs):
    mine_ref, theirs_ref = refs[12:]

    def grads(h_ref, dqkv_ref, o_ref, dyb_ref, asum_ref, fsum_ref):
        d = dyb_ref.shape[1]
        store = partial(store_halves, tab_ref, mine_ref, theirs_ref, slice(None))
        store(slice(0, 3 * d), dot_tn(h_ref[...], dqkv_ref[...]).astype(BF16))
        store(slice(3 * d, 4 * d), dot_tn(o_ref[...], dyb_ref[...]).astype(BF16))
        sums = jnp.concatenate([jnp.sum(asum_ref[...], axis=0)[:2], jnp.sum(fsum_ref[...], axis=0)[:2]])
        store(slice(4 * d, None), vec_columns(sums, PAIR))

    by_section(tab_ref, refs[:6], refs[6:12], grads)


def cross_grads_kernel(tab_ref, h_ref, dq_ref, image_ref, dkv_ref, o_ref, dyb_ref, sum_ref, mine_ref, theirs_ref):
    d = dyb_ref.shape[1]
    store = partial(store_halves, tab_ref, mine_ref, theirs_ref, slice(None))

    @pl.when(tab_ref[0] == 1)
    def _():
        store(slice(0, d), dot_tn(h_ref[...], dq_ref[...]))
        store(slice(d, 3 * d), dot_tn(image_ref[...], dkv_ref[...]))
        store(slice(3 * d, 4 * d), dot_tn(o_ref[...], dyb_ref[...]))
        store(slice(4 * d, None), vec_columns(jnp.sum(sum_ref[...], axis=0)[:2], PAIR).astype(F32))


def sds(shape, dtype):
    return jax.ShapeDtypeStruct(shape, dtype)


def rows_at(base, rows, cols):
    return pl.BlockSpec((rows, cols), lambda i, tab: (i + base, 0))


def whole_spec(shape):
    return pl.BlockSpec(shape, lambda i, tab: (0,) * len(shape), pipeline_mode=pl.Buffered(1))


ANY_SPEC = pl.BlockSpec(memory_space=pl.ANY)


class Unit(NamedTuple):
    arrays: Any
    moves: Any


def begin(unit, tab_ref, refs, targets, sems):
    copies = []
    for j, (array, start, rows, cols, target, lead, place) in enumerate(unit.moves):
        source = refs[array].at[pl.ds(start, rows)]
        if cols is not None:
            source = refs[array].at[pl.ds(start, rows), pl.ds(*cols)]
        row = 0
        if place is not None:
            offset, other, by_core = place
            chip = at_offset(tab_ref, offset)
            core = 1 - tab_ref[1] if other else tab_ref[1]
            at = core * RING + chip if by_core else chip * CORES + core
            row = pl.multiple_of(at * rows, rows)
        to = targets[target]
        to = to.at[pl.ds(row, rows)] if lead is None else to.at[lead, pl.ds(row, rows)]
        copy = pltpu.make_async_copy(source, to, sems.at[j])
        copy.start()
        copies.append(copy)
    return copies


def finish(copies):
    for copy in copies:
        copy.wait()


def vector_rows(table_ref, *vec_refs):
    rows = table_ref[...].astype(F32).T
    for j, vec_ref in enumerate(vec_refs):
        vec_ref[0:2, :] = rows[2 * j : 2 * j + 2, :]


class Stage(NamedTuple):
    kernel: Any
    only: Any
    steps: int
    ins: Any
    outs: Any
    cost: Any
    units: Any = ()
    scratch: Any = ()
    carried: Any = ()


def pinned(spec, stage, steps):
    index = spec.index_map

    def at(i, tab):
        if stage.steps < steps:
            i = jnp.minimum(i, stage.steps - 1)
        if stage.only is not None:
            i = jnp.where(tab[0] == stage.only, i, 0)
        return index(i, tab)

    return pl.BlockSpec(spec.block_shape, at, pipeline_mode=spec.pipeline_mode)


def taken(refs, count):
    return refs[:count], refs[count:]


def run(tab, stages, after=(), vmem_limit=VMEM_LIMIT):
    steps = max(stage.steps for stage in stages)
    ins = [(array, pinned(spec, stage, steps)) for stage in stages for array, spec in stage.ins]
    loaded = [array for stage in stages for unit in stage.units for array in unit.arrays]
    outs = [(sds(shape, dtype), pinned(spec, stage, steps)) for stage in stages for shape, dtype, spec in stage.outs]
    carried = [buffer for stage in stages for buffer in stage.carried]
    n_skip = len(carried) + len(after)
    aliases, out_base = {}, 0
    for stage in stages:
        out_base += len(stage.outs)
        for j in range(len(stage.carried)):
            aliases[1 + len(ins) + len(loaded) + len(aliases)] = out_base - len(stage.carried) + j

    def body(tab_ref, *refs):
        in_refs, refs = taken(refs, len(ins))
        any_refs, refs = taken(refs, len(loaded))
        out_refs, scratch_refs = taken(refs[n_skip:], len(outs))
        for stage in stages:
            own_in, in_refs = taken(in_refs, len(stage.ins))
            own_any, any_refs = taken(any_refs, sum(len(unit.arrays) for unit in stage.units))
            own_out, out_refs = taken(out_refs, len(stage.outs))
            own_scratch, scratch_refs = taken(scratch_refs, len(stage.scratch))
            part = partial(stage.kernel, tab_ref, *own_in, *own_any, *own_out, *own_scratch)
            wanted = []
            if stage.only is not None:
                wanted.append(tab_ref[0] == stage.only)
            if stage.steps < steps:
                wanted.append(pl.program_id(0) < stage.steps)
            if wanted:
                pl.when(wanted[0] if len(wanted) == 1 else wanted[0] & wanted[1])(part)
            else:
                part()

    results = pl.pallas_call(
        body,
        grid_spec=pltpu.PrefetchScalarGridSpec(
            num_scalar_prefetch=1,
            grid=(steps,),
            in_specs=[spec for _, spec in ins] + [ANY_SPEC] * (len(loaded) + n_skip),
            out_specs=[spec for _, spec in outs],
            scratch_shapes=[shape for stage in stages for shape in stage.scratch],
        ),
        out_shape=[shape for shape, _ in outs],
        input_output_aliases=aliases,
        compiler_params=pltpu.CompilerParams(vmem_limit_bytes=vmem_limit),
        cost_estimate=pl.CostEstimate(
            flops=max(stage.cost[0] for stage in stages),
            bytes_accessed=max(stage.cost[1] for stage in stages),
            transcendentals=0,
        ),
    )(tab, *[array for array, _ in ins], *loaded, *carried, *after)
    split, start = [], 0
    for stage in stages:
        split.append(list(results[start : start + len(stage.outs)]))
        start += len(stage.outs)
    return split


def call(kernel, on, steps, ins, outs, flops, moved, trans=0, carried=(), after=(), vmem_limit=VMEM_LIMIT):
    own = kernel if on[1] is None else lambda tab_ref, *refs: kernel(*refs)
    stage = Stage(own, on[1], steps, ins, outs, (flops, moved), carried=carried)
    if len(on) > 2:
        return stage
    return run(on[0], [stage], after, vmem_limit)[0]


def sums_at(base, d):
    return pl.BlockSpec((1, 8, d), lambda i, tab: (i + base, 0, 0))


def code_at(base):
    return pl.BlockSpec((1, 1, BLOCK), lambda i, tab: (i + base, 0, 0))


def dma(unit):
    return pltpu.SemaphoreType.DMA((len(unit.moves),))


def vmem(shape, dtype=BF16):
    return pltpu.VMEM(shape, dtype)


def first_attention(steps, x, code, code_row, attn):
    t, d = x.shape
    n = len(attn.arrays)

    def kernel(tab_ref, x_ref, code_ref, code_row_ref, *refs):
        pieces, refs = taken(refs, n)
        outs, (w_ref, vec_ref, sems) = taken(refs, 5)

        @pl.when(pl.program_id(0) == 0)
        def _():
            finish(begin(attn, tab_ref, pieces, (w_ref,), sems))
            vector_rows(w_ref.at[:, 4 * d : 4 * d + PAIR], vec_ref)

        self_fwd_kernel(x_ref, vec_ref, code_ref, code_row_ref, w_ref, *outs)

    widths = ((d, F32), (d, BF16), (3 * d, BF16), (HEADS * TILE, BF16), (d, BF16))
    return Stage(
        kernel,
        0,
        steps,
        [(x, rows_at(0, BLOCK, d)), (code, rows_at(0, BLOCK, 1)), (code_row, code_at(0))],
        [((t, wide), dtype, rows_at(0, BLOCK, wide)) for wide, dtype in widths],
        (t * d * 8 * d, d * d * 8 + t * d * 24),
        (attn,),
        (vmem((d, 4 * d + PAIR)), vmem((8, d), F32), dma(attn)),
    )


def first_feed(base, x, ffn, vecs, up_shape, down_shape, carried):
    t, d = x.shape
    ff = down_shape[0]
    n = len(ffn.arrays)

    def kernel(tab_ref, x_ref, *refs):
        pieces, refs = taken(refs, n)
        tables, refs = taken(refs, len(vecs.arrays))
        outs, (up_ref, down_ref, table_ref, unused_ref, vec_ref, sems, vec_sems) = taken(refs, 4)
        copies = begin(ffn, tab_ref, pieces, (up_ref, down_ref), sems)
        finish(begin(vecs, tab_ref, tables, (table_ref,), vec_sems))
        vector_rows(table_ref, unused_ref, vec_ref)
        finish(copies)
        ffn_fwd_kernel(x_ref, vec_ref, up_ref, down_ref, *outs)

    return Stage(
        kernel,
        0,
        1,
        [(x, rows_at(base, BLOCK, d))],
        [((BLOCK, d), BF16, rows_at(0, BLOCK, d))]
        + [((t, wide), BF16, rows_at(base, BLOCK, wide)) for wide in (d, ff, ff)],
        (BLOCK * d * 4 * ff, d * ff * 4),
        (ffn, vecs),
        (
            vmem(up_shape),
            vmem(down_shape),
            vmem((d, PAIR)),
            vmem((8, d), F32),
            vmem((8, d), F32),
            dma(ffn),
            dma(vecs),
        ),
        carried,
    )


def second_layer(base, t, x, code, code_row, image, kv, cot, attn, cross, ffn, up_shape, down_shape, carried):
    d = x.shape[1]
    ff = down_shape[0]
    n = IMG_MB * PATCHES
    nb = t // BLOCK
    counts = [len(unit.arrays) for unit in (attn, cross, ffn)]

    def kernel(tab_ref, x_ref, code_ref, code_row_ref, image_ref, kv_ref, cot_ref, *refs):
        attn_refs, refs = taken(refs, counts[0])
        cross_refs, refs = taken(refs, counts[1])
        ffn_refs, refs = taken(refs, counts[2])
        outs, scratch = taken(refs, 19)
        (y, dxb, h, o, m, g, dy, du, fsum, ch, co, cdy, cdq, cdkv, csum, dx0, dy1, dqkv, asum) = outs
        (wa, wc, up, down, va, vf, vc, x1, qkv, p, cq, cp, x2, slope, dx2, dx1, sa, sc, sf) = scratch
        attn_copies = begin(attn, tab_ref, attn_refs, (wa,), sa)
        cross_copies = begin(cross, tab_ref, cross_refs, (wc,), sc)
        ffn_copies = begin(ffn, tab_ref, ffn_refs, (up, down), sf)
        finish(attn_copies)
        vector_rows(wa.at[:, 4 * d : 4 * d + PAIR], va, vf)
        self_fwd_kernel(x_ref, va, code_ref, code_row_ref, wa, x1, h, qkv, p, o)
        finish(cross_copies)
        vector_rows(wc.at[:, 4 * d : 4 * d + PAIR], vc)
        cross_fwd_kernel(x1, vc, image_ref, kv_ref, wc, x2, ch, cq, cp, co)
        finish(ffn_copies)
        ffn_fwd_kernel(x2, vf, up, down, y, m, g, slope)
        ffn_bwd_kernel(x2, cot_ref, None, vf, slope, up, down, dx2, dy, du, fsum)
        cross_bwd_kernel(x1, dx2, vc, image_ref, cq, cp, kv_ref, wc, dx1, cdy, cdq, cdkv, csum)
        self_bwd_kernel(x_ref, dx1, va, qkv, p, wa, dxb, dx0, dy1, dqkv, asum)

    def rows(wide, dtype=BF16):
        return ((t, wide), dtype, rows_at(base, BLOCK, wide))

    sums = ((nb, 8, d), F32, sums_at(base, d))
    own = ((BLOCK, d), BF16, rows_at(0, BLOCK, d))
    return Stage(
        kernel,
        1,
        1,
        [
            (x, rows_at(0, BLOCK, d)),
            (code, rows_at(base, BLOCK, 1)),
            (code_row, code_at(base)),
            (image, rows_at(base, BLOCK, 1)),
            (kv, rows_at(base, n, 2 * d)),
            (cot, rows_at(base, BLOCK, d)),
        ],
        [own, own, rows(d), rows(d), rows(d), rows(ff), rows(d), rows(ff), sums]
        + [rows(d), rows(d), rows(d), rows(d), ((nb * n, 2 * d), BF16, rows_at(base, n, 2 * d)), sums]
        + [rows(d, F32), rows(d), rows(3 * d), sums],
        (BLOCK * d * 24 * d, d * d * 40),
        (attn, cross, ffn),
        (
            vmem((d, 4 * d + PAIR)),
            vmem((d, 4 * d + PAIR)),
            vmem(up_shape),
            vmem(down_shape),
            vmem((8, d), F32),
            vmem((8, d), F32),
            vmem((8, d), F32),
            vmem((BLOCK, d), F32),
            vmem((BLOCK, 3 * d)),
            vmem((BLOCK, HEADS * TILE)),
            vmem((BLOCK, d)),
            vmem((HEADS, BLOCK, PATCHES)),
            vmem((BLOCK, d), F32),
            vmem((BLOCK, ff)),
            vmem((BLOCK, d), F32),
            vmem((BLOCK, d), F32),
            dma(attn),
            dma(cross),
            dma(ffn),
        ),
        carried,
    )


def first_back(base, x1, cot, more, slope, x, qkv, probs, attn, ffn, up_shape, down_shape, carried):
    t, d = x.shape
    ff = down_shape[0]
    nb = t // BLOCK
    counts = [len(unit.arrays) for unit in (attn, ffn)]

    def kernel(tab_ref, x1_ref, cot_ref, more_ref, slope_ref, x_ref, qkv_ref, p_ref, *refs):
        attn_refs, refs = taken(refs, counts[0])
        ffn_refs, refs = taken(refs, counts[1])
        (dy, du, fsum, dx0, dy1, dqkv, asum), scratch = taken(refs, 7)
        wa, up, down, va, vf, dx1, dxb, sa, sf = scratch
        ffn_copies = begin(ffn, tab_ref, ffn_refs, (up, down), sf)
        finish(begin(attn, tab_ref, attn_refs, (wa,), sa))
        vector_rows(wa.at[:, 4 * d : 4 * d + PAIR], va, vf)
        finish(ffn_copies)
        ffn_bwd_kernel(x1_ref, cot_ref, more_ref, vf, slope_ref, up, down, dx1, dy, du, fsum)
        self_bwd_kernel(x_ref, dx1, va, qkv_ref, p_ref, wa, dxb, dx0, dy1, dqkv, asum)

    def rows(wide, dtype=BF16):
        return ((t, wide), dtype, rows_at(base, BLOCK, wide))

    sums = ((nb, 8, d), F32, sums_at(base, d))
    here = rows_at(base, BLOCK, d)
    return Stage(
        kernel,
        0,
        1,
        [
            (x1, here),
            (cot, here),
            (more, rows_at(0, BLOCK, d)),
            (slope, rows_at(base, BLOCK, ff)),
            (x, here),
            (qkv, rows_at(base, BLOCK, 3 * d)),
            (probs, rows_at(base, BLOCK, HEADS * TILE)),
        ],
        [rows(d), rows(ff), sums, rows(d, F32), rows(d), rows(3 * d), sums],
        (BLOCK * d * 12 * d, d * d * 24),
        (attn, ffn),
        (
            vmem((d, 4 * d + PAIR)),
            vmem(up_shape),
            vmem(down_shape),
            vmem((8, d), F32),
            vmem((8, d), F32),
            vmem((BLOCK, d), F32),
            vmem((BLOCK, d)),
            dma(attn),
            dma(ffn),
        ),
        carried,
    )


def first_feed_back(base, x1, cot, more, slope, ffn, vecs, up_shape, down_shape, carried):
    t, d = x1.shape
    ff = down_shape[0]
    nb = t // BLOCK

    def kernel(tab_ref, x1_ref, cot_ref, more_ref, slope_ref, *refs):
        pieces, refs = taken(refs, len(ffn.arrays))
        tables, refs = taken(refs, len(vecs.arrays))
        (dx1, dy, du, fsum), (up, down, table, va, vf, sf, sv) = taken(refs, 4)
        copies = begin(ffn, tab_ref, pieces, (up, down), sf)
        finish(begin(vecs, tab_ref, tables, (table,), sv))
        vector_rows(table, va, vf)
        finish(copies)
        ffn_bwd_kernel(x1_ref, cot_ref, more_ref, vf, slope_ref, up, down, dx1, dy, du, fsum)

    here = rows_at(base, BLOCK, d)
    return Stage(
        kernel,
        0,
        1,
        [(x1, here), (cot, here), (more, rows_at(0, BLOCK, d)), (slope, rows_at(base, BLOCK, ff))],
        [
            ((BLOCK, d), F32, rows_at(0, BLOCK, d)),
            ((t, d), BF16, here),
            ((t, ff), BF16, rows_at(base, BLOCK, ff)),
            ((nb, 8, d), F32, sums_at(base, d)),
        ],
        (BLOCK * d * 4 * ff, d * d * 16),
        (ffn, vecs),
        (
            vmem(up_shape),
            vmem(down_shape),
            vmem((d, PAIR)),
            vmem((8, d), F32),
            vmem((8, d), F32),
            dma(ffn),
            dma(vecs),
        ),
        carried,
    )


def first_attention_back(base, x, dx1, qkv, probs, attn, carried):
    t, d = x.shape
    nb = t // BLOCK

    def kernel(tab_ref, x_ref, dx1_ref, qkv_ref, p_ref, *refs):
        pieces, refs = taken(refs, len(attn.arrays))
        (dx0, dy1, dqkv, asum), (wa, va, dxb, sa) = taken(refs, 4)
        finish(begin(attn, tab_ref, pieces, (wa,), sa))
        vector_rows(wa.at[:, 4 * d : 4 * d + PAIR], va)
        self_bwd_kernel(x_ref, dx1_ref, va, qkv_ref, p_ref, wa, dxb, dx0, dy1, dqkv, asum)

    here = rows_at(base, BLOCK, d)
    return Stage(
        kernel,
        0,
        1,
        [
            (x, here),
            (dx1, rows_at(0, BLOCK, d)),
            (qkv, rows_at(base, BLOCK, 3 * d)),
            (probs, rows_at(base, BLOCK, HEADS * TILE)),
        ],
        [
            ((t, d), F32, here),
            ((t, d), BF16, here),
            ((t, 3 * d), BF16, rows_at(base, BLOCK, 3 * d)),
            ((nb, 8, d), F32, sums_at(base, d)),
        ],
        (BLOCK * d * 8 * d, d * d * 8),
        (attn,),
        (vmem((d, 4 * d + PAIR)), vmem((8, d), F32), vmem((BLOCK, d)), dma(attn)),
        carried,
    )


def with_unit(kernel, unit, outs):
    def own(tab_ref, x_ref, *refs):
        pieces, refs = taken(refs, len(unit.arrays))
        out_refs, (w_ref, sems) = taken(refs, outs)

        @pl.when(pl.program_id(0) == 0)
        def _():
            finish(begin(unit, tab_ref, pieces, (w_ref,), sems))

        kernel(x_ref, w_ref, *out_refs)

    return own


def image_kv(patches, unit):
    n, d = patches.shape
    return Stage(
        with_unit(kv_kernel, unit, 1),
        1,
        n // PATCHES,
        [(patches, rows_at(0, PATCHES, d))],
        [((n, 2 * d), BF16, rows_at(0, PATCHES, 2 * d))],
        (n * d * d * 4, n * d * 6 + d * d * 4),
        (unit,),
        (vmem((d, 2 * d)), dma(unit)),
    )


def image_back(dkv, unit):
    n, d = dkv.shape[0], dkv.shape[1] // 2
    return Stage(
        with_unit(image_back_kernel, unit, 2),
        1,
        n // PATCHES,
        [(dkv, rows_at(0, PATCHES, 2 * d))],
        [
            ((n, d // 2), BF16, rows_at(0, PATCHES, d // 2)),
            ((n, d // 2), F32, rows_at(0, PATCHES, d // 2)),
        ],
        (n * d * d * 4, n * d * 7 + d * d * 4),
        (unit,),
        (vmem((d, 2 * d)), dma(unit)),
    )


def columns_of(section, rows, cols):
    def index(i, tab):
        return (0, i * (tab[0] if section else 1 - tab[0]))

    return pl.BlockSpec((rows, cols), index)


def sums_of(section, shape):
    def index(i, tab):
        return (0, 0, i * (tab[0] if section else 1 - tab[0]))

    return pl.BlockSpec(shape, index)


def ffn_grads(tab, sets, after=()):
    t, d = sets[0][0].shape
    ff = sets[0][2].shape[1]
    steps = 2
    rows = (ff + 4 * d) // (RING * CORES)
    out = pl.BlockSpec((RING // steps, rows, d), lambda i, tab: (i, 0, 0))
    ins = []
    for section, (m, du, g, dyb) in enumerate(sets):
        ins += [
            (m, columns_of(section, t, d // steps)),
            (du, whole_spec((t, ff))),
            (g, columns_of(section, t, ff // steps)),
            (dyb, whole_spec((t, d))),
        ]
    return call(
        ffn_grads_kernel,
        (tab, None),
        steps,
        ins,
        [((RING, rows, d), BF16, out)] * 2,
        t * d * ff * 4,
        t * (ff + d) * 8 + d * ff * 4,
        after=after,
    )


def attn_grads(tab, sets, after=()):
    t, d = sets[0][0].shape
    steps = 2
    wide = 4 * d + PAIR
    rows = d // (RING * CORES)
    out = pl.BlockSpec((RING // steps, rows, wide), lambda i, tab: (i, 0, 0))
    ins = []
    for section, (h, dqkv, o, dyb, asum, fsum) in enumerate(sets):
        tall = columns_of(section, t, d // steps)
        part = sums_of(section, asum.shape[:2] + (d // steps,))
        ins += [
            (h, tall),
            (dqkv, whole_spec(dqkv.shape)),
            (o, tall),
            (dyb, whole_spec(dyb.shape)),
            (asum, part),
            (fsum, part),
        ]
    return call(
        attn_grads_kernel,
        (tab, None),
        steps,
        ins,
        [((RING, rows, wide), BF16, out)] * 2,
        t * d * d * 8,
        t * d * 24 + d * d * 8,
        after=after,
    )


def cross_grads(on, h, dq, patches, dkv, o, dyb, sums, after=()):
    t, d = h.shape
    n = patches.shape[0]
    steps = CORES
    tall = columns_of(1, t, d // steps)
    wide = 4 * d + PAIR
    rows = d // (2 * RING * CORES)
    out = ((2 * RING, rows, wide), BF16, pl.BlockSpec((RING, rows, wide), lambda i, tab: (i, 0, 0)))
    return call(
        cross_grads_kernel,
        on,
        steps,
        [
            (h, tall),
            (dq, whole_spec(dq.shape)),
            (patches, columns_of(1, n, d // steps)),
            (dkv, whole_spec(dkv.shape)),
            (o, tall),
            (dyb, whole_spec(dyb.shape)),
            (sums, sums_of(1, sums.shape[:2] + (d // steps,))),
        ],
        [out, out],
        t * d * d * 4 + n * d * d * 4,
        t * d * 8 + n * d * 6 + d * d * 8,
        after=after,
    )


def at_offset(tab, offset):
    return tab[2 + RING // 2 + offset]


def join_kernel(tab_ref, *refs, extra):
    mine_ref, theirs_ref = refs[:2]
    moving_refs, out_ref = refs[2 + extra : -1], refs[-1]
    rows = mine_ref.shape[1]
    parts = [(slice(0, rows), mine_ref[0].astype(F32) + theirs_ref[0].astype(F32))]
    if extra:
        more = jnp.where(tab_ref[0] == 0, refs[2][0], refs[3][0]).astype(F32)
        parts.append((slice(rows, rows + more.shape[0]), more))
    for at, value in parts:
        for ref in moving_refs:
            value = value + ref[at, :].astype(F32)
        out_ref[at, :] = value.astype(out_ref.dtype)


def join(tab, offset, mine, theirs, extra, moving, dtype, after=()):
    cols = mine.shape[2]

    def part(array):
        return (array, pl.BlockSpec((1,) + array.shape[1:], lambda i, tab: (at_offset(tab, offset), 0, 0)))

    rows = mine.shape[1] + (extra[0].shape[1] if extra else 0)
    piece = pl.BlockSpec((rows, cols), lambda i, tab: (0, 0))
    return call(
        partial(join_kernel, extra=len(extra)),
        (tab, None),
        1,
        [part(array) for array in (mine, theirs) + tuple(extra)] + [(array, piece) for array in moving],
        [((rows, cols), dtype, piece)],
        rows * cols * 3,
        rows * cols * 2 * (3 + len(moving)),
        after=after,
        vmem_limit=SMALL_LIMIT,
    )[0]


def cross_join_kernel(tab_ref, mine_ref, theirs_ref, first_ref, second_ref):
    value = (mine_ref[...].astype(F32) + theirs_ref[...].astype(F32)).astype(BF16)

    @pl.when(pl.program_id(0) == 0)
    def _():
        first_ref[...] = value

    @pl.when(pl.program_id(0) == 1)
    def _():
        second_ref[...] = value


def cross_join(mine, theirs):
    shape = (RING,) + mine.shape[1:]
    part = pl.BlockSpec(shape, lambda i, tab: (i, 0, 0))
    out = (shape, BF16, pl.BlockSpec(shape, lambda i, tab: (0, 0, 0)))
    return Stage(cross_join_kernel, 1, 2, [(mine, part), (theirs, part)], [out, out], (mine.size, mine.size * 6))


def pick_kernel(tab_ref, first_ref, second_ref, out_ref):
    def copy(ref):
        out_ref[...] = ref[...].astype(out_ref.dtype)

    by_section(tab_ref, (first_ref,), (second_ref,), copy)


def pick(tab, first, second, steps, dtype, after=()):
    rows, cols = first.shape
    spec = rows_at(0, rows // steps, cols)
    return call(
        pick_kernel,
        (tab, None),
        steps,
        [(first, spec), (second, spec)],
        [((rows, cols), dtype, spec)],
        0,
        rows * cols * 12,
        after=after,
        vmem_limit=SMALL_LIMIT,
    )[0]


def cross_chunk_kernel(tab_ref, one_ref, two_ref, own_ref, out_ref):
    rows = one_ref.shape[0]
    out_ref[:rows, :] = one_ref[...]
    out_ref[rows:, :] = jnp.where(tab_ref[1] == 0, two_ref[...], own_ref[...])


def cross_chunk_of(tab, one, two, own, after):
    rows, cols = one.shape
    part = rows_at(0, rows, cols)
    return call(
        cross_chunk_kernel,
        (tab, None),
        1,
        [(one, part), (two, part), (own, part)],
        [((2 * rows, cols), BF16, rows_at(0, 2 * rows, cols))],
        0,
        rows * cols * 10,
        after=after,
        vmem_limit=SMALL_LIMIT,
    )[0]


def ring_tables():
    half = RING // 2
    chip_at = [2 * z for z in range(half)] + [2 * z + 1 for z in range(half - 1, -1, -1)]
    pos_of = [chip_at.index(chip) for chip in range(RING)]
    return chip_at, pos_of


CHIP_AT, POS_OF = ring_tables()


def flat(section, chip, core):
    return section * RING * CORES + chip * CORES + core


def ring_pairs(sections, step):
    return [
        (flat(s, CHIP_AT[i], c), flat(s, CHIP_AT[(i + step) % RING], c))
        for s in sections
        for i in range(RING)
        for c in range(CORES)
    ]


def core_pairs(sections):
    return [
        (flat(s, chip, c), flat(s, chip, 1 - c))
        for s in sections
        for chip in range(RING)
        for c in range(CORES)
    ]


def send(x, pairs):
    return lax.ppermute(x, ("section", "dp"), pairs)


def tie(x, *deps):
    return lax.optimization_barrier((x, *deps))[0] if deps else x


def device_table():
    rank = lax.axis_index("dp")
    pos = jnp.asarray(POS_OF, jnp.int32)[rank // CORES % RING]
    offsets = jnp.arange(-(RING // 2), RING // 2 + 1, dtype=jnp.int32)
    chips = jnp.asarray(CHIP_AT, jnp.int32)[(pos + offsets + RING) % RING]
    here = jnp.stack([lax.axis_index("section"), rank % CORES]).astype(jnp.int32)
    return jnp.concatenate([here, chips])


class Gather:
    def __init__(self, chunk, sections, long_way, by_core):
        self.chunk, self.sections, self.long_way, self.by_core = chunk, sections, long_way, by_core
        self.arrived = {1: [], -1: []}

    def step(self, *deps):
        done = len(self.arrived[self.long_way])
        ways = [way for way in (1, -1) if done < RING // 2 - 1 or way == self.long_way]
        held = {way: self.arrived[way][-1] if done else self.chunk for way in ways}
        for way in ways:
            self.arrived[way].append(send(tie(held[way], *deps), ring_pairs(self.sections, way)))

    def third(self):
        return [self.arrived[way][2] for way in (1, -1)]

    def pieces(self):
        held = [(0, self.chunk)]
        for step in range(1, RING // 2 + 1):
            held += [
                (-way * step, self.arrived[way][step - 1]) for way in (1, -1) if step <= len(self.arrived[way])
            ]
        pieces, places = [], []
        for offset, piece in held:
            pieces += [piece, send(piece, core_pairs(self.sections))]
            places += [(offset, False, self.by_core), (offset, True, self.by_core)]
        return pieces, tuple(places)


class Order:
    def __init__(self):
        self.last = ()

    def mark(self, *outputs):
        self.last = outputs
        return outputs[0]


class Scatter:
    def __init__(self, tab, order, mine, out, sections, long_way, extra=()):
        self.tab, self.order, self.mine = tab, order, mine
        self.sections, self.long_way, self.extra = sections, long_way, extra
        self.theirs = send(out, core_pairs(sections))
        self.moving = {1: [], -1: []}
        self.done = 0

    def step(self):
        for way in (1, -1):
            hops = RING // 2 if way == self.long_way else RING // 2 - 1
            if self.done < hops:
                piece = join(
                    self.tab,
                    way * (hops - self.done),
                    self.mine,
                    self.theirs,
                    self.extra,
                    self.moving[way],
                    BF16,
                    self.order.last,
                )
                self.order.mark(piece)
                self.moving[way] = [send(piece, ring_pairs(self.sections, way))]
        self.done += 1

    def finish(self):
        moving = self.moving[1] + self.moving[-1]
        return self.order.mark(join(self.tab, 0, self.mine, self.theirs, self.extra, moving, F32, self.order.last))


def lanes_of(vectors, width):
    table = jnp.stack(vectors, axis=1)
    return jnp.pad(table, ((0, 0), (0, width - table.shape[1])))


def local(
    tokens,
    images,
    segments,
    image_ids,
    cotangent,
    norm_gain,
    norm_bias,
    qkv_weight,
    out_weight,
    up_weight,
    down_weight,
    cross_gain,
    cross_bias,
    cross_query,
    cross_kv,
    cross_out,
):
    section = lax.axis_index("section")
    multimodal = section == 1
    tab = device_table()
    t, d = tokens.shape
    ff = up_weight.shape[2]
    nb = t // BLOCK
    members = lax.axis_size("dp")
    ringed = members == RING * CORES and lax.axis_size("section") == 2
    up_rows, down_rows = up_weight.shape[1], down_weight.shape[1]
    split = ff // d

    attn_piece = jnp.concatenate(
        [
            qkv_weight[0],
            out_weight[0],
            lanes_of([norm_gain[0, 0], norm_bias[0, 0], norm_gain[0, 1], norm_bias[0, 1]], PAIR),
        ],
        axis=1,
    ).astype(BF16)
    ffn_piece = jnp.concatenate(
        [up_weight[0, :, j * d : (j + 1) * d] for j in range(split)] + [down_weight[0]], axis=0
    ).astype(BF16)
    cross_piece = jnp.concatenate(
        [cross_query, cross_kv, cross_out, lanes_of([cross_gain, cross_bias], PAIR)], axis=1
    ).astype(BF16)

    row_in_tile = lax.broadcasted_iota(jnp.int32, segments.shape, 0) % (TILE // ROW_LEN)
    code = (row_in_tile * (SEGS + 1) + segments).reshape(-1)
    code_col = code[:, None]
    code_row = code.reshape(nb, 1, BLOCK)
    slots = lax.broadcasted_iota(jnp.int32, (1, 1, SEGS), 2)
    token_image = jnp.sum(
        jnp.where(segments[:, :, None] == slots, image_ids[:, None, :], 0), axis=-1
    )
    image_col = token_image.reshape(-1, 1).astype(F32)
    patches = images.reshape(-1, d)

    up_shape, down_shape = (split, d, d), (ff, d)
    wide = attn_piece.shape[1]
    cot = cotangent[0]
    order = Order()
    if ringed:
        both, s1 = (0, 1), (1,)
        attn_ring = Gather(attn_piece, both, 1, False)
        ffn_ring = Gather(ffn_piece, both, -1, False)
        for _ in range(RING // 2):
            attn_ring.step()
            ffn_ring.step()
        one = send(
            cross_piece,
            [(flat(0, k, 0), flat(1, k, 0)) for k in range(RING)]
            + [(flat(1, k, 0), flat(1, k, 1)) for k in range(RING)],
        )
        two = send(cross_piece, [(flat(0, k, 1), flat(1, k, 0)) for k in range(RING)])
        core = lax.axis_index("dp") % CORES
        cross_chunk = jnp.concatenate([one, jnp.where(core == 0, two, cross_piece)], axis=0)
        cross_ring = Gather(cross_chunk, s1, -1, True)
        for _ in range(RING // 2):
            cross_ring.step()

        def unit_of(ring, layout):
            pieces, places = ring.pieces()
            moves = [
                (j, start, rows, cols, target, lead, place)
                for j, place in enumerate(places)
                for start, rows, cols, target, lead in layout
            ]
            return Unit(pieces, moves)

        def columns_of_unit(unit, cols):
            return Unit(unit.arrays, [move[:3] + (cols,) + move[4:] for move in unit.moves])

        attn = unit_of(attn_ring, [(0, up_rows, None, 0, None)])
        cross = unit_of(cross_ring, [(0, up_rows, None, 0, None)])
        ffn = unit_of(
            ffn_ring,
            [(j * up_rows, up_rows, None, 0, j) for j in range(split)]
            + [(split * up_rows, down_rows, None, 1, None)],
        )
    else:
        w_attn = lax.all_gather(attn_piece, "dp", axis=0, tiled=True)
        w_ffn = lax.all_gather(ffn_piece, "dp", axis=0, tiled=False)
        w_up = w_ffn[:, : split * up_rows].reshape(members, split, up_rows, d).swapaxes(0, 1).reshape(up_shape)
        w_down = w_ffn[:, split * up_rows :].reshape(down_shape)
        w_cross = lax.all_gather(cross_piece, ("section", "dp"), axis=0, tiled=True)

        def columns_of_unit(unit, cols):
            return Unit(unit.arrays, [move[:3] + (cols,) + move[4:] for move in unit.moves])

        attn = Unit([w_attn], [(0, 0, d, None, 0, None, None)])
        cross = Unit([w_cross], [(0, 0, d, None, 0, None, None)])
        ffn = Unit(
            [w_up.reshape(split * d, d), w_down],
            [(0, j * d, d, None, 0, j, None) for j in range(split)] + [(1, 0, ff, None, 1, None, None)],
        )
    vecs = columns_of_unit(attn, (4 * d, PAIR))
    kv_unit = columns_of_unit(cross, (d, 2 * d))

    ((a_x1, a_h, a_qkv, a_p, a_o),) = run(tab, [first_attention(nb, tokens, code_col, code_row, attn)])
    a_y, kept = [], ()
    for b in range(nb):
        stages = [first_feed(b, a_x1, ffn, vecs, up_shape, down_shape, kept)]
        if b == nb - 1:
            stages.append(image_kv(patches, kv_unit))
        (y, *kept), *more = run(tab, stages, a_y)
        a_y.append(y)
    a_m, a_g, a_slope = kept
    ((kv,),) = more
    arrived = [lax.ppermute(y, "section", [(0, 1)]) for y in a_y]

    b_y, leaving, kept = [], [], ()
    for b in range(nb):
        ((y, low, *kept),) = run(
            tab,
            [
                second_layer(
                    b, t, arrived[b], code_col, code_row, image_col, kv, cot, attn, cross, ffn, up_shape, down_shape, kept
                )
            ],
        )
        b_y.append(y)
        leaving.append(low)
    (b_h, b_o, b_m, b_g, b_dy, b_du, b_fsum, c_h, c_o, c_dy, c_dq, c_dkv, c_sum) = kept[:13]
    b_dx0, b_dy1, b_dqkv, b_asum = kept[13:]
    returning = [lax.ppermute(low, "section", [(1, 0)]) for low in leaving]

    def layer_zero_back(b, kept):
        return first_back(
            b, a_x1, cot, returning[b], a_slope, tokens, a_qkv, a_p, attn, ffn, up_shape, down_shape, kept
        )

    def cross_terms():
        return jnp.concatenate(
            [dot_tn(c_h, c_dq), dot_tn(patches, c_dkv), dot_tn(c_o, c_dy), columns(c_sum)], axis=1
        )

    def columns(*sums):
        table = jnp.concatenate([jnp.sum(part, axis=0)[:2] for part in sums]).T
        return jnp.pad(table, ((0, 0), (0, PAIR - table.shape[1])))

    if ringed:
        later1, later = (tab, 1, True), (tab, None, True)
        (kept,) = run(tab, [layer_zero_back(0, ())], leaving)
        feed_kept, attn_kept = kept[:3], kept[3:]
        (a_dx1, a_dy, a_du, a_fsum), (c_mine, c_out) = run(
            tab,
            [
                first_feed_back(1, a_x1, cot, returning[1], a_slope, ffn, vecs, up_shape, down_shape, feed_kept),
                cross_grads(later, c_h, c_dq, patches, c_dkv, c_o, c_dy, c_sum),
            ],
        )
        order.mark(c_mine)
        c_theirs = send(c_out, core_pairs(s1))
        ffn_mine, ffn_out = ffn_grads(
            tab, ((a_m, a_du, a_g, a_dy), (b_m, b_du, b_g, b_dy)), order.last
        )
        order.mark(ffn_mine)
        ffn_sum = Scatter(tab, order, ffn_mine, ffn_out, both, 1)
        (a_dx0, a_dy1, a_dqkv, a_asum), (c_first, c_second), (image_theirs, image_mine) = run(
            tab,
            [
                first_attention_back(1, tokens, a_dx1, a_qkv, a_p, attn, attn_kept),
                cross_join(c_mine, c_theirs),
                image_back(c_dkv, kv_unit),
            ],
            order.last,
        )
        order.mark(a_asum)
        c_first = lax.ppermute(c_first, "section", [(1, 0)])
        image_theirs = lax.ppermute(image_theirs, "section", [(1, 0)])
        ffn_sum.step()
        attn_mine, attn_out = attn_grads(
            tab,
            (
                (a_h, a_dqkv, a_o, a_dy1, a_asum, a_fsum),
                (b_h, b_dqkv, b_o, b_dy1, b_asum, b_fsum),
            ),
            order.last,
        )
        order.mark(attn_mine)
        attn_sum = Scatter(tab, order, attn_mine, attn_out, both, -1, (c_first, c_second))
        while ffn_sum.done < RING // 2:
            ffn_sum.step()
            attn_sum.step()
        ffn_g = ffn_sum.finish()
        attn_sum.step()
        image_shard = pick(tab, image_theirs, image_mine, images.shape[0], F32, order.last)
        order.mark(image_shard)
        attn_g = attn_sum.finish()
        attn_g, cross_g = attn_g[: attn_mine.shape[1]], attn_g[attn_mine.shape[1] :]
    else:

        def summed(first, second):
            grads = jnp.where(multimodal, second, first)
            return lax.psum_scatter(grads, "dp", scatter_dimension=0, tiled=True)

        def ffn_terms(m, du, g, dyb):
            up = dot_tn(m, du).reshape(members, up_rows, split, d).swapaxes(1, 2)
            down = dot_tn(g, dyb).reshape(members, down_rows, d)
            return jnp.concatenate([up.reshape(members, split * up_rows, d), down], axis=1)

        def attn_terms(h, dqkv, o, dyb, asum, fsum):
            return jnp.concatenate([dot_tn(h, dqkv), dot_tn(o, dyb), columns(asum, fsum)], axis=1)

        kept = ()
        for b in range(nb):
            (kept,) = run(tab, [layer_zero_back(b, kept)])
        a_dy, a_du, a_fsum, a_dx0, a_dy1, a_dqkv, a_asum = kept
        ((image_theirs, image_mine),) = run(tab, [image_back(c_dkv, kv_unit)])
        image_theirs = lax.ppermute(image_theirs, "section", [(1, 0)])
        image_shard = jnp.where(multimodal, image_mine, image_theirs.astype(F32))
        ffn_g = summed(ffn_terms(a_m, a_du, a_g, a_dy), ffn_terms(b_m, b_du, b_g, b_dy))[0]
        attn_g = summed(
            attn_terms(a_h, a_dqkv, a_o, a_dy1, a_asum, a_fsum),
            attn_terms(b_h, b_dqkv, b_o, b_dy1, b_asum, b_fsum),
        )
        cross_g = lax.psum_scatter(
            jnp.where(multimodal, cross_terms(), 0.0),
            ("section", "dp"),
            scatter_dimension=0,
            tiled=True,
        )

    vec_g = attn_g[:, 4 * d : 4 * d + 4].T
    up_g = jnp.concatenate([ffn_g[j * up_rows : (j + 1) * up_rows] for j in range(split)], axis=1)
    return (
        jnp.where(multimodal, jnp.concatenate(b_y), jnp.concatenate(a_y))[None],
        jnp.where(multimodal, b_dx0, a_dx0)[None],
        image_shard.reshape(images.shape[0], images.shape[1], d // 2),
        jnp.stack([vec_g[0], vec_g[2]])[None],
        jnp.stack([vec_g[1], vec_g[3]])[None],
        attn_g[None, :, : 3 * d],
        attn_g[None, :, 3 * d : 4 * d],
        up_g[None],
        ffn_g[None, split * up_rows :],
        cross_g[:, 4 * d],
        cross_g[:, 4 * d + 1],
        cross_g[:, :d],
        cross_g[:, d : 3 * d],
        cross_g[:, 3 * d : 4 * d],
    )


def solution(mesh):
    in_specs = (
        P("dp", None),
        P("dp", None, None),
        P("dp", None),
        P("dp", None),
        P("section", "dp", None),
        P("section", None, "dp"),
        P("section", None, "dp"),
        P("section", "dp", None),
        P("section", "dp", None),
        P("section", "dp", None),
        P("section", "dp", None),
        P(("section", "dp")),
        P(("section", "dp")),
        P(("section", "dp"), None),
        P(("section", "dp"), None),
        P(("section", "dp"), None),
    )
    out_specs = (
        P("section", "dp", None),
        P("section", "dp", None),
        P("dp", None, "section"),
        P("section", None, "dp"),
        P("section", None, "dp"),
        P("section", "dp", None),
        P("section", "dp", None),
        P("section", "dp", None),
        P("section", "dp", None),
        P(("section", "dp")),
        P(("section", "dp")),
        P(("section", "dp"), None),
        P(("section", "dp"), None),
        P(("section", "dp"), None),
    )
    return jax.shard_map(local, mesh=mesh, in_specs=in_specs, out_specs=out_specs, check_vma=False)
```

```python
from functools import partial
from typing import Any, NamedTuple

import jax
import jax.numpy as jnp
import numpy as np
from jax import lax
from jax.experimental import pallas as pl
from jax.experimental.pallas import tpu as pltpu
from jax.sharding import PartitionSpec as P

HEADS = 12
HEAD_DIM = 64
PATCHES = 576
ROW_LEN = 64
SEGS = 3
IMG_MB = 2
ROWS_MB = 4
CORES = 2
RING = 8
BLOCK = ROWS_MB * ROW_LEN
PAIR = 2 * HEAD_DIM
PAIRS = HEADS // 2
TILE = 2 * ROW_LEN
MASKED_SCORE = -1000000000.0
NORM_EPS = 1e-05
SCALE = HEAD_DIM ** (-0.5)
VMEM_LIMIT = 56 * 1024 * 1024
SMALL_LIMIT = 12 * 1024 * 1024

F32 = jnp.float32
BF16 = jnp.bfloat16


def dot(a, b):
    return lax.dot_general(a, b, (((1,), (0,)), ((), ())), preferred_element_type=F32)


def dot_nt(a, b):
    return lax.dot_general(a, b, (((1,), (1,)), ((), ())), preferred_element_type=F32)


def dot_tn(a, b):
    return lax.dot_general(a, b, (((0,), (0,)), ((), ())), preferred_element_type=F32)


def norm_parts(x):
    mean = jnp.mean(x, axis=-1, keepdims=True)
    centred = x - mean
    inv = lax.rsqrt(jnp.mean(centred * centred, axis=-1, keepdims=True) + NORM_EPS)
    return centred * inv, inv


def norm_back(d_out, normed, inv, gain):
    d_normed = d_out * gain
    d_input = inv * (
        d_normed
        - jnp.mean(d_normed, axis=-1, keepdims=True)
        - normed * jnp.mean(d_normed * normed, axis=-1, keepdims=True)
    )
    sums = jnp.concatenate(
        [
            jnp.sum(d_out * normed, axis=0, keepdims=True),
            jnp.sum(d_out, axis=0, keepdims=True),
            jnp.zeros((6, d_out.shape[1]), F32),
        ],
        axis=0,
    )
    return d_input, sums


def lane_masks(dtype):
    lane = lax.broadcasted_iota(jnp.int32, (1, PAIR), 1)
    even = (lane < HEAD_DIM).astype(F32)
    return even.astype(dtype), (1.0 - even).astype(dtype)


def softmax(scores):
    top = jnp.max(scores, axis=-1, keepdims=True)
    e = jnp.exp(scores - top)
    return (e * (1.0 / jnp.sum(e, axis=-1, keepdims=True))).astype(BF16)


def stack_heads(part, even, odd):
    return jnp.concatenate([part * even, part * odd], axis=0)


def self_fwd_kernel(x_ref, vec_ref, code_ref, code_row_ref, w_ref, x1_ref, h_ref, qkv_ref, p_ref, o_ref):
    d = x_ref.shape[1]
    x = x_ref[...].astype(F32)
    normed, _ = norm_parts(x)
    h = (normed * vec_ref[0:1, :] + vec_ref[1:2, :]).astype(BF16)
    h_ref[...] = h
    qkv_ref[...] = dot(h, w_ref[:, : 3 * d]).astype(BF16)
    even, odd = lane_masks(BF16)
    for t in range(BLOCK // TILE):
        rows = slice(t * TILE, (t + 1) * TILE)
        causal = lax.broadcasted_iota(jnp.int32, (TILE, TILE), 1) <= lax.broadcasted_iota(
            jnp.int32, (TILE, TILE), 0
        )
        allowed = (code_ref[rows, 0:1] == code_row_ref[0, :, rows]) & causal
        for p in range(PAIRS):
            lanes = slice(p * PAIR, (p + 1) * PAIR)
            q = qkv_ref[rows, lanes] * jnp.asarray(SCALE, BF16)
            k2 = stack_heads(qkv_ref[rows, d + p * PAIR : d + (p + 1) * PAIR], even, odd)
            v2 = stack_heads(qkv_ref[rows, 2 * d + p * PAIR : 2 * d + (p + 1) * PAIR], even, odd)
            s = dot_nt(q, k2)
            probs = jnp.concatenate(
                [
                    softmax(jnp.where(allowed, s[:, :TILE], MASKED_SCORE)),
                    softmax(jnp.where(allowed, s[:, TILE:], MASKED_SCORE)),
                ],
                axis=1,
            )
            p_ref[rows, 2 * p * TILE : 2 * (p + 1) * TILE] = probs
            o_ref[rows, lanes] = dot(probs, v2).astype(BF16)
    x1_ref[...] = x + dot(o_ref[...], w_ref[:, 3 * d : 4 * d])


def self_bwd_kernel(x_ref, dy_ref, vec_ref, qkv_ref, p_ref, w_ref, dxb_ref, dx_ref, dyb_ref, dqkv_ref, sums_ref):
    d = x_ref.shape[1]
    dy = dy_ref[...]
    dyb = dy.astype(BF16)
    dyb_ref[...] = dyb
    d_mixed = dot_nt(dyb, w_ref[:, 3 * d : 4 * d]).astype(BF16)
    even, odd = lane_masks(BF16)
    for t in range(BLOCK // TILE):
        rows = slice(t * TILE, (t + 1) * TILE)
        for p in range(PAIRS):
            lanes = slice(p * PAIR, (p + 1) * PAIR)
            q2 = stack_heads(qkv_ref[rows, lanes] * jnp.asarray(SCALE, BF16), even, odd)
            k2 = stack_heads(qkv_ref[rows, d + p * PAIR : d + (p + 1) * PAIR], even, odd)
            v2 = stack_heads(qkv_ref[rows, 2 * d + p * PAIR : 2 * d + (p + 1) * PAIR], even, odd)
            do = d_mixed[rows, lanes]
            do2 = stack_heads(do, even, odd)
            dp = dot_nt(do, v2)
            probs_e = p_ref[rows, 2 * p * TILE : (2 * p + 1) * TILE]
            probs_o = p_ref[rows, (2 * p + 1) * TILE : (2 * p + 2) * TILE]
            ds = []
            for probs, part in ((probs_e, dp[:, :TILE]), (probs_o, dp[:, TILE:])):
                pf = probs.astype(F32)
                term = pf * part
                ds.append((term - pf * jnp.sum(term, axis=-1, keepdims=True)).astype(BF16))
            dq = dot(jnp.concatenate(ds, axis=1), k2) * SCALE
            dk = dot_tn(jnp.concatenate(ds, axis=0), q2)
            dv = dot_tn(jnp.concatenate([probs_e, probs_o], axis=0), do2)
            dqkv_ref[rows, lanes] = dq.astype(BF16)
            dqkv_ref[rows, d + p * PAIR : d + (p + 1) * PAIR] = dk.astype(BF16)
            dqkv_ref[rows, 2 * d + p * PAIR : 2 * d + (p + 1) * PAIR] = dv.astype(BF16)
    dh = dot_nt(dqkv_ref[...], w_ref[:, : 3 * d])
    normed, inv = norm_parts(x_ref[...].astype(F32))
    d_input, sums = norm_back(dh, normed, inv, vec_ref[0:1, :])
    dx = dy + d_input
    dx_ref[...] = dx
    dxb_ref[...] = dx.astype(BF16)
    sums_ref[0] = sums


def gelu_parts(u):
    phi = 0.5 + 0.5 * lax.erf(u * (0.5**0.5))
    slope = phi + u * (jnp.exp(-0.5 * (u * u)) * ((2.0 * np.pi) ** -0.5))
    return u * phi, slope


def ffn_fwd_kernel(x_ref, vec_ref, up_ref, down_ref, y_ref, m_ref, g_ref, slope_ref):
    d = x_ref.shape[1]
    x = x_ref[...]
    normed, _ = norm_parts(x)
    m = (normed * vec_ref[0:1, :] + vec_ref[1:2, :]).astype(BF16)
    m_ref[...] = m
    acc = x
    for j in range(up_ref.shape[0]):
        cols = slice(j * d, (j + 1) * d)
        g, slope = gelu_parts(dot(m, up_ref[j]))
        g = g.astype(BF16)
        g_ref[:, cols] = g
        slope_ref[:, cols] = slope.astype(BF16)
        acc = acc + dot(g, down_ref[cols, :])
    y_ref[...] = acc.astype(y_ref.dtype)


def ffn_bwd_kernel(x_ref, dy_ref, more_ref, vec_ref, slope_ref, up_ref, down_ref, dx_ref, dyb_ref, du_ref, sums_ref):
    d = x_ref.shape[1]
    dy = dy_ref[...].astype(F32)
    if more_ref is not None:
        dy = dy + more_ref[...].astype(F32)
    dyb = dy.astype(BF16)
    dyb_ref[...] = dyb
    acc = None
    for j in range(up_ref.shape[0]):
        cols = slice(j * d, (j + 1) * d)
        du = (dot_nt(dyb, down_ref[cols, :]) * slope_ref[:, cols].astype(F32)).astype(BF16)
        du_ref[:, cols] = du
        part = dot_nt(du, up_ref[j])
        acc = part if acc is None else acc + part
    normed, inv = norm_parts(x_ref[...])
    d_input, sums = norm_back(acc, normed, inv, vec_ref[0:1, :])
    dx_ref[...] = dy + d_input
    sums_ref[0] = sums


def tied(part, first, second):
    return jnp.concatenate([part * first, part * second], axis=1)


def cross_fwd_kernel(x_ref, vec_ref, image_ref, kv_ref, w_ref, x2_ref, h_ref, q_ref, p_ref, o_ref):
    d = x_ref.shape[1]
    n = PATCHES
    x = x_ref[...]
    normed, _ = norm_parts(x)
    h = (normed * vec_ref[0:1, :] + vec_ref[1:2, :]).astype(BF16)
    h_ref[...] = h
    q_ref[...] = dot(h, w_ref[:, :d]).astype(BF16)
    even, odd = lane_masks(BF16)
    image = image_ref[:, 1:2].astype(F32)
    second = image.astype(BF16)
    first = (1.0 - image).astype(BF16)
    lane_even = lax.broadcasted_iota(jnp.int32, (BLOCK, PAIR), 1) < HEAD_DIM
    is_first = jnp.broadcast_to(image, (BLOCK, PAIR)) < 0.5
    for p in range(PAIRS):
        lanes = slice(p * PAIR, (p + 1) * PAIR)
        vlanes = slice(d + p * PAIR, d + (p + 1) * PAIR)
        k2 = jnp.concatenate([kv_ref[:n, lanes], kv_ref[n:, lanes]], axis=1)
        v2 = jnp.concatenate([kv_ref[:n, vlanes], kv_ref[n:, vlanes]], axis=1)
        q = q_ref[:, lanes] * jnp.asarray(SCALE, BF16)
        out = []
        for half, mask in enumerate((even, odd)):
            probs = softmax(dot_nt(tied(q * mask, first, second), k2))
            p_ref[2 * p + half] = probs
            both = dot(probs, v2)
            out.append(jnp.where(is_first, both[:, :PAIR], both[:, PAIR:]))
        o_ref[:, lanes] = jnp.where(lane_even, out[0], out[1]).astype(BF16)
    x2_ref[...] = x + dot(o_ref[...], w_ref[:, 3 * d : 4 * d])


def cross_bwd_kernel(
    x_ref, dy_ref, vec_ref, image_ref, q_ref, p_ref, kv_ref, w_ref, dx_ref, dyb_ref, dq_ref, dkv_ref, sums_ref
):
    d = x_ref.shape[1]
    n = PATCHES
    dy = dy_ref[...]
    dyb = dy.astype(BF16)
    dyb_ref[...] = dyb
    d_mixed = dot_nt(dyb, w_ref[:, 3 * d : 4 * d]).astype(BF16)
    even, odd = lane_masks(BF16)
    image = image_ref[:, 1:2].astype(F32)
    second = image.astype(BF16)
    first = (1.0 - image).astype(BF16)
    lane_even = lax.broadcasted_iota(jnp.int32, (BLOCK, PAIR), 1) < HEAD_DIM
    is_first = jnp.broadcast_to(image, (BLOCK, PAIR)) < 0.5
    for p in range(PAIRS):
        lanes = slice(p * PAIR, (p + 1) * PAIR)
        vlanes = slice(d + p * PAIR, d + (p + 1) * PAIR)
        k2 = jnp.concatenate([kv_ref[:n, lanes], kv_ref[n:, lanes]], axis=1)
        v2 = jnp.concatenate([kv_ref[:n, vlanes], kv_ref[n:, vlanes]], axis=1)
        q = q_ref[:, lanes] * jnp.asarray(SCALE, BF16)
        do = d_mixed[:, lanes]
        ds, qq, dd, dq = [], [], [], []
        for half, mask in enumerate((even, odd)):
            qq.append(tied(q * mask, first, second))
            dd.append(tied(do * mask, first, second))
            dp = dot_nt(dd[half], v2)
            pf = p_ref[2 * p + half].astype(F32)
            term = pf * dp
            ds.append((term - pf * jnp.sum(term, axis=-1, keepdims=True)).astype(BF16))
            both = dot(ds[half], k2)
            dq.append(jnp.where(is_first, both[:, :PAIR], both[:, PAIR:]))
        dq_ref[:, lanes] = (jnp.where(lane_even, dq[0], dq[1]) * SCALE).astype(BF16)
        dk = dot_tn(jnp.concatenate(ds, axis=0), jnp.concatenate(qq, axis=0)).astype(BF16)
        dv = dot_tn(
            jnp.concatenate([p_ref[2 * p], p_ref[2 * p + 1]], axis=0), jnp.concatenate(dd, axis=0)
        ).astype(BF16)
        dkv_ref[:n, lanes] = dk[:, :PAIR]
        dkv_ref[n:, lanes] = dk[:, PAIR:]
        dkv_ref[:n, vlanes] = dv[:, :PAIR]
        dkv_ref[n:, vlanes] = dv[:, PAIR:]
    dh = dot_nt(dq_ref[...], w_ref[:, :d])
    normed, inv = norm_parts(x_ref[...])
    d_input, sums = norm_back(dh, normed, inv, vec_ref[0:1, :])
    dx_ref[...] = dy + d_input
    sums_ref[0] = sums


def kv_kernel(x_ref, w_ref, out_ref):
    out_ref[...] = dot(x_ref[...], w_ref[...]).astype(BF16)


def image_back_kernel(dkv_ref, w_ref, theirs_ref, mine_ref):
    half = theirs_ref.shape[1]
    both = dot_nt(dkv_ref[...], w_ref[...])
    theirs_ref[...] = both[:, :half].astype(BF16)
    mine_ref[...] = both[:, half:]


def vec_columns(sums, width):
    rows = sums.shape[0]
    full = jnp.concatenate([sums, jnp.zeros((width - rows, sums.shape[1]), F32)], axis=0)
    return full.T.astype(BF16)


def by_section(tab_ref, first, second, kernel):
    @pl.when(tab_ref[0] == 0)
    def _():
        kernel(*first)

    @pl.when(tab_ref[0] == 1)
    def _():
        kernel(*second)


def store_halves(tab_ref, mine_ref, theirs_ref, rows, cols, value):
    chips = mine_ref.shape[0]
    count = value.shape[0] // (2 * chips)
    pairs = value.reshape(chips, 2, count, value.shape[1])
    here = tab_ref[1] == 0
    mine_ref[:, rows, cols] = jnp.where(here, pairs[:, 0], pairs[:, 1]).astype(BF16)
    theirs_ref[:, rows, cols] = jnp.where(here, pairs[:, 1], pairs[:, 0]).astype(BF16)


def ffn_grads_kernel(tab_ref, io, m_ref, du_ref, g_ref, dyb_ref, *out_refs):
    d = dyb_ref.shape[1]
    blocks = du_ref.shape[1] // d
    io.need(m_ref, du_ref)
    for j, (mine_ref, theirs_ref) in enumerate(zip(out_refs[0::2], out_refs[1::2])):
        parts = len(out_refs) // 2
        cols = m_ref.shape[1] // parts
        m = m_ref[:, j * cols : (j + 1) * cols]
        up_rows = cols // (2 * mine_ref.shape[0])
        store = partial(store_halves, tab_ref, mine_ref, theirs_ref)
        for k in range(blocks):
            part = dot_tn(m, du_ref[:, k * d : (k + 1) * d]).astype(BF16)
            store(slice(k * up_rows, (k + 1) * up_rows), slice(None), part)
        if j == 0:
            io.need(g_ref, dyb_ref)
        cols = g_ref.shape[1] // parts
        down = dot_tn(g_ref[:, j * cols : (j + 1) * cols], dyb_ref[...]).astype(BF16)
        store(slice(blocks * up_rows, None), slice(None), down)
        io.flush(mine_ref, theirs_ref)


def attn_grads_kernel(tab_ref, io, h_ref, dqkv_ref, o_ref, dyb_ref, asum_ref, fsum_ref, mine_ref, theirs_ref):
    d = dyb_ref.shape[1]
    store = partial(store_halves, tab_ref, mine_ref, theirs_ref, slice(None))
    io.need(o_ref, dyb_ref, asum_ref, fsum_ref)
    store(slice(3 * d, 4 * d), dot_tn(o_ref[...], dyb_ref[...]).astype(BF16))
    sums = jnp.concatenate([jnp.sum(asum_ref[...], axis=0)[:2], jnp.sum(fsum_ref[...], axis=0)[:2]])
    store(slice(4 * d, None), vec_columns(sums, PAIR))
    io.need(h_ref, dqkv_ref)
    store(slice(0, 3 * d), dot_tn(h_ref[...], dqkv_ref[...]).astype(BF16))


def cross_grads_kernel(
    tab_ref, io, h_ref, dq_ref, o_ref, dyb_ref, sum_ref, image_ref, dkv_ref, mine_ref, theirs_ref
):
    d = dyb_ref.shape[1]
    io.need(h_ref, dq_ref, o_ref, dyb_ref, sum_ref)

    def store(cols, value):
        half = value.shape[0] // 2
        for s in range(2):
            chips = pl.ds(s * RING, RING)
            store_halves(
                tab_ref, mine_ref.at[chips], theirs_ref.at[chips], slice(None), cols, value[s * half : (s + 1) * half]
            )

    store(slice(0, d), dot_tn(h_ref[...], dq_ref[...]))
    store(slice(3 * d, 4 * d), dot_tn(o_ref[...], dyb_ref[...]))
    store(slice(4 * d, None), vec_columns(jnp.sum(sum_ref[...], axis=0)[:2], PAIR).astype(F32))
    io.need(image_ref, dkv_ref)
    store(slice(d, 3 * d), dot_tn(image_ref[...], dkv_ref[...]))


def sds(shape, dtype):
    return jax.ShapeDtypeStruct(shape, dtype)


def rows_at(base, rows, cols):
    return pl.BlockSpec((rows, cols), lambda i, tab: (i + base, 0))


def whole_spec(shape):
    return pl.BlockSpec(shape, lambda i, tab: (0,) * len(shape), pipeline_mode=pl.Buffered(1))


ANY_SPEC = pl.BlockSpec(memory_space=pl.ANY)


class Unit(NamedTuple):
    arrays: Any
    moves: Any


def begin(unit, tab_ref, refs, targets, sems):
    copies = []
    for j, (array, start, rows, cols, target, lead, place) in enumerate(unit.moves):
        source = refs[array].at[pl.ds(start, rows)]
        if cols is not None:
            source = refs[array].at[pl.ds(start, rows), pl.ds(*cols)]
        row = 0
        if place is not None:
            offset, other, by_core = place
            chip = at_offset(tab_ref, offset)
            core = 1 - tab_ref[1] if other else tab_ref[1]
            at = core * RING + chip if by_core else chip * CORES + core
            row = pl.multiple_of(at * rows, rows)
        to = targets[target]
        to = to.at[pl.ds(row, rows)] if lead is None else to.at[lead, pl.ds(row, rows)]
        copy = pltpu.make_async_copy(source, to, sems.at[j])
        copy.start()
        copies.append(copy)
    return copies


def finish(copies):
    for copy in copies:
        copy.wait()


def vector_rows(table_ref, *vec_refs):
    rows = table_ref[...].astype(F32).T
    for j, vec_ref in enumerate(vec_refs):
        vec_ref[0:2, :] = rows[2 * j : 2 * j + 2, :]


class Stage(NamedTuple):
    kernel: Any
    only: Any
    steps: int
    ins: Any
    outs: Any
    cost: Any
    units: Any = ()
    scratch: Any = ()
    carried: Any = ()
    manual: bool = False


class Transfers:
    def __init__(self, incoming, outgoing):
        self.incoming, self.outgoing, self.sent = list(incoming), list(outgoing), []
        for copy, _ in self.incoming:
            copy.start()

    def need(self, *refs):
        left = []
        for copy, ref in self.incoming:
            if any(ref is one for one in refs):
                copy.wait()
            else:
                left.append((copy, ref))
        self.incoming = left

    def flush(self, *refs):
        left = []
        for copy, ref in self.outgoing:
            if any(ref is one for one in refs):
                copy.start()
                self.sent.append(copy)
            else:
                left.append((copy, ref))
        self.outgoing = left

    def close(self):
        self.need(*[ref for _, ref in self.incoming])
        self.flush(*[ref for _, ref in self.outgoing])
        for copy in self.sent:
            copy.wait()


def window(spec):
    return tuple(pl.ds(at * size, size) for at, size in zip(spec.index_map(0, None), spec.block_shape))


def pinned(spec, stage, steps):
    index = spec.index_map

    def at(i, tab):
        if stage.steps < steps:
            i = jnp.minimum(i, stage.steps - 1)
        if stage.only is not None:
            i = jnp.where(tab[0] == stage.only, i, 0)
        return index(i, tab)

    return pl.BlockSpec(spec.block_shape, at, pipeline_mode=spec.pipeline_mode)


def taken(refs, count):
    return refs[:count], refs[count:]


def run(tab, stages, after=(), vmem_limit=VMEM_LIMIT):
    steps = max(stage.steps for stage in stages)
    ins, loaded, outs, scratch = [], [], [], []
    for stage in stages:
        if stage.manual:
            loaded += [array for array, _ in stage.ins]
            outs += [(sds(shape, dtype), ANY_SPEC) for shape, dtype, _ in stage.outs]
            scratch += [pltpu.VMEM(spec.block_shape, array.dtype) for array, spec in stage.ins]
            scratch += [pltpu.VMEM(spec.block_shape, dtype) for _, dtype, spec in stage.outs]
            scratch.append(pltpu.SemaphoreType.DMA((len(stage.ins) + len(stage.outs),)))
        else:
            ins += [(array, pinned(spec, stage, steps)) for array, spec in stage.ins]
            outs += [(sds(shape, dtype), pinned(spec, stage, steps)) for shape, dtype, spec in stage.outs]
        loaded += [array for unit in stage.units for array in unit.arrays]
        scratch += list(stage.scratch)
    carried = [buffer for stage in stages for buffer in stage.carried]
    n_skip = len(carried) + len(after)
    aliases, out_base = {}, 0
    for stage in stages:
        out_base += len(stage.outs)
        for j in range(len(stage.carried)):
            aliases[1 + len(ins) + len(loaded) + len(aliases)] = out_base - len(stage.carried) + j

    def manual_part(stage, tab_ref, in_any, unit_any, out_any, own):
        own_in, own = taken(own, len(stage.ins))
        own_out, own = taken(own, len(stage.outs))
        sems, own = own[0], own[1:]
        incoming = [
            (pltpu.make_async_copy(ref.at[window(spec)], to, sems.at[j]), to)
            for j, (ref, (_, spec), to) in enumerate(zip(in_any, stage.ins, own_in))
        ]
        outgoing = [
            (pltpu.make_async_copy(source, ref.at[window(spec)], sems.at[len(stage.ins) + j]), source)
            for j, (ref, (_, _, spec), source) in enumerate(zip(out_any, stage.outs, own_out))
        ]
        transfers = Transfers(incoming, outgoing)
        stage.kernel(tab_ref, transfers, *own_in, *unit_any, *own_out, *own)
        transfers.close()

    def body(tab_ref, *refs):
        in_refs, refs = taken(refs, len(ins))
        any_refs, refs = taken(refs, len(loaded))
        out_refs, scratch_refs = taken(refs[n_skip:], len(outs))
        for stage in stages:
            own_in, in_refs = taken(in_refs, 0 if stage.manual else len(stage.ins))
            in_any, any_refs = taken(any_refs, len(stage.ins) if stage.manual else 0)
            unit_any, any_refs = taken(any_refs, sum(len(unit.arrays) for unit in stage.units))
            own_out, out_refs = taken(out_refs, len(stage.outs))
            extra = len(stage.ins) + len(stage.outs) + 1 if stage.manual else 0
            own_scratch, scratch_refs = taken(scratch_refs, extra + len(stage.scratch))
            if stage.manual:
                part = partial(manual_part, stage, tab_ref, in_any, unit_any, own_out, own_scratch)
            else:
                part = partial(stage.kernel, tab_ref, *own_in, *unit_any, *own_out, *own_scratch)
            wanted = []
            if stage.only is not None:
                wanted.append(tab_ref[0] == stage.only)
            if stage.steps < steps:
                wanted.append(pl.program_id(0) < stage.steps)
            if wanted:
                pl.when(wanted[0] if len(wanted) == 1 else wanted[0] & wanted[1])(part)
            else:
                part()

    results = pl.pallas_call(
        body,
        grid_spec=pltpu.PrefetchScalarGridSpec(
            num_scalar_prefetch=1,
            grid=(steps,),
            in_specs=[spec for _, spec in ins] + [ANY_SPEC] * (len(loaded) + n_skip),
            out_specs=[spec for _, spec in outs],
            scratch_shapes=scratch,
        ),
        out_shape=[shape for shape, _ in outs],
        input_output_aliases=aliases,
        compiler_params=pltpu.CompilerParams(vmem_limit_bytes=vmem_limit),
        cost_estimate=pl.CostEstimate(
            flops=max(stage.cost[0] for stage in stages),
            bytes_accessed=max(stage.cost[1] for stage in stages),
            transcendentals=0,
        ),
    )(tab, *[array for array, _ in ins], *loaded, *carried, *after)
    split, start = [], 0
    for stage in stages:
        split.append(list(results[start : start + len(stage.outs)]))
        start += len(stage.outs)
    return split


def call(kernel, on, steps, ins, outs, flops, moved, trans=0, carried=(), after=(), vmem_limit=VMEM_LIMIT):
    own = kernel if on[1] is None else lambda tab_ref, *refs: kernel(*refs)
    stage = Stage(own, on[1], steps, ins, outs, (flops, moved), carried=carried)
    if len(on) > 2:
        return stage
    return run(on[0], [stage], after, vmem_limit)[0]


def sums_at(base, d):
    return pl.BlockSpec((1, 8, d), lambda i, tab: (i + base, 0, 0))


def code_at(base):
    return pl.BlockSpec((1, 1, BLOCK), lambda i, tab: (i + base, 0, 0))


def dma(unit):
    return pltpu.SemaphoreType.DMA((len(unit.moves),))


def vmem(shape, dtype=BF16):
    return pltpu.VMEM(shape, dtype)


def first_attention(base, x, code, code_row, attn, carried):
    t, d = x.shape
    n = len(attn.arrays)

    def kernel(tab_ref, io, x_ref, code_ref, code_row_ref, *refs):
        pieces, refs = taken(refs, n)
        outs, (w_ref, vec_ref, sems) = taken(refs, 5)
        finish(begin(attn, tab_ref, pieces, (w_ref,), sems))
        vector_rows(w_ref.at[:, 4 * d : 4 * d + PAIR], vec_ref)
        io.need(x_ref, code_ref, code_row_ref)
        self_fwd_kernel(x_ref, vec_ref, code_ref, code_row_ref, w_ref, *outs)

    widths = ((d, F32), (d, BF16), (3 * d, BF16), (HEADS * TILE, BF16), (d, BF16))
    return Stage(
        kernel,
        0,
        1,
        [(x, rows_at(base, BLOCK, d)), (code, rows_at(base, BLOCK, 2)), (code_row, code_at(base))],
        [((t, wide), dtype, rows_at(base, BLOCK, wide)) for wide, dtype in widths],
        (t * d * 8 * d, d * d * 8 + t * d * 24),
        (attn,),
        (vmem((d, 4 * d + PAIR)), vmem((8, d), F32), dma(attn)),
        carried,
        manual=True,
    )


def first_feed(base, x, ffn, vecs, up_shape, down_shape, carried):
    t, d = x.shape
    ff = down_shape[0]
    n = len(ffn.arrays)

    def kernel(tab_ref, io, x_ref, *refs):
        pieces, refs = taken(refs, n)
        tables, refs = taken(refs, len(vecs.arrays))
        outs, (up_ref, down_ref, table_ref, unused_ref, vec_ref, sems, vec_sems) = taken(refs, 4)
        copies = begin(ffn, tab_ref, pieces, (up_ref, down_ref), sems)
        finish(begin(vecs, tab_ref, tables, (table_ref,), vec_sems))
        vector_rows(table_ref, unused_ref, vec_ref)
        io.need(x_ref)
        finish(copies)
        ffn_fwd_kernel(x_ref, vec_ref, up_ref, down_ref, *outs)

    return Stage(
        kernel,
        0,
        1,
        [(x, rows_at(base, BLOCK, d))],
        [((BLOCK, d), BF16, rows_at(0, BLOCK, d))]
        + [((t, wide), BF16, rows_at(base, BLOCK, wide)) for wide in (d, ff, ff)],
        (BLOCK * d * 4 * ff, d * ff * 4),
        (ffn, vecs),
        (
            vmem(up_shape),
            vmem(down_shape),
            vmem((d, PAIR)),
            vmem((8, d), F32),
            vmem((8, d), F32),
            dma(ffn),
            dma(vecs),
        ),
        carried,
        manual=True,
    )


def second_layer(base, t, x, code, code_row, kv, cot, attn, cross, ffn, up_shape, down_shape, carried):
    d = x.shape[1]
    ff = down_shape[0]
    n = IMG_MB * PATCHES
    nb = t // BLOCK
    counts = [len(unit.arrays) for unit in (attn, cross, ffn)]

    def kernel(tab_ref, io, x_ref, code_ref, code_row_ref, kv_ref, cot_ref, *refs):
        attn_refs, refs = taken(refs, counts[0])
        cross_refs, refs = taken(refs, counts[1])
        ffn_refs, refs = taken(refs, counts[2])
        outs, scratch = taken(refs, 19)
        (y, dxb, h, o, m, g, dy, du, fsum, ch, co, cdy, cdq, cdkv, csum, dx0, dy1, dqkv, asum) = outs
        (wa, wc, up, down, va, vf, vc, x1, qkv, p, cq, cp, x2, slope, dx2, dx1, sa, sc, sf) = scratch
        attn_copies = begin(attn, tab_ref, attn_refs, (wa,), sa)
        cross_copies = begin(cross, tab_ref, cross_refs, (wc,), sc)
        ffn_copies = begin(ffn, tab_ref, ffn_refs, (up, down), sf)
        finish(attn_copies)
        vector_rows(wa.at[:, 4 * d : 4 * d + PAIR], va, vf)
        io.need(x_ref, code_ref, code_row_ref)
        self_fwd_kernel(x_ref, va, code_ref, code_row_ref, wa, x1, h, qkv, p, o)
        io.flush(h, o)
        io.need(kv_ref)
        finish(cross_copies)
        vector_rows(wc.at[:, 4 * d : 4 * d + PAIR], vc)
        cross_fwd_kernel(x1, vc, code_ref, kv_ref, wc, x2, ch, cq, cp, co)
        io.flush(ch, co)
        finish(ffn_copies)
        ffn_fwd_kernel(x2, vf, up, down, y, m, g, slope)
        io.flush(y, m, g)
        io.need(cot_ref)
        ffn_bwd_kernel(x2, cot_ref, None, vf, slope, up, down, dx2, dy, du, fsum)
        io.flush(dy, du, fsum)
        cross_bwd_kernel(x1, dx2, vc, code_ref, cq, cp, kv_ref, wc, dx1, cdy, cdq, cdkv, csum)
        io.flush(cdy, cdq, cdkv, csum)
        self_bwd_kernel(x_ref, dx1, va, qkv, p, wa, dxb, dx0, dy1, dqkv, asum)

    def rows(wide, dtype=BF16):
        return ((t, wide), dtype, rows_at(base, BLOCK, wide))

    sums = ((nb, 8, d), F32, sums_at(base, d))
    own = ((BLOCK, d), BF16, rows_at(0, BLOCK, d))
    return Stage(
        kernel,
        1,
        1,
        [
            (x, rows_at(0, BLOCK, d)),
            (code, rows_at(base, BLOCK, 2)),
            (code_row, code_at(base)),
            (kv, rows_at(base, n, 2 * d)),
            (cot, rows_at(base, BLOCK, d)),
        ],
        [own, own, rows(d), rows(d), rows(d), rows(ff), rows(d), rows(ff), sums]
        + [rows(d), rows(d), rows(d), rows(d), ((nb * n, 2 * d), BF16, rows_at(base, n, 2 * d)), sums]
        + [rows(d, F32), rows(d), rows(3 * d), sums],
        (BLOCK * d * 24 * d, d * d * 40),
        (attn, cross, ffn),
        (
            vmem((d, 4 * d + PAIR)),
            vmem((d, 4 * d + PAIR)),
            vmem(up_shape),
            vmem(down_shape),
            vmem((8, d), F32),
            vmem((8, d), F32),
            vmem((8, d), F32),
            vmem((BLOCK, d), F32),
            vmem((BLOCK, 3 * d)),
            vmem((BLOCK, HEADS * TILE)),
            vmem((BLOCK, d)),
            vmem((HEADS, BLOCK, PATCHES)),
            vmem((BLOCK, d), F32),
            vmem((BLOCK, ff)),
            vmem((BLOCK, d), F32),
            vmem((BLOCK, d), F32),
            dma(attn),
            dma(cross),
            dma(ffn),
        ),
        carried,
        manual=True,
    )


def first_back(base, x1, cot, more, slope, x, qkv, probs, attn, ffn, up_shape, down_shape, carried):
    t, d = x.shape
    ff = down_shape[0]
    nb = t // BLOCK
    counts = [len(unit.arrays) for unit in (attn, ffn)]

    def kernel(tab_ref, io, x1_ref, cot_ref, more_ref, slope_ref, x_ref, qkv_ref, p_ref, *refs):
        attn_refs, refs = taken(refs, counts[0])
        ffn_refs, refs = taken(refs, counts[1])
        (dy, du, fsum, dx0, dy1, dqkv, asum), scratch = taken(refs, 7)
        wa, up, down, va, vf, dx1, dxb, sa, sf = scratch
        ffn_copies = begin(ffn, tab_ref, ffn_refs, (up, down), sf)
        finish(begin(attn, tab_ref, attn_refs, (wa,), sa))
        vector_rows(wa.at[:, 4 * d : 4 * d + PAIR], va, vf)
        finish(ffn_copies)
        io.need(x1_ref, cot_ref, more_ref, slope_ref)
        ffn_bwd_kernel(x1_ref, cot_ref, more_ref, vf, slope_ref, up, down, dx1, dy, du, fsum)
        io.flush(dy, du, fsum)
        io.need(x_ref, qkv_ref, p_ref)
        self_bwd_kernel(x_ref, dx1, va, qkv_ref, p_ref, wa, dxb, dx0, dy1, dqkv, asum)

    def rows(wide, dtype=BF16):
        return ((t, wide), dtype, rows_at(base, BLOCK, wide))

    sums = ((nb, 8, d), F32, sums_at(base, d))
    here = rows_at(base, BLOCK, d)
    return Stage(
        kernel,
        0,
        1,
        [
            (x1, here),
            (cot, here),
            (more, rows_at(0, BLOCK, d)),
            (slope, rows_at(base, BLOCK, ff)),
            (x, here),
            (qkv, rows_at(base, BLOCK, 3 * d)),
            (probs, rows_at(base, BLOCK, HEADS * TILE)),
        ],
        [rows(d), rows(ff), sums, rows(d, F32), rows(d), rows(3 * d), sums],
        (BLOCK * d * 12 * d, d * d * 24),
        (attn, ffn),
        (
            vmem((d, 4 * d + PAIR)),
            vmem(up_shape),
            vmem(down_shape),
            vmem((8, d), F32),
            vmem((8, d), F32),
            vmem((BLOCK, d), F32),
            vmem((BLOCK, d)),
            dma(attn),
            dma(ffn),
        ),
        carried,
        manual=True,
    )


def first_feed_back(base, x1, cot, more, slope, ffn, vecs, up_shape, down_shape, carried):
    t, d = x1.shape
    ff = down_shape[0]
    nb = t // BLOCK

    def kernel(tab_ref, io, x1_ref, cot_ref, more_ref, slope_ref, *refs):
        pieces, refs = taken(refs, len(ffn.arrays))
        tables, refs = taken(refs, len(vecs.arrays))
        (dx1, dy, du, fsum), (up, down, table, va, vf, sf, sv) = taken(refs, 4)
        copies = begin(ffn, tab_ref, pieces, (up, down), sf)
        finish(begin(vecs, tab_ref, tables, (table,), sv))
        vector_rows(table, va, vf)
        io.need(x1_ref, cot_ref, more_ref, slope_ref)
        finish(copies)
        ffn_bwd_kernel(x1_ref, cot_ref, more_ref, vf, slope_ref, up, down, dx1, dy, du, fsum)

    here = rows_at(base, BLOCK, d)
    return Stage(
        kernel,
        0,
        1,
        [(x1, here), (cot, here), (more, rows_at(0, BLOCK, d)), (slope, rows_at(base, BLOCK, ff))],
        [
            ((BLOCK, d), F32, rows_at(0, BLOCK, d)),
            ((t, d), BF16, here),
            ((t, ff), BF16, rows_at(base, BLOCK, ff)),
            ((nb, 8, d), F32, sums_at(base, d)),
        ],
        (BLOCK * d * 4 * ff, d * d * 16),
        (ffn, vecs),
        (
            vmem(up_shape),
            vmem(down_shape),
            vmem((d, PAIR)),
            vmem((8, d), F32),
            vmem((8, d), F32),
            dma(ffn),
            dma(vecs),
        ),
        carried,
        manual=True,
    )


def first_attention_back(base, x, dx1, qkv, probs, attn, carried):
    t, d = x.shape
    nb = t // BLOCK

    def kernel(tab_ref, io, x_ref, dx1_ref, qkv_ref, p_ref, *refs):
        pieces, refs = taken(refs, len(attn.arrays))
        (dx0, dy1, dqkv, asum), (wa, va, dxb, sa) = taken(refs, 4)
        finish(begin(attn, tab_ref, pieces, (wa,), sa))
        vector_rows(wa.at[:, 4 * d : 4 * d + PAIR], va)
        io.need(x_ref, dx1_ref, qkv_ref, p_ref)
        self_bwd_kernel(x_ref, dx1_ref, va, qkv_ref, p_ref, wa, dxb, dx0, dy1, dqkv, asum)

    here = rows_at(base, BLOCK, d)
    return Stage(
        kernel,
        0,
        1,
        [
            (x, here),
            (dx1, rows_at(0, BLOCK, d)),
            (qkv, rows_at(base, BLOCK, 3 * d)),
            (probs, rows_at(base, BLOCK, HEADS * TILE)),
        ],
        [
            ((t, d), F32, here),
            ((t, d), BF16, here),
            ((t, 3 * d), BF16, rows_at(base, BLOCK, 3 * d)),
            ((nb, 8, d), F32, sums_at(base, d)),
        ],
        (BLOCK * d * 8 * d, d * d * 8),
        (attn,),
        (vmem((d, 4 * d + PAIR)), vmem((8, d), F32), vmem((BLOCK, d)), dma(attn)),
        carried,
        manual=True,
    )


def with_unit(kernel, unit, outs):
    def own(tab_ref, io, x_ref, *refs):
        pieces, refs = taken(refs, len(unit.arrays))
        out_refs, (w_ref, sems) = taken(refs, outs)
        finish(begin(unit, tab_ref, pieces, (w_ref,), sems))
        io.need(x_ref)
        for j in range(x_ref.shape[0] // PATCHES):
            rows = pl.ds(j * PATCHES, PATCHES)
            kernel(x_ref.at[rows], w_ref, *[ref.at[rows] for ref in out_refs])

    return own


def image_kv(patches, unit):
    n, d = patches.shape
    return Stage(
        with_unit(kv_kernel, unit, 1),
        1,
        1,
        [(patches, rows_at(0, n, d))],
        [((n, 2 * d), BF16, rows_at(0, n, 2 * d))],
        (n * d * d * 4, n * d * 6 + d * d * 4),
        (unit,),
        (vmem((d, 2 * d)), dma(unit)),
        manual=True,
    )


def image_back(dkv, unit):
    n, d = dkv.shape[0], dkv.shape[1] // 2
    return Stage(
        with_unit(image_back_kernel, unit, 2),
        1,
        1,
        [(dkv, rows_at(0, n, 2 * d))],
        [
            ((n, d // 2), BF16, rows_at(0, n, d // 2)),
            ((n, d // 2), F32, rows_at(0, n, d // 2)),
        ],
        (n * d * d * 4, n * d * 7 + d * d * 4),
        (unit,),
        (vmem((d, 2 * d)), dma(unit)),
        manual=True,
    )


def columns_of(section, rows, cols):
    def index(i, tab):
        return (0, i * (tab[0] if section else 1 - tab[0]))

    return pl.BlockSpec((rows, cols), index)


def sums_of(section, shape):
    def index(i, tab):
        return (0, 0, i * (tab[0] if section else 1 - tab[0]))

    return pl.BlockSpec(shape, index)


def either(kernel, sets, specs, outs, cost):
    n = len(specs)

    def own(tab_ref, io, *refs):
        first, refs = taken(refs, n)
        second, refs = taken(refs, n)
        out_refs, refs = taken(refs, len(outs))
        to, sems = refs[:n], refs[n]

        def fetched(source):
            return [pltpu.make_async_copy(ref, one, sems.at[j]) for j, (ref, one) in enumerate(zip(source, to))]

        for section, source in enumerate((first, second)):

            @pl.when(tab_ref[0] == section)
            def _(source=source):
                for copy in fetched(source):
                    copy.start()

        waiting = Transfers([], [])
        waiting.incoming = list(zip(fetched(first), to))
        waiting.outgoing = io.outgoing
        kernel(tab_ref, waiting, *to, *out_refs)
        waiting.need(*[ref for _, ref in waiting.incoming])
        io.outgoing, io.sent = waiting.outgoing, waiting.sent

    return Stage(
        own,
        None,
        1,
        [],
        outs,
        cost,
        (Unit(list(sets[0]), ()), Unit(list(sets[1]), ())),
        tuple(pltpu.VMEM(array.shape, array.dtype) for array in sets[0]) + (pltpu.SemaphoreType.DMA((n,)),),
        manual=True,
    )


def ffn_grads(tab, sets, after=()):
    t, d = sets[0][0].shape
    ff = sets[0][2].shape[1]
    shape = (RING, (ff + 4 * d) // (RING * CORES), d)
    stage = either(
        ffn_grads_kernel,
        sets,
        sets[0],
        [(shape, BF16, whole_spec(shape))] * 2,
        (t * d * ff * 4, t * (ff + d) * 4 + d * ff * 4),
    )
    return run(tab, [stage], after)[0]


def attn_grads(tab, sets, after=()):
    t, d = sets[0][0].shape
    shape = (RING, d // (RING * CORES), 4 * d + PAIR)
    stage = either(
        attn_grads_kernel,
        sets,
        sets[0],
        [(shape, BF16, whole_spec(shape))] * 2,
        (t * d * d * 8, t * d * 12 + d * d * 8),
    )
    return run(tab, [stage], after)[0]


def cross_grads(h, dq, patches, dkv, o, dyb, sums):
    t, d = h.shape
    n = patches.shape[0]
    wide = 4 * d + PAIR
    shape = (2 * RING, d // (2 * RING * CORES), wide)
    return Stage(
        cross_grads_kernel,
        1,
        1,
        [
            (h, rows_at(0, t, d)),
            (dq, rows_at(0, t, d)),
            (o, rows_at(0, t, d)),
            (dyb, rows_at(0, t, d)),
            (sums, whole_spec(sums.shape)),
            (patches, rows_at(0, n, d)),
            (dkv, rows_at(0, n, 2 * d)),
        ],
        [(shape, BF16, whole_spec(shape))] * 2,
        (t * d * d * 4 + n * d * d * 4, t * d * 8 + n * d * 6 + d * d * 8),
        manual=True,
    )


def at_offset(tab, offset):
    return tab[2 + RING // 2 + offset]


def join_kernel(tab_ref, *refs, extra, moving, cuts):
    mine_ref, theirs_ref = refs[:2]
    moving_refs, out_refs = taken(refs[2 + extra :], moving)
    rows = mine_ref.shape[1]
    parts = [(0, mine_ref[0].astype(F32) + theirs_ref[0].astype(F32))]
    if extra:
        parts.append((rows, jnp.where(tab_ref[0] == 0, refs[2][0], refs[3][0]).astype(F32)))
    for start, value in parts:
        for ref in moving_refs:
            value = value + ref[start : start + value.shape[0], :].astype(F32)
        for out, row, at, first, count, column, columns in cuts:
            if start <= first < start + value.shape[0]:
                piece = value[first - start : first - start + count, column : column + columns]
                out_refs[out][row : row + count, at : at + columns] = piece.astype(out_refs[out].dtype)


def join(tab, offset, mine, theirs, extra, moving, dtype, after=(), cuts=None):
    cols = mine.shape[2]
    rows = mine.shape[1] + (extra[0].shape[1] if extra else 0)

    def part(array):
        return (array, pl.BlockSpec((1,) + array.shape[1:], lambda i, tab: (at_offset(tab, offset), 0, 0)))

    if cuts is None:
        cuts = [(0, 0, 0, 0, mine.shape[1], 0, cols)]
        if extra:
            cuts.append((0, mine.shape[1], 0, mine.shape[1], extra[0].shape[1], 0, cols))
    shapes = {}
    for out, row, at, _, count, _, columns in cuts:
        have = shapes.get(out, (0, 0))
        shapes[out] = (max(row + count, have[0]), max(at + columns, have[1]))
    shapes = [shapes[out] for out in range(len(shapes))]
    results = call(
        partial(join_kernel, extra=len(extra), moving=len(moving), cuts=cuts),
        (tab, None),
        1,
        [part(array) for array in (mine, theirs) + tuple(extra)]
        + [(array, pl.BlockSpec((rows, cols), lambda i, tab: (0, 0))) for array in moving],
        [(shape, dtype, pl.BlockSpec(shape, lambda i, tab: (0, 0))) for shape in shapes],
        rows * cols * 3,
        rows * cols * 2 * (3 + len(moving)),
        after=after,
        vmem_limit=SMALL_LIMIT,
    )
    return results[0] if len(shapes) == 1 else results


def cross_join_kernel(tab_ref, io, mine_ref, theirs_ref, first_ref, second_ref):
    io.need(mine_ref, theirs_ref)
    first_ref[...] = (mine_ref[:RING].astype(F32) + theirs_ref[:RING].astype(F32)).astype(BF16)
    io.flush(first_ref)
    second_ref[...] = (mine_ref[RING:].astype(F32) + theirs_ref[RING:].astype(F32)).astype(BF16)


def cross_join(mine, theirs):
    shape = (RING,) + mine.shape[1:]
    return Stage(
        cross_join_kernel,
        1,
        1,
        [(mine, whole_spec(mine.shape)), (theirs, whole_spec(theirs.shape))],
        [(shape, BF16, whole_spec(shape))] * 2,
        (mine.size, mine.size * 6),
        manual=True,
    )


def widen_kernel(tab_ref, io, x_ref, out_ref):
    io.need(x_ref)
    out_ref[...] = x_ref[...].astype(F32)


def widen(x, buffer):
    block = whole_spec(x.shape)
    return Stage(
        widen_kernel, 0, 1, [(x, block)], [(x.shape, F32, block)], (0, x.size * 6), carried=(buffer,), manual=True
    )


def relay_kernel(tab_ref, x_ref, out_ref):
    out_ref[...] = x_ref[...]


def relay(x):
    spec = pl.BlockSpec(x.shape, lambda i, tab: (0, 0))
    return Stage(relay_kernel, 1, 1, [(x, spec)], [(x.shape, x.dtype, spec)], (0, x.size * 4))


def pack_kernel(tab_ref, *refs):
    pieces, out_ref = refs[:-1], refs[-1]
    rows = pieces[0].shape[0]
    for j, ref in enumerate(pieces):
        out_ref[j * rows : (j + 1) * rows, :] = ref[...]


def pack(pieces):
    rows, cols = pieces[0].shape
    shape = (len(pieces) * rows, cols)
    return Stage(
        pack_kernel,
        1,
        1,
        [(piece, pl.BlockSpec((rows, cols), lambda i, tab: (0, 0))) for piece in pieces],
        [(shape, BF16, pl.BlockSpec(shape, lambda i, tab: (0, 0)))],
        (0, rows * cols * len(pieces) * 4),
    )


def ring_tables():
    half = RING // 2
    return [2 * z for z in range(half)] + [2 * z + 1 for z in range(half - 1, -1, -1)]


CHIP_AT = ring_tables()


def flat(section, chip, core):
    return section * RING * CORES + chip * CORES + core


def ring_pairs(sections, step):
    return [
        (flat(s, CHIP_AT[i], c), flat(s, CHIP_AT[(i + step) % RING], c))
        for s in sections
        for i in range(RING)
        for c in range(CORES)
    ]


def core_pairs(sections):
    return [
        (flat(s, chip, c), flat(s, chip, 1 - c))
        for s in sections
        for chip in range(RING)
        for c in range(CORES)
    ]


def send(x, pairs):
    return lax.ppermute(x, ("section", "dp"), pairs)


def device_table():
    rank = lax.axis_index("dp")
    chip = rank // CORES % RING
    half = RING // 2
    pos = jnp.where(chip % 2 == 0, chip // 2, RING - 1 - chip // 2)
    slot = lax.iota(jnp.int32, RING + 3)
    at = (pos + slot - 2 - half + RING) % RING
    chips = jnp.where(at < half, 2 * at, 2 * (RING - 1 - at) + 1)
    return jnp.where(slot == 0, lax.axis_index("section"), jnp.where(slot == 1, rank % CORES, chips)).astype(jnp.int32)


class Gather:
    def __init__(self, chunk, sections, long_way, by_core):
        self.chunk, self.sections, self.long_way, self.by_core = chunk, sections, long_way, by_core
        self.arrived = {1: [], -1: []}

    def step(self):
        done = len(self.arrived[self.long_way])
        ways = [way for way in (1, -1) if done < RING // 2 - 1 or way == self.long_way]
        held = {way: self.arrived[way][-1] if done else self.chunk for way in ways}
        for way in ways:
            self.arrived[way].append(send(held[way], ring_pairs(self.sections, way)))

    def last_step(self, held):
        self.arrived[self.long_way].append(send(held, ring_pairs(self.sections, self.long_way)))

    def own_pieces(self):
        held = [(0, self.chunk)]
        for step in range(1, RING // 2 + 1):
            held += [
                (-way * step, self.arrived[way][step - 1]) for way in (1, -1) if step <= len(self.arrived[way])
            ]
        return held

    def pieces(self):
        pieces, places = [], []
        for offset, piece in self.own_pieces():
            pieces += [piece, send(piece, core_pairs(self.sections))]
            places += [(offset, False, self.by_core), (offset, True, self.by_core)]
        return pieces, tuple(places)


class Order:
    def __init__(self):
        self.last = ()

    def mark(self, *outputs):
        self.last = outputs
        return outputs[0]


class Scatter:
    def __init__(self, tab, order, mine, out, sections, long_way, extra=()):
        self.tab, self.order, self.mine = tab, order, mine
        self.sections, self.long_way, self.extra = sections, long_way, extra
        self.theirs = send(out, core_pairs(sections))
        self.moving = {1: [], -1: []}
        self.done = 0

    def step(self):
        for way in (1, -1):
            hops = RING // 2 if way == self.long_way else RING // 2 - 1
            if self.done < hops:
                piece = join(
                    self.tab,
                    way * (hops - self.done),
                    self.mine,
                    self.theirs,
                    self.extra,
                    self.moving[way],
                    BF16,
                    self.order.last,
                )
                self.order.mark(piece)
                self.moving[way] = [send(piece, ring_pairs(self.sections, way))]
        self.done += 1

    def finish(self, cuts):
        moving = self.moving[1] + self.moving[-1]
        results = join(self.tab, 0, self.mine, self.theirs, self.extra, moving, F32, self.order.last, cuts)
        self.order.mark(results[0])
        return results


def lanes_of(vectors, width):
    table = jnp.stack(vectors, axis=1)
    return jnp.pad(table, ((0, 0), (0, width - table.shape[1])))


def local(
    tokens,
    images,
    segments,
    image_ids,
    cotangent,
    norm_gain,
    norm_bias,
    qkv_weight,
    out_weight,
    up_weight,
    down_weight,
    cross_gain,
    cross_bias,
    cross_query,
    cross_kv,
    cross_out,
):
    section = lax.axis_index("section")
    multimodal = section == 1
    tab = device_table()
    t, d = tokens.shape
    ff = up_weight.shape[2]
    nb = t // BLOCK
    members = lax.axis_size("dp")
    ringed = members == RING * CORES and lax.axis_size("section") == 2
    up_rows, down_rows = up_weight.shape[1], down_weight.shape[1]
    split = ff // d

    attn_piece = jnp.concatenate(
        [
            qkv_weight[0],
            out_weight[0],
            lanes_of([norm_gain[0, 0], norm_bias[0, 0], norm_gain[0, 1], norm_bias[0, 1]], PAIR),
        ],
        axis=1,
    ).astype(BF16)
    ffn_piece = jnp.concatenate(
        [up_weight[0, :, j * d : (j + 1) * d] for j in range(split)] + [down_weight[0]], axis=0
    ).astype(BF16)
    cross_piece = jnp.concatenate(
        [cross_query, cross_kv, cross_out, lanes_of([cross_gain, cross_bias], PAIR)], axis=1
    ).astype(BF16)

    row_in_tile = lax.broadcasted_iota(jnp.int32, segments.shape, 0) % (TILE // ROW_LEN)
    code = row_in_tile * (SEGS + 1) + segments
    code_row = code.reshape(nb, 1, BLOCK)
    slots = lax.broadcasted_iota(jnp.int32, (1, 1, SEGS), 2)
    token_image = jnp.sum(
        jnp.where(segments[:, :, None] == slots, image_ids[:, None, :], 0), axis=-1
    )
    codes = jnp.stack([code, token_image], axis=-1).reshape(-1, 2)
    patches = images.reshape(-1, d)

    up_shape, down_shape = (split, d, d), (ff, d)
    cot = cotangent[0]
    order = Order()
    if ringed:
        both, s1 = (0, 1), (1,)
        attn_ring = Gather(attn_piece, both, 1, False)
        ffn_ring = Gather(ffn_piece, both, -1, False)
        for _ in range(RING // 2):
            attn_ring.step()
            ffn_ring.step()
        w_cross = lax.all_gather(cross_piece, ("section", "dp"), axis=0, tiled=True)

        def unit_of(ring, layout):
            pieces, places = ring.pieces()
            moves = [
                (j, start, rows, cols, target, lead, place)
                for j, place in enumerate(places)
                for start, rows, cols, target, lead in layout
            ]
            return Unit(pieces, moves)

        def columns_of_unit(unit, cols):
            return Unit(unit.arrays, [move[:3] + (cols,) + move[4:] for move in unit.moves])

        attn = unit_of(attn_ring, [(0, up_rows, None, 0, None)])
        ffn = unit_of(
            ffn_ring,
            [(j * up_rows, up_rows, None, 0, j) for j in range(split)]
            + [(split * up_rows, down_rows, None, 1, None)],
        )
        cross = Unit([w_cross], [(0, 0, d, None, 0, None, None)])
    else:
        w_attn = lax.all_gather(attn_piece, "dp", axis=0, tiled=True)
        w_ffn = lax.all_gather(ffn_piece, "dp", axis=0, tiled=False)
        w_up = w_ffn[:, : split * up_rows].reshape(members, split, up_rows, d).swapaxes(0, 1).reshape(up_shape)
        w_down = w_ffn[:, split * up_rows :].reshape(down_shape)
        w_cross = lax.all_gather(cross_piece, ("section", "dp"), axis=0, tiled=True)

        def columns_of_unit(unit, cols):
            return Unit(unit.arrays, [move[:3] + (cols,) + move[4:] for move in unit.moves])

        attn = Unit([w_attn], [(0, 0, d, None, 0, None, None)])
        cross = Unit([w_cross], [(0, 0, d, None, 0, None, None)])
        ffn = Unit(
            [w_up.reshape(split * d, d), w_down],
            [(0, j * d, d, None, 0, j, None) for j in range(split)] + [(1, 0, ff, None, 1, None, None)],
        )
    vecs = columns_of_unit(attn, (4 * d, PAIR))
    kv_unit = columns_of_unit(cross, (d, 2 * d))
    a_y, kept, held = [], (), ()
    for b in range(nb):
        (held,) = run(tab, [first_attention(b, tokens, codes, code_row, attn, held)], a_y)
        a_x1 = held[0]
        stages = [first_feed(b, a_x1, ffn, vecs, up_shape, down_shape, kept)]
        if b == nb - 1:
            stages.append(image_kv(patches, kv_unit))
        (y, *kept), *more = run(tab, stages, a_y)
        a_y.append(y)
    a_x1, a_h, a_qkv, a_p, a_o = held
    a_m, a_g, a_slope = kept
    ((kv,),) = more
    arrived = [lax.ppermute(y, "section", [(0, 1)]) for y in a_y]

    b_y, leaving, kept = [], [], ()
    for b in range(nb):
        ((y, low, *kept),) = run(
            tab,
            [
                second_layer(
                    b, t, arrived[b], codes, code_row, kv, cot, attn, cross, ffn, up_shape, down_shape, kept
                )
            ],
        )
        b_y.append(y)
        leaving.append(low)
    (b_h, b_o, b_m, b_g, b_dy, b_du, b_fsum, c_h, c_o, c_dy, c_dq, c_dkv, c_sum) = kept[:13]
    b_dx0, b_dy1, b_dqkv, b_asum = kept[13:]
    returning = [lax.ppermute(low, "section", [(1, 0)]) for low in leaving]

    def layer_zero_back(b, kept):
        return first_back(
            b, a_x1, cot, returning[b], a_slope, tokens, a_qkv, a_p, attn, ffn, up_shape, down_shape, kept
        )

    def cross_terms():
        return jnp.concatenate(
            [dot_tn(c_h, c_dq), dot_tn(patches, c_dkv), dot_tn(c_o, c_dy), columns(c_sum)], axis=1
        )

    def columns(*sums):
        table = jnp.concatenate([jnp.sum(part, axis=0)[:2] for part in sums]).T
        return jnp.pad(table, ((0, 0), (0, PAIR - table.shape[1])))

    if ringed:
        (kept,) = run(tab, [layer_zero_back(0, ())], leaving)
        feed_kept, attn_kept = kept[:3], kept[3:]
        (a_dx1, a_dy, a_du, a_fsum), (c_mine, c_out) = run(
            tab,
            [
                first_feed_back(1, a_x1, cot, returning[1], a_slope, ffn, vecs, up_shape, down_shape, feed_kept),
                cross_grads(c_h, c_dq, patches, c_dkv, c_o, c_dy, c_sum),
            ],
        )
        order.mark(c_mine)
        c_theirs = send(c_out, core_pairs(s1))
        ffn_mine, ffn_out = ffn_grads(
            tab, ((a_m, a_du, a_g, a_dy), (b_m, b_du, b_g, b_dy)), order.last
        )
        order.mark(ffn_mine)
        ffn_sum = Scatter(tab, order, ffn_mine, ffn_out, both, 1)
        ((c_first, c_second),) = run(tab, [cross_join(c_mine, c_theirs)], order.last)
        order.mark(c_first)
        c_first = lax.ppermute(c_first, "section", [(1, 0)])
        ((a_dx0, a_dy1, a_dqkv, a_asum),) = run(
            tab, [first_attention_back(1, tokens, a_dx1, a_qkv, a_p, attn, attn_kept)], order.last
        )
        order.mark(a_asum)
        attn_mine, attn_out = attn_grads(
            tab,
            (
                (a_h, a_dqkv, a_o, a_dy1, a_asum, a_fsum),
                (b_h, b_dqkv, b_o, b_dy1, b_asum, b_fsum),
            ),
            order.last,
        )
        order.mark(attn_mine)
        ffn_sum.step()
        ((image_theirs, image_mine),) = run(tab, [image_back(c_dkv, kv_unit)], order.last)
        order.mark(image_theirs)
        image_theirs = lax.ppermute(image_theirs, "section", [(1, 0)])
        attn_sum = Scatter(tab, order, attn_mine, attn_out, both, -1, (c_first, c_second))
        while ffn_sum.done < RING // 2:
            ffn_sum.step()
            attn_sum.step()
        ((image_shard,),) = run(tab, [widen(image_theirs, image_mine)], order.last)
        order.mark(image_shard)
        up_g, down_g = ffn_sum.finish(
            [(0, 0, j * d, j * up_rows, up_rows, 0, d) for j in range(split)]
            + [(1, 0, 0, split * up_rows, down_rows, 0, d)]
        )
        attn_sum.step()
        below, few = up_rows, up_rows // 2
        qkv_g, out_g, vec_g, query_g, kv_g, cross_out_g, cross_vec_g = attn_sum.finish(
            [
                (0, 0, 0, 0, up_rows, 0, 3 * d),
                (1, 0, 0, 0, up_rows, 3 * d, d),
                (2, 0, 0, 0, up_rows, 4 * d, PAIR),
                (3, 0, 0, below, few, 0, d),
                (4, 0, 0, below, few, d, 2 * d),
                (5, 0, 0, below, few, 3 * d, d),
                (6, 0, 0, below, few, 4 * d, PAIR),
            ]
        )
    else:

        def summed(first, second):
            grads = jnp.where(multimodal, second, first)
            return lax.psum_scatter(grads, "dp", scatter_dimension=0, tiled=True)

        def ffn_terms(m, du, g, dyb):
            up = dot_tn(m, du).reshape(members, up_rows, split, d).swapaxes(1, 2)
            down = dot_tn(g, dyb).reshape(members, down_rows, d)
            return jnp.concatenate([up.reshape(members, split * up_rows, d), down], axis=1)

        def attn_terms(h, dqkv, o, dyb, asum, fsum):
            return jnp.concatenate([dot_tn(h, dqkv), dot_tn(o, dyb), columns(asum, fsum)], axis=1)

        kept = ()
        for b in range(nb):
            (kept,) = run(tab, [layer_zero_back(b, kept)])
        a_dy, a_du, a_fsum, a_dx0, a_dy1, a_dqkv, a_asum = kept
        ((image_theirs, image_mine),) = run(tab, [image_back(c_dkv, kv_unit)])
        image_theirs = lax.ppermute(image_theirs, "section", [(1, 0)])
        image_shard = jnp.where(multimodal, image_mine, image_theirs.astype(F32))
        ffn_g = summed(ffn_terms(a_m, a_du, a_g, a_dy), ffn_terms(b_m, b_du, b_g, b_dy))[0]
        attn_g = summed(
            attn_terms(a_h, a_dqkv, a_o, a_dy1, a_asum, a_fsum),
            attn_terms(b_h, b_dqkv, b_o, b_dy1, b_asum, b_fsum),
        )
        cross_g = lax.psum_scatter(
            jnp.where(multimodal, cross_terms(), 0.0),
            ("section", "dp"),
            scatter_dimension=0,
            tiled=True,
        )
        qkv_g, out_g, vec_g = attn_g[:, : 3 * d], attn_g[:, 3 * d : 4 * d], attn_g[:, 4 * d :]
        query_g, kv_g, cross_out_g = cross_g[:, :d], cross_g[:, d : 3 * d], cross_g[:, 3 * d : 4 * d]
        cross_vec_g = cross_g[:, 4 * d :]
        up_g = jnp.concatenate([ffn_g[j * up_rows : (j + 1) * up_rows] for j in range(split)], axis=1)
        down_g = ffn_g[split * up_rows :]

    return (
        jnp.where(multimodal, jnp.concatenate(b_y), jnp.concatenate(a_y))[None],
        jnp.where(multimodal, b_dx0, a_dx0)[None],
        image_shard.reshape(images.shape[0], images.shape[1], d // 2),
        vec_g[:, 0:4:2].T[None],
        vec_g[:, 1:4:2].T[None],
        qkv_g[None],
        out_g[None],
        up_g[None],
        down_g[None],
        cross_vec_g[:, 0],
        cross_vec_g[:, 1],
        query_g,
        kv_g,
        cross_out_g,
    )


def solution(mesh):
    in_specs = (
        P("dp", None),
        P("dp", None, None),
        P("dp", None),
        P("dp", None),
        P("section", "dp", None),
        P("section", None, "dp"),
        P("section", None, "dp"),
        P("section", "dp", None),
        P("section", "dp", None),
        P("section", "dp", None),
        P("section", "dp", None),
        P(("section", "dp")),
        P(("section", "dp")),
        P(("section", "dp"), None),
        P(("section", "dp"), None),
        P(("section", "dp"), None),
    )
    out_specs = (
        P("section", "dp", None),
        P("section", "dp", None),
        P("dp", None, "section"),
        P("section", None, "dp"),
        P("section", None, "dp"),
        P("section", "dp", None),
        P("section", "dp", None),
        P("section", "dp", None),
        P("section", "dp", None),
        P(("section", "dp")),
        P(("section", "dp")),
        P(("section", "dp"), None),
        P(("section", "dp"), None),
        P(("section", "dp"), None),
    )
    return jax.shard_map(local, mesh=mesh, in_specs=in_specs, out_specs=out_specs, check_vma=False)
```

```python
from functools import partial
from typing import Any, NamedTuple

import jax
import jax.numpy as jnp
import numpy as np
from jax import lax
from jax.experimental import pallas as pl
from jax.experimental.pallas import tpu as pltpu
from jax.sharding import PartitionSpec as P

HEADS = 12
HEAD_DIM = 64
PATCHES = 576
ROW_LEN = 64
SEGS = 3
IMG_MB = 2
ROWS_MB = 4
CORES = 2
RING = 8
BLOCK = ROWS_MB * ROW_LEN
PAIR = 2 * HEAD_DIM
PAIRS = HEADS // 2
TILE = 2 * ROW_LEN
MASKED_SCORE = -1000000000.0
NORM_EPS = 1e-05
SCALE = HEAD_DIM ** (-0.5)
VMEM_LIMIT = 56 * 1024 * 1024
SMALL_LIMIT = 12 * 1024 * 1024

F32 = jnp.float32
BF16 = jnp.bfloat16


def dot(a, b):
    return lax.dot_general(a, b, (((1,), (0,)), ((), ())), preferred_element_type=F32)


def dot_nt(a, b):
    return lax.dot_general(a, b, (((1,), (1,)), ((), ())), preferred_element_type=F32)


def dot_tn(a, b):
    return lax.dot_general(a, b, (((0,), (0,)), ((), ())), preferred_element_type=F32)


def norm_parts(x):
    mean = jnp.mean(x, axis=-1, keepdims=True)
    centred = x - mean
    inv = lax.rsqrt(jnp.mean(centred * centred, axis=-1, keepdims=True) + NORM_EPS)
    return centred * inv, inv


def norm_back(d_out, normed, inv, gain):
    d_normed = d_out * gain
    d_input = inv * (
        d_normed
        - jnp.mean(d_normed, axis=-1, keepdims=True)
        - normed * jnp.mean(d_normed * normed, axis=-1, keepdims=True)
    )
    sums = jnp.concatenate(
        [
            jnp.sum(d_out * normed, axis=0, keepdims=True),
            jnp.sum(d_out, axis=0, keepdims=True),
            jnp.zeros((6, d_out.shape[1]), F32),
        ],
        axis=0,
    )
    return d_input, sums


def lane_masks(dtype):
    lane = lax.broadcasted_iota(jnp.int32, (1, PAIR), 1)
    even = (lane < HEAD_DIM).astype(F32)
    return even.astype(dtype), (1.0 - even).astype(dtype)


def softmax(scores):
    top = jnp.max(scores, axis=-1, keepdims=True)
    e = jnp.exp(scores - top)
    return (e * (1.0 / jnp.sum(e, axis=-1, keepdims=True))).astype(BF16)


def stack_heads(part, even, odd):
    return jnp.concatenate([part * even, part * odd], axis=0)


def self_fwd_kernel(x_ref, vec_ref, code_ref, code_row_ref, w_ref, x1_ref, h_ref, qkv_ref, p_ref, o_ref):
    d = x_ref.shape[1]
    x = x_ref[...].astype(F32)
    normed, _ = norm_parts(x)
    h = (normed * vec_ref[0:1, :] + vec_ref[1:2, :]).astype(BF16)
    h_ref[...] = h
    qkv_ref[...] = dot(h, w_ref[:, : 3 * d]).astype(BF16)
    even, odd = lane_masks(BF16)
    for t in range(BLOCK // TILE):
        rows = slice(t * TILE, (t + 1) * TILE)
        causal = lax.broadcasted_iota(jnp.int32, (TILE, TILE), 1) <= lax.broadcasted_iota(
            jnp.int32, (TILE, TILE), 0
        )
        allowed = (code_ref[rows, 0:1] == code_row_ref[0, :, rows]) & causal
        for p in range(PAIRS):
            lanes = slice(p * PAIR, (p + 1) * PAIR)
            q = qkv_ref[rows, lanes] * jnp.asarray(SCALE, BF16)
            k2 = stack_heads(qkv_ref[rows, d + p * PAIR : d + (p + 1) * PAIR], even, odd)
            v2 = stack_heads(qkv_ref[rows, 2 * d + p * PAIR : 2 * d + (p + 1) * PAIR], even, odd)
            s = dot_nt(q, k2)
            probs = jnp.concatenate(
                [
                    softmax(jnp.where(allowed, s[:, :TILE], MASKED_SCORE)),
                    softmax(jnp.where(allowed, s[:, TILE:], MASKED_SCORE)),
                ],
                axis=1,
            )
            p_ref[rows, 2 * p * TILE : 2 * (p + 1) * TILE] = probs
            o_ref[rows, lanes] = dot(probs, v2).astype(BF16)
    x1_ref[...] = x + dot(o_ref[...], w_ref[:, 3 * d : 4 * d])


def self_bwd_kernel(x_ref, dy_ref, vec_ref, qkv_ref, p_ref, w_ref, dxb_ref, dx_ref, dyb_ref, dqkv_ref, sums_ref):
    d = x_ref.shape[1]
    dy = dy_ref[...]
    dyb = dy.astype(BF16)
    dyb_ref[...] = dyb
    d_mixed = dot_nt(dyb, w_ref[:, 3 * d : 4 * d]).astype(BF16)
    even, odd = lane_masks(BF16)
    for t in range(BLOCK // TILE):
        rows = slice(t * TILE, (t + 1) * TILE)
        for p in range(PAIRS):
            lanes = slice(p * PAIR, (p + 1) * PAIR)
            q2 = stack_heads(qkv_ref[rows, lanes] * jnp.asarray(SCALE, BF16), even, odd)
            k2 = stack_heads(qkv_ref[rows, d + p * PAIR : d + (p + 1) * PAIR], even, odd)
            v2 = stack_heads(qkv_ref[rows, 2 * d + p * PAIR : 2 * d + (p + 1) * PAIR], even, odd)
            do = d_mixed[rows, lanes]
            do2 = stack_heads(do, even, odd)
            dp = dot_nt(do, v2)
            probs_e = p_ref[rows, 2 * p * TILE : (2 * p + 1) * TILE]
            probs_o = p_ref[rows, (2 * p + 1) * TILE : (2 * p + 2) * TILE]
            ds = []
            for probs, part in ((probs_e, dp[:, :TILE]), (probs_o, dp[:, TILE:])):
                pf = probs.astype(F32)
                term = pf * part
                ds.append((term - pf * jnp.sum(term, axis=-1, keepdims=True)).astype(BF16))
            dq = dot(jnp.concatenate(ds, axis=1), k2) * SCALE
            dk = dot_tn(jnp.concatenate(ds, axis=0), q2)
            dv = dot_tn(jnp.concatenate([probs_e, probs_o], axis=0), do2)
            dqkv_ref[rows, lanes] = dq.astype(BF16)
            dqkv_ref[rows, d + p * PAIR : d + (p + 1) * PAIR] = dk.astype(BF16)
            dqkv_ref[rows, 2 * d + p * PAIR : 2 * d + (p + 1) * PAIR] = dv.astype(BF16)
    dh = dot_nt(dqkv_ref[...], w_ref[:, : 3 * d])
    normed, inv = norm_parts(x_ref[...].astype(F32))
    d_input, sums = norm_back(dh, normed, inv, vec_ref[0:1, :])
    dx = dy + d_input
    dx_ref[...] = dx
    dxb_ref[...] = dx.astype(BF16)
    sums_ref[0] = sums


def gelu_parts(u):
    phi = 0.5 + 0.5 * lax.erf(u * (0.5**0.5))
    slope = phi + u * (jnp.exp(-0.5 * (u * u)) * ((2.0 * np.pi) ** -0.5))
    return u * phi, slope


def ffn_fwd_kernel(x_ref, vec_ref, up_ref, down_ref, y_ref, m_ref, g_ref, slope_ref, ready=None):
    d = x_ref.shape[1]
    x = x_ref[...]
    normed, _ = norm_parts(x)
    m = (normed * vec_ref[0:1, :] + vec_ref[1:2, :]).astype(BF16)
    m_ref[...] = m
    acc = x
    for j in range(up_ref.shape[0]):
        cols = slice(j * d, (j + 1) * d)
        if ready is not None:
            ready(j)
        g, slope = gelu_parts(dot(m, up_ref[j]))
        g = g.astype(BF16)
        g_ref[:, cols] = g
        slope_ref[:, cols] = slope.astype(BF16)
        if ready is None:
            acc = acc + dot(g, down_ref[cols, :])
    if ready is not None:
        ready(up_ref.shape[0])
        acc = acc + dot(g_ref[...], down_ref[...])
    y_ref[...] = acc.astype(y_ref.dtype)


def ffn_bwd_kernel(x_ref, dy_ref, more_ref, vec_ref, slope_ref, up_ref, down_ref, dx_ref, dyb_ref, du_ref, sums_ref, ready=None):
    d = x_ref.shape[1]
    dy = dy_ref[...].astype(F32)
    if more_ref is not None:
        dy = dy + more_ref[...].astype(F32)
    dyb = dy.astype(BF16)
    dyb_ref[...] = dyb
    acc = None
    for j in range(up_ref.shape[0]):
        cols = slice(j * d, (j + 1) * d)
        du = (dot_nt(dyb, down_ref[cols, :]) * slope_ref[:, cols].astype(F32)).astype(BF16)
        du_ref[:, cols] = du
        if ready is not None:
            ready(j)
        part = dot_nt(du, up_ref[j])
        acc = part if acc is None else acc + part
    normed, inv = norm_parts(x_ref[...])
    d_input, sums = norm_back(acc, normed, inv, vec_ref[0:1, :])
    dx_ref[...] = dy + d_input
    sums_ref[0] = sums


def tied(part, first, second):
    return jnp.concatenate([part * first, part * second], axis=1)


def cross_fwd_kernel(x_ref, vec_ref, image_ref, kv_ref, w_ref, x2_ref, h_ref, q_ref, p_ref, o_ref):
    d = x_ref.shape[1]
    n = PATCHES
    x = x_ref[...]
    normed, _ = norm_parts(x)
    h = (normed * vec_ref[0:1, :] + vec_ref[1:2, :]).astype(BF16)
    h_ref[...] = h
    q_ref[...] = dot(h, w_ref[:, :d]).astype(BF16)
    even, odd = lane_masks(BF16)
    image = image_ref[:, 1:2].astype(F32)
    second = image.astype(BF16)
    first = (1.0 - image).astype(BF16)
    lane_even = lax.broadcasted_iota(jnp.int32, (BLOCK, PAIR), 1) < HEAD_DIM
    is_first = jnp.broadcast_to(image, (BLOCK, PAIR)) < 0.5
    for p in range(PAIRS):
        lanes = slice(p * PAIR, (p + 1) * PAIR)
        vlanes = slice(d + p * PAIR, d + (p + 1) * PAIR)
        k2 = jnp.concatenate([kv_ref[:n, lanes], kv_ref[n:, lanes]], axis=1)
        v2 = jnp.concatenate([kv_ref[:n, vlanes], kv_ref[n:, vlanes]], axis=1)
        q = q_ref[:, lanes] * jnp.asarray(SCALE, BF16)
        out = []
        for half, mask in enumerate((even, odd)):
            probs = softmax(dot_nt(tied(q * mask, first, second), k2))
            p_ref[2 * p + half] = probs
            both = dot(probs, v2)
            out.append(jnp.where(is_first, both[:, :PAIR], both[:, PAIR:]))
        o_ref[:, lanes] = jnp.where(lane_even, out[0], out[1]).astype(BF16)
    x2_ref[...] = x + dot(o_ref[...], w_ref[:, 3 * d : 4 * d])


def cross_bwd_kernel(
    x_ref, dy_ref, vec_ref, image_ref, q_ref, p_ref, kv_ref, w_ref, dx_ref, dyb_ref, dq_ref, dkv_ref, sums_ref
):
    d = x_ref.shape[1]
    n = PATCHES
    dy = dy_ref[...]
    dyb = dy.astype(BF16)
    dyb_ref[...] = dyb
    d_mixed = dot_nt(dyb, w_ref[:, 3 * d : 4 * d]).astype(BF16)
    even, odd = lane_masks(BF16)
    image = image_ref[:, 1:2].astype(F32)
    second = image.astype(BF16)
    first = (1.0 - image).astype(BF16)
    lane_even = lax.broadcasted_iota(jnp.int32, (BLOCK, PAIR), 1) < HEAD_DIM
    is_first = jnp.broadcast_to(image, (BLOCK, PAIR)) < 0.5
    for p in range(PAIRS):
        lanes = slice(p * PAIR, (p + 1) * PAIR)
        vlanes = slice(d + p * PAIR, d + (p + 1) * PAIR)
        k2 = jnp.concatenate([kv_ref[:n, lanes], kv_ref[n:, lanes]], axis=1)
        v2 = jnp.concatenate([kv_ref[:n, vlanes], kv_ref[n:, vlanes]], axis=1)
        q = q_ref[:, lanes] * jnp.asarray(SCALE, BF16)
        do = d_mixed[:, lanes]
        ds, qq, dd, dq = [], [], [], []
        for half, mask in enumerate((even, odd)):
            qq.append(tied(q * mask, first, second))
            dd.append(tied(do * mask, first, second))
            dp = dot_nt(dd[half], v2)
            pf = p_ref[2 * p + half].astype(F32)
            term = pf * dp
            ds.append((term - pf * jnp.sum(term, axis=-1, keepdims=True)).astype(BF16))
            both = dot(ds[half], k2)
            dq.append(jnp.where(is_first, both[:, :PAIR], both[:, PAIR:]))
        dq_ref[:, lanes] = (jnp.where(lane_even, dq[0], dq[1]) * SCALE).astype(BF16)
        dk = dot_tn(jnp.concatenate(ds, axis=0), jnp.concatenate(qq, axis=0)).astype(BF16)
        dv = dot_tn(
            jnp.concatenate([p_ref[2 * p], p_ref[2 * p + 1]], axis=0), jnp.concatenate(dd, axis=0)
        ).astype(BF16)
        dkv_ref[:n, lanes] = dk[:, :PAIR]
        dkv_ref[n:, lanes] = dk[:, PAIR:]
        dkv_ref[:n, vlanes] = dv[:, :PAIR]
        dkv_ref[n:, vlanes] = dv[:, PAIR:]
    dh = dot_nt(dq_ref[...], w_ref[:, :d])
    normed, inv = norm_parts(x_ref[...])
    d_input, sums = norm_back(dh, normed, inv, vec_ref[0:1, :])
    dx_ref[...] = dy + d_input
    sums_ref[0] = sums


def kv_kernel(x_ref, w_ref, out_ref):
    out_ref[...] = dot(x_ref[...], w_ref[...]).astype(BF16)


def image_back_kernel(dkv_ref, w_ref, theirs_ref, mine_ref):
    half = theirs_ref.shape[1]
    both = dot_nt(dkv_ref[...], w_ref[...])
    theirs_ref[...] = both[:, :half].astype(BF16)
    mine_ref[...] = both[:, half:]


def vec_columns(sums, width):
    rows = sums.shape[0]
    full = jnp.concatenate([sums, jnp.zeros((width - rows, sums.shape[1]), F32)], axis=0)
    return full.T.astype(BF16)


def by_section(tab_ref, first, second, kernel):
    @pl.when(tab_ref[0] == 0)
    def _():
        kernel(*first)

    @pl.when(tab_ref[0] == 1)
    def _():
        kernel(*second)


def store_halves(tab_ref, mine_ref, theirs_ref, rows, cols, value):
    chips = mine_ref.shape[0]
    count = value.shape[0] // (2 * chips)
    pairs = value.reshape(chips, 2, count, value.shape[1])
    here = tab_ref[1] == 0
    mine_ref[:, rows, cols] = jnp.where(here, pairs[:, 0], pairs[:, 1]).astype(BF16)
    theirs_ref[:, rows, cols] = jnp.where(here, pairs[:, 1], pairs[:, 0]).astype(BF16)


def ffn_grads_kernel(tab_ref, io, m_ref, du_ref, g_ref, dyb_ref, mine_ref, theirs_ref):
    d = dyb_ref.shape[1]
    blocks = du_ref.shape[1] // d
    store = partial(store_halves, tab_ref, mine_ref, theirs_ref)
    io.need(m_ref, du_ref)
    m = m_ref[...]
    up_rows = m.shape[1] // (2 * mine_ref.shape[0])
    for k in range(blocks):
        part = dot_tn(m, du_ref[:, k * d : (k + 1) * d]).astype(BF16)
        store(slice(k * up_rows, (k + 1) * up_rows), slice(None), part)
    io.flush(theirs_ref, mine_ref, part=0)
    io.need(g_ref, dyb_ref)
    down = dot_tn(g_ref[...], dyb_ref[...]).astype(BF16)
    store(slice(blocks * up_rows, None), slice(None), down)
    io.flush(theirs_ref, mine_ref)


def attn_grads_kernel(tab_ref, io, h_ref, dqkv_ref, o_ref, dyb_ref, asum_ref, fsum_ref, mine_ref, theirs_ref):
    d = dyb_ref.shape[1]
    store = partial(store_halves, tab_ref, mine_ref, theirs_ref, slice(None))
    io.need(h_ref, dqkv_ref)
    store(slice(0, 3 * d), dot_tn(h_ref[...], dqkv_ref[...]).astype(BF16))
    io.flush(theirs_ref, mine_ref, part=0)
    io.need(o_ref, dyb_ref, asum_ref, fsum_ref)
    store(slice(3 * d, 4 * d), dot_tn(o_ref[...], dyb_ref[...]).astype(BF16))
    sums = jnp.concatenate([jnp.sum(asum_ref[...], axis=0)[:2], jnp.sum(fsum_ref[...], axis=0)[:2]])
    store(slice(4 * d, None), vec_columns(sums, PAIR))
    io.flush(theirs_ref, mine_ref)


def cross_grads_kernel(
    tab_ref, io, h_ref, dq_ref, o_ref, dyb_ref, sum_ref, image_ref, dkv_ref, mine_ref, theirs_ref
):
    d = dyb_ref.shape[1]
    io.need(h_ref, dq_ref, o_ref, dyb_ref, sum_ref)

    def store(cols, value):
        half = value.shape[0] // 2
        for s in range(2):
            chips = pl.ds(s * RING, RING)
            store_halves(
                tab_ref, mine_ref.at[chips], theirs_ref.at[chips], slice(None), cols, value[s * half : (s + 1) * half]
            )

    store(slice(0, d), dot_tn(h_ref[...], dq_ref[...]))
    store(slice(3 * d, 4 * d), dot_tn(o_ref[...], dyb_ref[...]))
    store(slice(4 * d, None), vec_columns(jnp.sum(sum_ref[...], axis=0)[:2], PAIR).astype(F32))
    io.need(image_ref, dkv_ref)
    store(slice(d, 3 * d), dot_tn(image_ref[...], dkv_ref[...]))


def sds(shape, dtype):
    return jax.ShapeDtypeStruct(shape, dtype)


def rows_at(base, rows, cols):
    return pl.BlockSpec((rows, cols), lambda i, tab: (i + base, 0))


def whole_spec(shape):
    return pl.BlockSpec(shape, lambda i, tab: (0,) * len(shape), pipeline_mode=pl.Buffered(1))


ANY_SPEC = pl.BlockSpec(memory_space=pl.ANY)


class Unit(NamedTuple):
    arrays: Any
    moves: Any


def begin(unit, tab_ref, refs, targets, sems):
    copies = []
    for j, (array, start, rows, cols, target, lead, place) in enumerate(unit.moves):
        source = refs[array].at[pl.ds(start, rows)]
        if cols is not None:
            source = refs[array].at[pl.ds(start, rows), pl.ds(*cols)]
        row = 0
        if place is not None:
            offset, other, by_core = place
            chip = at_offset(tab_ref, offset)
            core = 1 - tab_ref[1] if other else tab_ref[1]
            at = core * RING + chip if by_core else chip * CORES + core
            row = pl.multiple_of(at * rows, rows)
        to = targets[target]
        to = to.at[pl.ds(row, rows)] if lead is None else to.at[lead, pl.ds(row, rows)]
        copy = pltpu.make_async_copy(source, to, sems.at[j])
        copy.start()
        copies.append(copy)
    return copies


def finish(copies):
    for copy in copies:
        copy.wait()


def vector_rows(table_ref, *vec_refs):
    rows = table_ref[...].astype(F32).T
    for j, vec_ref in enumerate(vec_refs):
        vec_ref[0:2, :] = rows[2 * j : 2 * j + 2, :]


class Stage(NamedTuple):
    kernel: Any
    only: Any
    steps: int
    ins: Any
    outs: Any
    cost: Any
    units: Any = ()
    scratch: Any = ()
    carried: Any = ()
    manual: bool = False
    lazy: bool = False
    cuts: Any = None


class Transfers:
    def __init__(self, incoming, outgoing):
        self.incoming, self.outgoing, self.sent, self.begun = list(incoming), list(outgoing), [], []

    def fetch(self, *refs):
        for copy, ref in self.incoming:
            if any(ref is one for one in refs) and not any(ref is one for one in self.begun):
                copy.start()
                self.begun.append(ref)

    def fetch_all(self):
        self.fetch(*[ref for _, ref in self.incoming])

    def need(self, *refs):
        self.fetch(*refs)
        left = []
        for copy, ref in self.incoming:
            if any(ref is one for one in refs):
                copy.wait()
            else:
                left.append((copy, ref))
        self.incoming = left

    def flush(self, *refs, part=None):
        left = []
        for copy, ref, own in self.outgoing:
            if any(ref is one for one in refs) and (part is None or part == own):
                copy.start()
                self.sent.append(copy)
            else:
                left.append((copy, ref, own))
        self.outgoing = left

    def close(self):
        self.need(*[ref for _, ref in self.incoming])
        self.flush(*[ref for _, ref, _ in self.outgoing])
        for copy in self.sent:
            copy.wait()


def window(spec):
    return tuple(pl.ds(at * size, size) for at, size in zip(spec.index_map(0, None), spec.block_shape))


def pinned(spec, stage, steps):
    index = spec.index_map

    def at(i, tab):
        if stage.steps < steps:
            i = jnp.minimum(i, stage.steps - 1)
        if stage.only is not None:
            i = jnp.where(tab[0] == stage.only, i, 0)
        return index(i, tab)

    return pl.BlockSpec(spec.block_shape, at, pipeline_mode=spec.pipeline_mode)


def taken(refs, count):
    return refs[:count], refs[count:]


def run(tab, stages, after=(), vmem_limit=VMEM_LIMIT):
    steps = max(stage.steps for stage in stages)
    ins, loaded, outs, scratch = [], [], [], []
    for stage in stages:
        if stage.manual:
            loaded += [array for array, _ in stage.ins]
            outs += [(sds(shape, dtype), ANY_SPEC) for shape, dtype, _ in stage.outs]
            scratch += [pltpu.VMEM(spec.block_shape, array.dtype) for array, spec in stage.ins]
            scratch += [pltpu.VMEM(spec.block_shape, dtype) for _, dtype, spec in stage.outs]
            parts = len(stage.cuts[1]) if stage.cuts else 1
            scratch.append(pltpu.SemaphoreType.DMA((len(stage.ins) + parts * len(stage.outs),)))
        else:
            ins += [(array, pinned(spec, stage, steps)) for array, spec in stage.ins]
            outs += [(sds(shape, dtype), pinned(spec, stage, steps)) for shape, dtype, spec in stage.outs]
        loaded += [array for unit in stage.units for array in unit.arrays]
        scratch += list(stage.scratch)
    carried = [buffer for stage in stages for buffer in stage.carried]
    n_skip = len(carried) + len(after)
    aliases, out_base = {}, 0
    for stage in stages:
        out_base += len(stage.outs)
        for j in range(len(stage.carried)):
            aliases[1 + len(ins) + len(loaded) + len(aliases)] = out_base - len(stage.carried) + j

    def manual_part(stage, tab_ref, in_any, unit_any, out_any, own):
        own_in, own = taken(own, len(stage.ins))
        own_out, own = taken(own, len(stage.outs))
        sems, own = own[0], own[1:]
        incoming = [
            (pltpu.make_async_copy(ref.at[window(spec)], to, sems.at[j]), to)
            for j, (ref, (_, spec), to) in enumerate(zip(in_any, stage.ins, own_in))
        ]
        outgoing = []
        for ref, (_, _, spec), source in zip(out_any, stage.outs, own_out):
            to = ref.at[window(spec)]
            start = 0
            for part, end in enumerate(stage.cuts[1] if stage.cuts else (None,)):
                at = (slice(None),) * (stage.cuts[0] if stage.cuts else 0) + (slice(start, end),)
                piece = (source.at[at], to.at[at]) if stage.cuts else (source, to)
                copy = pltpu.make_async_copy(*piece, sems.at[len(stage.ins) + len(outgoing)])
                outgoing.append((copy, source, part))
                start = end
        transfers = Transfers(incoming, outgoing)
        if not stage.lazy:
            transfers.fetch_all()
        stage.kernel(tab_ref, transfers, *own_in, *unit_any, *own_out, *own)
        transfers.close()

    def body(tab_ref, *refs):
        in_refs, refs = taken(refs, len(ins))
        any_refs, refs = taken(refs, len(loaded))
        out_refs, scratch_refs = taken(refs[n_skip:], len(outs))
        for stage in stages:
            own_in, in_refs = taken(in_refs, 0 if stage.manual else len(stage.ins))
            in_any, any_refs = taken(any_refs, len(stage.ins) if stage.manual else 0)
            unit_any, any_refs = taken(any_refs, sum(len(unit.arrays) for unit in stage.units))
            own_out, out_refs = taken(out_refs, len(stage.outs))
            extra = len(stage.ins) + len(stage.outs) + 1 if stage.manual else 0
            own_scratch, scratch_refs = taken(scratch_refs, extra + len(stage.scratch))
            if stage.manual:
                part = partial(manual_part, stage, tab_ref, in_any, unit_any, own_out, own_scratch)
            else:
                part = partial(stage.kernel, tab_ref, *own_in, *unit_any, *own_out, *own_scratch)
            wanted = []
            if stage.only is not None:
                wanted.append(tab_ref[0] == stage.only)
            if stage.steps < steps:
                wanted.append(pl.program_id(0) < stage.steps)
            if wanted:
                pl.when(wanted[0] if len(wanted) == 1 else wanted[0] & wanted[1])(part)
            else:
                part()

    results = pl.pallas_call(
        body,
        grid_spec=pltpu.PrefetchScalarGridSpec(
            num_scalar_prefetch=1,
            grid=(steps,),
            in_specs=[spec for _, spec in ins] + [ANY_SPEC] * (len(loaded) + n_skip),
            out_specs=[spec for _, spec in outs],
            scratch_shapes=scratch,
        ),
        out_shape=[shape for shape, _ in outs],
        input_output_aliases=aliases,
        compiler_params=pltpu.CompilerParams(vmem_limit_bytes=vmem_limit),
        cost_estimate=pl.CostEstimate(
            flops=max(stage.cost[0] for stage in stages),
            bytes_accessed=max(stage.cost[1] for stage in stages),
            transcendentals=0,
        ),
    )(tab, *[array for array, _ in ins], *loaded, *carried, *after)
    split, start = [], 0
    for stage in stages:
        split.append(list(results[start : start + len(stage.outs)]))
        start += len(stage.outs)
    return split


def call(kernel, on, steps, ins, outs, flops, moved, trans=0, carried=(), after=(), vmem_limit=VMEM_LIMIT):
    own = kernel if on[1] is None else lambda tab_ref, *refs: kernel(*refs)
    stage = Stage(own, on[1], steps, ins, outs, (flops, moved), carried=carried)
    if len(on) > 2:
        return stage
    return run(on[0], [stage], after, vmem_limit)[0]


def sums_at(base, d):
    return pl.BlockSpec((1, 8, d), lambda i, tab: (i + base, 0, 0))


def code_at(base):
    return pl.BlockSpec((1, 1, BLOCK), lambda i, tab: (i + base, 0, 0))


def dma(unit):
    return pltpu.SemaphoreType.DMA((len(unit.moves),))


def vmem(shape, dtype=BF16):
    return pltpu.VMEM(shape, dtype)


def first_attention(base, x, code, code_row, attn, carried):
    t, d = x.shape
    n = len(attn.arrays)

    def kernel(tab_ref, io, x_ref, code_ref, code_row_ref, *refs):
        pieces, refs = taken(refs, n)
        outs, (w_ref, vec_ref, sems) = taken(refs, 5)
        finish(begin(attn, tab_ref, pieces, (w_ref,), sems))
        vector_rows(w_ref.at[:, 4 * d : 4 * d + PAIR], vec_ref)
        io.need(x_ref, code_ref, code_row_ref)
        self_fwd_kernel(x_ref, vec_ref, code_ref, code_row_ref, w_ref, *outs)

    widths = ((d, F32), (d, BF16), (3 * d, BF16), (HEADS * TILE, BF16), (d, BF16))
    return Stage(
        kernel,
        0,
        1,
        [(x, rows_at(base, BLOCK, d)), (code, rows_at(base, BLOCK, 2)), (code_row, code_at(base))],
        [((t, wide), dtype, rows_at(base, BLOCK, wide)) for wide, dtype in widths],
        (t * d * 8 * d, d * d * 8 + t * d * 24),
        (attn,),
        (vmem((d, 4 * d + PAIR)), vmem((8, d), F32), dma(attn)),
        carried,
        manual=True,
    )


def first_feed(base, x, ffn, vecs, up_shape, down_shape, carried):
    t, d = x.shape
    ff = down_shape[0]
    n = len(ffn.arrays)

    def kernel(tab_ref, io, x_ref, *refs):
        pieces, refs = taken(refs, n)
        tables, refs = taken(refs, len(vecs.arrays))
        outs, (up_ref, down_ref, table_ref, unused_ref, vec_ref, sems, vec_sems) = taken(refs, 4)
        finish(begin(vecs, tab_ref, tables, (table_ref,), vec_sems))
        copies = begin(ffn, tab_ref, pieces, (up_ref, down_ref), sems)
        vector_rows(table_ref, unused_ref, vec_ref)
        io.need(x_ref)
        each = len(copies) // (up_shape[0] + 1)

        def ready(j):
            finish(copies[j * each : (j + 1) * each])
            if j == up_shape[0]:
                io.flush(*outs[1:])

        ffn_fwd_kernel(x_ref, vec_ref, up_ref, down_ref, *outs, ready=ready)

    return Stage(
        kernel,
        0,
        1,
        [(x, rows_at(base, BLOCK, d))],
        [((BLOCK, d), BF16, rows_at(0, BLOCK, d))]
        + [((t, wide), BF16, rows_at(base, BLOCK, wide)) for wide in (d, ff, ff)],
        (BLOCK * d * 4 * ff, d * ff * 4),
        (ffn, vecs),
        (
            vmem(up_shape),
            vmem(down_shape),
            vmem((d, PAIR)),
            vmem((8, d), F32),
            vmem((8, d), F32),
            dma(ffn),
            dma(vecs),
        ),
        carried,
        manual=True,
    )


def second_layer(base, t, x, code, code_row, kv, cot, attn, cross, ffn, up_shape, down_shape, carried):
    d = x.shape[1]
    ff = down_shape[0]
    n = IMG_MB * PATCHES
    nb = t // BLOCK
    counts = [len(unit.arrays) for unit in (attn, cross, ffn)]

    def kernel(tab_ref, io, x_ref, code_ref, code_row_ref, kv_ref, cot_ref, *refs):
        attn_refs, refs = taken(refs, counts[0])
        cross_refs, refs = taken(refs, counts[1])
        ffn_refs, refs = taken(refs, counts[2])
        outs, scratch = taken(refs, 19)
        (y, dxb, h, o, m, g, dy, du, fsum, ch, co, cdy, cdq, cdkv, csum, dx0, dy1, dqkv, asum) = outs
        (wa, wc, up, down, va, vf, vc, x1, qkv, p, cq, cp, x2, slope, dx2, dx1, sa, sc, sf) = scratch
        io.fetch(x_ref, code_ref, code_row_ref)
        finish(begin(attn, tab_ref, attn_refs, (wa,), sa))
        cross_copies = begin(cross, tab_ref, cross_refs, (wc,), sc)
        io.fetch(kv_ref)
        vector_rows(wa.at[:, 4 * d : 4 * d + PAIR], va, vf)
        io.need(x_ref, code_ref, code_row_ref)
        self_fwd_kernel(x_ref, va, code_ref, code_row_ref, wa, x1, h, qkv, p, o)
        ffn_copies = begin(ffn, tab_ref, ffn_refs, (up, down), sf)
        io.fetch(cot_ref)
        io.flush(h, o)
        io.need(kv_ref)
        finish(cross_copies)
        vector_rows(wc.at[:, 4 * d : 4 * d + PAIR], vc)
        cross_fwd_kernel(x1, vc, code_ref, kv_ref, wc, x2, ch, cq, cp, co)
        io.flush(ch, co)
        finish(ffn_copies)
        ffn_fwd_kernel(x2, vf, up, down, y, m, g, slope)
        io.flush(y, m, g)
        io.need(cot_ref)
        ffn_bwd_kernel(x2, cot_ref, None, vf, slope, up, down, dx2, dy, du, fsum)
        io.flush(dy, du, fsum)
        cross_bwd_kernel(x1, dx2, vc, code_ref, cq, cp, kv_ref, wc, dx1, cdy, cdq, cdkv, csum)
        io.flush(cdy, cdq, cdkv, csum)
        self_bwd_kernel(x_ref, dx1, va, qkv, p, wa, dxb, dx0, dy1, dqkv, asum)

    def rows(wide, dtype=BF16):
        return ((t, wide), dtype, rows_at(base, BLOCK, wide))

    sums = ((nb, 8, d), F32, sums_at(base, d))
    own = ((BLOCK, d), BF16, rows_at(0, BLOCK, d))
    return Stage(
        kernel,
        1,
        1,
        [
            (x, rows_at(0, BLOCK, d)),
            (code, rows_at(base, BLOCK, 2)),
            (code_row, code_at(base)),
            (kv, rows_at(base, n, 2 * d)),
            (cot, rows_at(base, BLOCK, d)),
        ],
        [own, own, rows(d), rows(d), rows(d), rows(ff), rows(d), rows(ff), sums]
        + [rows(d), rows(d), rows(d), rows(d), ((nb * n, 2 * d), BF16, rows_at(base, n, 2 * d)), sums]
        + [rows(d, F32), rows(d), rows(3 * d), sums],
        (BLOCK * d * 24 * d, d * d * 40),
        (attn, cross, ffn),
        (
            vmem((d, 4 * d + PAIR)),
            vmem((d, 4 * d + PAIR)),
            vmem(up_shape),
            vmem(down_shape),
            vmem((8, d), F32),
            vmem((8, d), F32),
            vmem((8, d), F32),
            vmem((BLOCK, d), F32),
            vmem((BLOCK, 3 * d)),
            vmem((BLOCK, HEADS * TILE)),
            vmem((BLOCK, d)),
            vmem((HEADS, BLOCK, PATCHES)),
            vmem((BLOCK, d), F32),
            vmem((BLOCK, ff)),
            vmem((BLOCK, d), F32),
            vmem((BLOCK, d), F32),
            dma(attn),
            dma(cross),
            dma(ffn),
        ),
        carried,
        manual=True,
        lazy=True,
    )


def first_back(base, x1, cot, more, slope, x, qkv, probs, attn, ffn, up_shape, down_shape, carried):
    t, d = x.shape
    ff = down_shape[0]
    nb = t // BLOCK
    counts = [len(unit.arrays) for unit in (attn, ffn)]

    def kernel(tab_ref, io, x1_ref, cot_ref, more_ref, slope_ref, x_ref, qkv_ref, p_ref, *refs):
        attn_refs, refs = taken(refs, counts[0])
        ffn_refs, refs = taken(refs, counts[1])
        (dy, du, fsum, dx0, dy1, dqkv, asum), scratch = taken(refs, 7)
        wa, up, down, va, vf, dx1, dxb, sa, sf = scratch
        ffn_copies = begin(ffn, tab_ref, ffn_refs, (up, down), sf)
        finish(begin(attn, tab_ref, attn_refs, (wa,), sa))
        vector_rows(wa.at[:, 4 * d : 4 * d + PAIR], va, vf)
        finish(ffn_copies)
        io.need(x1_ref, cot_ref, more_ref, slope_ref)
        ffn_bwd_kernel(x1_ref, cot_ref, more_ref, vf, slope_ref, up, down, dx1, dy, du, fsum)
        io.flush(dy, du, fsum)
        io.need(x_ref, qkv_ref, p_ref)
        self_bwd_kernel(x_ref, dx1, va, qkv_ref, p_ref, wa, dxb, dx0, dy1, dqkv, asum)

    def rows(wide, dtype=BF16):
        return ((t, wide), dtype, rows_at(base, BLOCK, wide))

    sums = ((nb, 8, d), F32, sums_at(base, d))
    here = rows_at(base, BLOCK, d)
    return Stage(
        kernel,
        0,
        1,
        [
            (x1, here),
            (cot, here),
            (more, rows_at(0, BLOCK, d)),
            (slope, rows_at(base, BLOCK, ff)),
            (x, here),
            (qkv, rows_at(base, BLOCK, 3 * d)),
            (probs, rows_at(base, BLOCK, HEADS * TILE)),
        ],
        [rows(d), rows(ff), sums, rows(d, F32), rows(d), rows(3 * d), sums],
        (BLOCK * d * 12 * d, d * d * 24),
        (attn, ffn),
        (
            vmem((d, 4 * d + PAIR)),
            vmem(up_shape),
            vmem(down_shape),
            vmem((8, d), F32),
            vmem((8, d), F32),
            vmem((BLOCK, d), F32),
            vmem((BLOCK, d)),
            dma(attn),
            dma(ffn),
        ),
        carried,
        manual=True,
    )


def first_feed_back(base, x1, cot, more, slope, ffn, vecs, up_shape, down_shape, carried):
    t, d = x1.shape
    ff = down_shape[0]
    nb = t // BLOCK

    def kernel(tab_ref, io, x1_ref, cot_ref, more_ref, slope_ref, *refs):
        pieces, refs = taken(refs, len(ffn.arrays))
        tables, refs = taken(refs, len(vecs.arrays))
        (dx1, dy, du, fsum), (up, down, table, va, vf, sf, sv) = taken(refs, 4)
        each = len(ffn.moves) // (up_shape[0] + 1)
        turned = Unit(ffn.arrays, list(ffn.moves[-each:]) + list(ffn.moves[:-each]))
        finish(begin(vecs, tab_ref, tables, (table,), sv))
        copies = begin(turned, tab_ref, pieces, (up, down), sf)
        vector_rows(table, va, vf)
        io.need(x1_ref, cot_ref, more_ref, slope_ref)
        finish(copies[:each])

        def ready(j):
            finish(copies[(j + 1) * each : (j + 2) * each])

        ffn_bwd_kernel(x1_ref, cot_ref, more_ref, vf, slope_ref, up, down, dx1, dy, du, fsum, ready=ready)

    here = rows_at(base, BLOCK, d)
    return Stage(
        kernel,
        0,
        1,
        [(x1, here), (cot, here), (more, rows_at(0, BLOCK, d)), (slope, rows_at(base, BLOCK, ff))],
        [
            ((BLOCK, d), F32, rows_at(0, BLOCK, d)),
            ((t, d), BF16, here),
            ((t, ff), BF16, rows_at(base, BLOCK, ff)),
            ((nb, 8, d), F32, sums_at(base, d)),
        ],
        (BLOCK * d * 4 * ff, d * d * 16),
        (ffn, vecs),
        (
            vmem(up_shape),
            vmem(down_shape),
            vmem((d, PAIR)),
            vmem((8, d), F32),
            vmem((8, d), F32),
            dma(ffn),
            dma(vecs),
        ),
        carried,
        manual=True,
    )


def first_attention_back(base, x, dx1, qkv, probs, attn, carried):
    t, d = x.shape
    nb = t // BLOCK

    def kernel(tab_ref, io, x_ref, dx1_ref, qkv_ref, p_ref, *refs):
        pieces, refs = taken(refs, len(attn.arrays))
        (dx0, dy1, dqkv, asum), (wa, va, dxb, sa) = taken(refs, 4)
        finish(begin(attn, tab_ref, pieces, (wa,), sa))
        vector_rows(wa.at[:, 4 * d : 4 * d + PAIR], va)
        io.need(x_ref, dx1_ref, qkv_ref, p_ref)
        self_bwd_kernel(x_ref, dx1_ref, va, qkv_ref, p_ref, wa, dxb, dx0, dy1, dqkv, asum)

    here = rows_at(base, BLOCK, d)
    return Stage(
        kernel,
        0,
        1,
        [
            (x, here),
            (dx1, rows_at(0, BLOCK, d)),
            (qkv, rows_at(base, BLOCK, 3 * d)),
            (probs, rows_at(base, BLOCK, HEADS * TILE)),
        ],
        [
            ((t, d), F32, here),
            ((t, d), BF16, here),
            ((t, 3 * d), BF16, rows_at(base, BLOCK, 3 * d)),
            ((nb, 8, d), F32, sums_at(base, d)),
        ],
        (BLOCK * d * 8 * d, d * d * 8),
        (attn,),
        (vmem((d, 4 * d + PAIR)), vmem((8, d), F32), vmem((BLOCK, d)), dma(attn)),
        carried,
        manual=True,
    )


def with_unit(kernel, unit, outs):
    def own(tab_ref, io, x_ref, *refs):
        pieces, refs = taken(refs, len(unit.arrays))
        out_refs, (w_ref, sems) = taken(refs, outs)
        finish(begin(unit, tab_ref, pieces, (w_ref,), sems))
        io.need(x_ref)
        for j in range(x_ref.shape[0] // PATCHES):
            rows = pl.ds(j * PATCHES, PATCHES)
            kernel(x_ref.at[rows], w_ref, *[ref.at[rows] for ref in out_refs])

    return own


def image_kv(patches, unit):
    n, d = patches.shape
    return Stage(
        with_unit(kv_kernel, unit, 1),
        1,
        1,
        [(patches, rows_at(0, n, d))],
        [((n, 2 * d), BF16, rows_at(0, n, 2 * d))],
        (n * d * d * 4, n * d * 6 + d * d * 4),
        (unit,),
        (vmem((d, 2 * d)), dma(unit)),
        manual=True,
    )


def image_back(dkv, unit):
    n, d = dkv.shape[0], dkv.shape[1] // 2
    return Stage(
        with_unit(image_back_kernel, unit, 2),
        1,
        1,
        [(dkv, rows_at(0, n, 2 * d))],
        [
            ((n, d // 2), BF16, rows_at(0, n, d // 2)),
            ((n, d // 2), F32, rows_at(0, n, d // 2)),
        ],
        (n * d * d * 4, n * d * 7 + d * d * 4),
        (unit,),
        (vmem((d, 2 * d)), dma(unit)),
        manual=True,
    )


def columns_of(section, rows, cols):
    def index(i, tab):
        return (0, i * (tab[0] if section else 1 - tab[0]))

    return pl.BlockSpec((rows, cols), index)


def sums_of(section, shape):
    def index(i, tab):
        return (0, 0, i * (tab[0] if section else 1 - tab[0]))

    return pl.BlockSpec(shape, index)


def either(kernel, sets, specs, outs, cost, cuts):
    n = len(specs)

    def own(tab_ref, io, *refs):
        first, refs = taken(refs, n)
        second, refs = taken(refs, n)
        out_refs, refs = taken(refs, len(outs))
        to, sems = refs[:n], refs[n]

        def fetched(source):
            return [pltpu.make_async_copy(ref, one, sems.at[j]) for j, (ref, one) in enumerate(zip(source, to))]

        for section, source in enumerate((first, second)):

            @pl.when(tab_ref[0] == section)
            def _(source=source):
                for copy in fetched(source):
                    copy.start()

        waiting = Transfers(list(zip(fetched(first), to)), io.outgoing)
        waiting.begun = list(to)
        kernel(tab_ref, waiting, *to, *out_refs)
        waiting.need(*[ref for _, ref in waiting.incoming])
        io.outgoing, io.sent = waiting.outgoing, waiting.sent

    return Stage(
        own,
        None,
        1,
        [],
        outs,
        cost,
        (Unit(list(sets[0]), ()), Unit(list(sets[1]), ())),
        tuple(pltpu.VMEM(array.shape, array.dtype) for array in sets[0]) + (pltpu.SemaphoreType.DMA((n,)),),
        manual=True,
        cuts=cuts,
    )


def ffn_grads(tab, sets, after=()):
    t, d = sets[0][0].shape
    ff = sets[0][2].shape[1]
    shape = (RING, (ff + 4 * d) // (RING * CORES), d)
    stage = either(
        ffn_grads_kernel,
        sets,
        sets[0],
        [(shape, BF16, whole_spec(shape))] * 2,
        (t * d * ff * 4, t * (ff + d) * 4 + d * ff * 4),
        (1, (ff // d * d // (RING * CORES), shape[1])),
    )
    return run(tab, [stage], after)[0]


def attn_grads(tab, sets, after=()):
    t, d = sets[0][0].shape
    shape = (RING, d // (RING * CORES), 4 * d + PAIR)
    stage = either(
        attn_grads_kernel,
        sets,
        sets[0],
        [(shape, BF16, whole_spec(shape))] * 2,
        (t * d * d * 8, t * d * 12 + d * d * 8),
        (2, (3 * d, shape[2])),
    )
    return run(tab, [stage], after)[0]


def cross_grads(h, dq, patches, dkv, o, dyb, sums):
    t, d = h.shape
    n = patches.shape[0]
    wide = 4 * d + PAIR
    shape = (2 * RING, d // (2 * RING * CORES), wide)
    return Stage(
        cross_grads_kernel,
        1,
        1,
        [
            (h, rows_at(0, t, d)),
            (dq, rows_at(0, t, d)),
            (o, rows_at(0, t, d)),
            (dyb, rows_at(0, t, d)),
            (sums, whole_spec(sums.shape)),
            (patches, rows_at(0, n, d)),
            (dkv, rows_at(0, n, 2 * d)),
        ],
        [(shape, BF16, whole_spec(shape))] * 2,
        (t * d * d * 4 + n * d * d * 4, t * d * 8 + n * d * 6 + d * d * 8),
        manual=True,
    )


def at_offset(tab, offset):
    return tab[2 + RING // 2 + offset]


def join_kernel(tab_ref, *refs, extra, moving, cuts):
    mine_ref, theirs_ref = refs[:2]
    moving_refs, out_refs = taken(refs[2 + extra :], moving)
    rows = mine_ref.shape[1]
    parts = [(0, mine_ref[0].astype(F32) + theirs_ref[0].astype(F32))]
    if extra:
        parts.append((rows, jnp.where(tab_ref[0] == 0, refs[2][0], refs[3][0]).astype(F32)))
    for start, value in parts:
        for ref in moving_refs:
            value = value + ref[start : start + value.shape[0], :].astype(F32)
        for out, row, at, first, count, column, columns in cuts:
            if start <= first < start + value.shape[0]:
                piece = value[first - start : first - start + count, column : column + columns]
                out_refs[out][row : row + count, at : at + columns] = piece.astype(out_refs[out].dtype)


def join(tab, offset, mine, theirs, extra, moving, dtype, after=(), cuts=None):
    cols = mine.shape[2]
    rows = mine.shape[1] + (extra[0].shape[1] if extra else 0)

    def part(array):
        return (array, pl.BlockSpec((1,) + array.shape[1:], lambda i, tab: (at_offset(tab, offset), 0, 0)))

    if cuts is None:
        cuts = [(0, 0, 0, 0, mine.shape[1], 0, cols)]
        if extra:
            cuts.append((0, mine.shape[1], 0, mine.shape[1], extra[0].shape[1], 0, cols))
    shapes = {}
    for out, row, at, _, count, _, columns in cuts:
        have = shapes.get(out, (0, 0))
        shapes[out] = (max(row + count, have[0]), max(at + columns, have[1]))
    shapes = [shapes[out] for out in range(len(shapes))]
    results = call(
        partial(join_kernel, extra=len(extra), moving=len(moving), cuts=cuts),
        (tab, None),
        1,
        [part(array) for array in (mine, theirs) + tuple(extra)]
        + [(array, pl.BlockSpec((rows, cols), lambda i, tab: (0, 0))) for array in moving],
        [(shape, dtype, pl.BlockSpec(shape, lambda i, tab: (0, 0))) for shape in shapes],
        rows * cols * 3,
        rows * cols * 2 * (3 + len(moving)),
        after=after,
        vmem_limit=SMALL_LIMIT,
    )
    return results[0] if len(shapes) == 1 else results


def cross_join_kernel(tab_ref, io, mine_ref, theirs_ref, first_ref, second_ref):
    io.need(mine_ref, theirs_ref)
    first_ref[...] = (mine_ref[:RING].astype(F32) + theirs_ref[:RING].astype(F32)).astype(BF16)
    io.flush(first_ref)
    second_ref[...] = (mine_ref[RING:].astype(F32) + theirs_ref[RING:].astype(F32)).astype(BF16)


def cross_join(mine, theirs):
    shape = (RING,) + mine.shape[1:]
    return Stage(
        cross_join_kernel,
        1,
        1,
        [(mine, whole_spec(mine.shape)), (theirs, whole_spec(theirs.shape))],
        [(shape, BF16, whole_spec(shape))] * 2,
        (mine.size, mine.size * 6),
        manual=True,
    )


def widen_kernel(tab_ref, io, x_ref, out_ref):
    io.need(x_ref)
    out_ref[...] = x_ref[...].astype(F32)


def widen(x, buffer):
    block = whole_spec(x.shape)
    return Stage(
        widen_kernel, 0, 1, [(x, block)], [(x.shape, F32, block)], (0, x.size * 6), carried=(buffer,), manual=True
    )


def relay_kernel(tab_ref, x_ref, out_ref):
    out_ref[...] = x_ref[...]


def relay(x):
    spec = pl.BlockSpec(x.shape, lambda i, tab: (0, 0))
    return Stage(relay_kernel, 1, 1, [(x, spec)], [(x.shape, x.dtype, spec)], (0, x.size * 4))


def pack_kernel(tab_ref, *refs):
    pieces, out_ref = refs[:-1], refs[-1]
    rows = pieces[0].shape[0]
    for j, ref in enumerate(pieces):
        out_ref[j * rows : (j + 1) * rows, :] = ref[...]


def pack(pieces):
    rows, cols = pieces[0].shape
    shape = (len(pieces) * rows, cols)
    return Stage(
        pack_kernel,
        1,
        1,
        [(piece, pl.BlockSpec((rows, cols), lambda i, tab: (0, 0))) for piece in pieces],
        [(shape, BF16, pl.BlockSpec(shape, lambda i, tab: (0, 0)))],
        (0, rows * cols * len(pieces) * 4),
    )


def ring_tables():
    half = RING // 2
    return [2 * z for z in range(half)] + [2 * z + 1 for z in range(half - 1, -1, -1)]


CHIP_AT = ring_tables()


def flat(section, chip, core):
    return section * RING * CORES + chip * CORES + core


def ring_pairs(sections, step):
    return [
        (flat(s, CHIP_AT[i], c), flat(s, CHIP_AT[(i + step) % RING], c))
        for s in sections
        for i in range(RING)
        for c in range(CORES)
    ]


def core_pairs(sections):
    return [
        (flat(s, chip, c), flat(s, chip, 1 - c))
        for s in sections
        for chip in range(RING)
        for c in range(CORES)
    ]


def send(x, pairs):
    return lax.ppermute(x, ("section", "dp"), pairs)


def device_table():
    rank = lax.axis_index("dp")
    chip = rank // CORES % RING
    half = RING // 2
    pos = jnp.where(chip % 2 == 0, chip // 2, RING - 1 - chip // 2)
    slot = lax.iota(jnp.int32, RING + 3)
    at = (pos + slot - 2 - half + RING) % RING
    chips = jnp.where(at < half, 2 * at, 2 * (RING - 1 - at) + 1)
    return jnp.where(slot == 0, lax.axis_index("section"), jnp.where(slot == 1, rank % CORES, chips)).astype(jnp.int32)


class Gather:
    def __init__(self, chunk, sections, long_way, by_core):
        self.chunk, self.sections, self.long_way, self.by_core = chunk, sections, long_way, by_core
        self.arrived = {1: [], -1: []}

    def step(self):
        done = len(self.arrived[self.long_way])
        ways = [way for way in (1, -1) if done < RING // 2 - 1 or way == self.long_way]
        held = {way: self.arrived[way][-1] if done else self.chunk for way in ways}
        for way in ways:
            self.arrived[way].append(send(held[way], ring_pairs(self.sections, way)))

    def last_step(self, held):
        self.arrived[self.long_way].append(send(held, ring_pairs(self.sections, self.long_way)))

    def own_pieces(self):
        held = [(0, self.chunk)]
        for step in range(1, RING // 2 + 1):
            held += [
                (-way * step, self.arrived[way][step - 1]) for way in (1, -1) if step <= len(self.arrived[way])
            ]
        return held

    def pieces(self):
        pieces, places = [], []
        for offset, piece in self.own_pieces():
            pieces += [piece, send(piece, core_pairs(self.sections))]
            places += [(offset, False, self.by_core), (offset, True, self.by_core)]
        return pieces, tuple(places)


class Order:
    def __init__(self):
        self.last = ()

    def mark(self, *outputs):
        self.last = outputs
        return outputs[0]


class Scatter:
    def __init__(self, tab, order, mine, out, sections, long_way, extra=()):
        self.tab, self.order, self.mine = tab, order, mine
        self.sections, self.long_way, self.extra = sections, long_way, extra
        self.theirs = send(out, core_pairs(sections))
        self.moving = {1: [], -1: []}
        self.done = 0

    def step(self):
        for way in (1, -1):
            hops = RING // 2 if way == self.long_way else RING // 2 - 1
            if self.done < hops:
                piece = join(
                    self.tab,
                    way * (hops - self.done),
                    self.mine,
                    self.theirs,
                    self.extra,
                    self.moving[way],
                    BF16,
                    self.order.last,
                )
                self.order.mark(piece)
                self.moving[way] = [send(piece, ring_pairs(self.sections, way))]
        self.done += 1

    def finish(self, cuts):
        moving = self.moving[1] + self.moving[-1]
        results = join(self.tab, 0, self.mine, self.theirs, self.extra, moving, F32, self.order.last, cuts)
        self.order.mark(results[0])
        return results


def lanes_of(vectors, width):
    table = jnp.stack(vectors, axis=1)
    return jnp.pad(table, ((0, 0), (0, width - table.shape[1])))


def local(
    tokens,
    images,
    segments,
    image_ids,
    cotangent,
    norm_gain,
    norm_bias,
    qkv_weight,
    out_weight,
    up_weight,
    down_weight,
    cross_gain,
    cross_bias,
    cross_query,
    cross_kv,
    cross_out,
):
    section = lax.axis_index("section")
    multimodal = section == 1
    tab = device_table()
    t, d = tokens.shape
    ff = up_weight.shape[2]
    nb = t // BLOCK
    members = lax.axis_size("dp")
    ringed = members == RING * CORES and lax.axis_size("section") == 2
    up_rows, down_rows = up_weight.shape[1], down_weight.shape[1]
    split = ff // d

    attn_piece = jnp.concatenate(
        [
            qkv_weight[0],
            out_weight[0],
            lanes_of([norm_gain[0, 0], norm_bias[0, 0], norm_gain[0, 1], norm_bias[0, 1]], PAIR),
        ],
        axis=1,
    ).astype(BF16)
    ffn_piece = jnp.concatenate(
        [up_weight[0, :, j * d : (j + 1) * d] for j in range(split)] + [down_weight[0]], axis=0
    ).astype(BF16)
    cross_piece = jnp.concatenate(
        [cross_query, cross_kv, cross_out, lanes_of([cross_gain, cross_bias], PAIR)], axis=1
    ).astype(BF16)

    row_in_tile = lax.broadcasted_iota(jnp.int32, segments.shape, 0) % (TILE // ROW_LEN)
    code = row_in_tile * (SEGS + 1) + segments
    code_row = code.reshape(nb, 1, BLOCK)
    slots = lax.broadcasted_iota(jnp.int32, (1, 1, SEGS), 2)
    token_image = jnp.sum(
        jnp.where(segments[:, :, None] == slots, image_ids[:, None, :], 0), axis=-1
    )
    codes = jnp.stack([code, token_image], axis=-1).reshape(-1, 2)
    patches = images.reshape(-1, d)

    up_shape, down_shape = (split, d, d), (ff, d)
    cot = cotangent[0]
    order = Order()
    if ringed:
        both, s1 = (0, 1), (1,)
        attn_ring = Gather(attn_piece, both, 1, False)
        ffn_ring = Gather(ffn_piece, both, -1, False)
        for _ in range(RING // 2):
            attn_ring.step()
            ffn_ring.step()
        w_cross = lax.all_gather(cross_piece, ("section", "dp"), axis=0, tiled=True)

        def unit_of(ring, layout):
            pieces, places = ring.pieces()
            moves = [
                (j, start, rows, cols, target, lead, place)
                for start, rows, cols, target, lead in layout
                for j, place in enumerate(places)
            ]
            return Unit(pieces, moves)

        def columns_of_unit(unit, cols):
            return Unit(unit.arrays, [move[:3] + (cols,) + move[4:] for move in unit.moves])

        attn = unit_of(attn_ring, [(0, up_rows, None, 0, None)])
        ffn = unit_of(
            ffn_ring,
            [(j * up_rows, up_rows, None, 0, j) for j in range(split)]
            + [(split * up_rows, down_rows, None, 1, None)],
        )
        cross = Unit([w_cross], [(0, 0, d, None, 0, None, None)])
    else:
        w_attn = lax.all_gather(attn_piece, "dp", axis=0, tiled=True)
        w_ffn = lax.all_gather(ffn_piece, "dp", axis=0, tiled=False)
        w_up = w_ffn[:, : split * up_rows].reshape(members, split, up_rows, d).swapaxes(0, 1).reshape(up_shape)
        w_down = w_ffn[:, split * up_rows :].reshape(down_shape)
        w_cross = lax.all_gather(cross_piece, ("section", "dp"), axis=0, tiled=True)

        def columns_of_unit(unit, cols):
            return Unit(unit.arrays, [move[:3] + (cols,) + move[4:] for move in unit.moves])

        attn = Unit([w_attn], [(0, 0, d, None, 0, None, None)])
        cross = Unit([w_cross], [(0, 0, d, None, 0, None, None)])
        ffn = Unit(
            [w_up.reshape(split * d, d), w_down],
            [(0, j * d, d, None, 0, j, None) for j in range(split)] + [(1, 0, ff, None, 1, None, None)],
        )
    vecs = columns_of_unit(attn, (4 * d, PAIR))
    kv_unit = columns_of_unit(cross, (d, 2 * d))
    a_y, kept, held = [], (), ()
    for b in range(nb):
        (held,) = run(tab, [first_attention(b, tokens, codes, code_row, attn, held)], a_y)
        a_x1 = held[0]
        stages = [first_feed(b, a_x1, ffn, vecs, up_shape, down_shape, kept)]
        if b == nb - 1:
            stages.append(image_kv(patches, kv_unit))
        (y, *kept), *more = run(tab, stages, a_y)
        a_y.append(y)
    a_x1, a_h, a_qkv, a_p, a_o = held
    a_m, a_g, a_slope = kept
    ((kv,),) = more
    arrived = [lax.ppermute(y, "section", [(0, 1)]) for y in a_y]

    b_y, leaving, kept = [], [], ()
    for b in range(nb):
        ((y, low, *kept),) = run(
            tab,
            [
                second_layer(
                    b, t, arrived[b], codes, code_row, kv, cot, attn, cross, ffn, up_shape, down_shape, kept
                )
            ],
        )
        b_y.append(y)
        leaving.append(low)
    (b_h, b_o, b_m, b_g, b_dy, b_du, b_fsum, c_h, c_o, c_dy, c_dq, c_dkv, c_sum) = kept[:13]
    b_dx0, b_dy1, b_dqkv, b_asum = kept[13:]
    returning = [lax.ppermute(low, "section", [(1, 0)]) for low in leaving]

    def layer_zero_back(b, kept):
        return first_back(
            b, a_x1, cot, returning[b], a_slope, tokens, a_qkv, a_p, attn, ffn, up_shape, down_shape, kept
        )

    def cross_terms():
        return jnp.concatenate(
            [dot_tn(c_h, c_dq), dot_tn(patches, c_dkv), dot_tn(c_o, c_dy), columns(c_sum)], axis=1
        )

    def columns(*sums):
        table = jnp.concatenate([jnp.sum(part, axis=0)[:2] for part in sums]).T
        return jnp.pad(table, ((0, 0), (0, PAIR - table.shape[1])))

    if ringed:
        (kept,) = run(tab, [layer_zero_back(0, ())], leaving)
        feed_kept, attn_kept = kept[:3], kept[3:]
        ((c_mine, c_out),) = run(
            tab, [cross_grads(c_h, c_dq, patches, c_dkv, c_o, c_dy, c_sum)], [kept[2]]
        )
        ((a_dx1, a_dy, a_du, a_fsum),) = run(
            tab,
            [first_feed_back(1, a_x1, cot, returning[1], a_slope, ffn, vecs, up_shape, down_shape, feed_kept)],
            [c_mine],
        )
        order.mark(a_dx1)
        c_theirs = send(c_out, core_pairs(s1))
        ffn_mine, ffn_out = ffn_grads(
            tab, ((a_m, a_du, a_g, a_dy), (b_m, b_du, b_g, b_dy)), order.last
        )
        order.mark(ffn_mine)
        ffn_sum = Scatter(tab, order, ffn_mine, ffn_out, both, 1)
        ((c_first, c_second),) = run(tab, [cross_join(c_mine, c_theirs)], order.last)
        order.mark(c_first)
        c_first = lax.ppermute(c_first, "section", [(1, 0)])
        ((a_dx0, a_dy1, a_dqkv, a_asum),) = run(
            tab, [first_attention_back(1, tokens, a_dx1, a_qkv, a_p, attn, attn_kept)], order.last
        )
        order.mark(a_asum)
        attn_mine, attn_out = attn_grads(
            tab,
            (
                (a_h, a_dqkv, a_o, a_dy1, a_asum, a_fsum),
                (b_h, b_dqkv, b_o, b_dy1, b_asum, b_fsum),
            ),
            order.last,
        )
        order.mark(attn_mine)
        ffn_sum.step()
        ((image_theirs, image_mine),) = run(tab, [image_back(c_dkv, kv_unit)], order.last)
        order.mark(image_theirs)
        image_theirs = lax.ppermute(image_theirs, "section", [(1, 0)])
        attn_sum = Scatter(tab, order, attn_mine, attn_out, both, -1, (c_first, c_second))
        while ffn_sum.done < RING // 2:
            ffn_sum.step()
            attn_sum.step()
        ((image_shard,),) = run(tab, [widen(image_theirs, image_mine)], order.last)
        order.mark(image_shard)
        up_g, down_g = ffn_sum.finish(
            [(0, 0, j * d, j * up_rows, up_rows, 0, d) for j in range(split)]
            + [(1, 0, 0, split * up_rows, down_rows, 0, d)]
        )
        attn_sum.step()
        below, few = up_rows, up_rows // 2
        qkv_g, out_g, vec_g, query_g, kv_g, cross_out_g, cross_vec_g = attn_sum.finish(
            [
                (0, 0, 0, 0, up_rows, 0, 3 * d),
                (1, 0, 0, 0, up_rows, 3 * d, d),
                (2, 0, 0, 0, up_rows, 4 * d, PAIR),
                (3, 0, 0, below, few, 0, d),
                (4, 0, 0, below, few, d, 2 * d),
                (5, 0, 0, below, few, 3 * d, d),
                (6, 0, 0, below, few, 4 * d, PAIR),
            ]
        )
    else:

        def summed(first, second):
            grads = jnp.where(multimodal, second, first)
            return lax.psum_scatter(grads, "dp", scatter_dimension=0, tiled=True)

        def ffn_terms(m, du, g, dyb):
            up = dot_tn(m, du).reshape(members, up_rows, split, d).swapaxes(1, 2)
            down = dot_tn(g, dyb).reshape(members, down_rows, d)
            return jnp.concatenate([up.reshape(members, split * up_rows, d), down], axis=1)

        def attn_terms(h, dqkv, o, dyb, asum, fsum):
            return jnp.concatenate([dot_tn(h, dqkv), dot_tn(o, dyb), columns(asum, fsum)], axis=1)

        kept = ()
        for b in range(nb):
            (kept,) = run(tab, [layer_zero_back(b, kept)])
        a_dy, a_du, a_fsum, a_dx0, a_dy1, a_dqkv, a_asum = kept
        ((image_theirs, image_mine),) = run(tab, [image_back(c_dkv, kv_unit)])
        image_theirs = lax.ppermute(image_theirs, "section", [(1, 0)])
        image_shard = jnp.where(multimodal, image_mine, image_theirs.astype(F32))
        ffn_g = summed(ffn_terms(a_m, a_du, a_g, a_dy), ffn_terms(b_m, b_du, b_g, b_dy))[0]
        attn_g = summed(
            attn_terms(a_h, a_dqkv, a_o, a_dy1, a_asum, a_fsum),
            attn_terms(b_h, b_dqkv, b_o, b_dy1, b_asum, b_fsum),
        )
        cross_g = lax.psum_scatter(
            jnp.where(multimodal, cross_terms(), 0.0),
            ("section", "dp"),
            scatter_dimension=0,
            tiled=True,
        )
        qkv_g, out_g, vec_g = attn_g[:, : 3 * d], attn_g[:, 3 * d : 4 * d], attn_g[:, 4 * d :]
        query_g, kv_g, cross_out_g = cross_g[:, :d], cross_g[:, d : 3 * d], cross_g[:, 3 * d : 4 * d]
        cross_vec_g = cross_g[:, 4 * d :]
        up_g = jnp.concatenate([ffn_g[j * up_rows : (j + 1) * up_rows] for j in range(split)], axis=1)
        down_g = ffn_g[split * up_rows :]

    return (
        jnp.where(multimodal, jnp.concatenate(b_y), jnp.concatenate(a_y))[None],
        jnp.where(multimodal, b_dx0, a_dx0)[None],
        image_shard.reshape(images.shape[0], images.shape[1], d // 2),
        vec_g[:, 0:4:2].T[None],
        vec_g[:, 1:4:2].T[None],
        qkv_g[None],
        out_g[None],
        up_g[None],
        down_g[None],
        cross_vec_g[:, 0],
        cross_vec_g[:, 1],
        query_g,
        kv_g,
        cross_out_g,
    )


def solution(mesh):
    in_specs = (
        P("dp", None),
        P("dp", None, None),
        P("dp", None),
        P("dp", None),
        P("section", "dp", None),
        P("section", None, "dp"),
        P("section", None, "dp"),
        P("section", "dp", None),
        P("section", "dp", None),
        P("section", "dp", None),
        P("section", "dp", None),
        P(("section", "dp")),
        P(("section", "dp")),
        P(("section", "dp"), None),
        P(("section", "dp"), None),
        P(("section", "dp"), None),
    )
    out_specs = (
        P("section", "dp", None),
        P("section", "dp", None),
        P("dp", None, "section"),
        P("section", None, "dp"),
        P("section", None, "dp"),
        P("section", "dp", None),
        P("section", "dp", None),
        P("section", "dp", None),
        P("section", "dp", None),
        P(("section", "dp")),
        P(("section", "dp")),
        P(("section", "dp"), None),
        P(("section", "dp"), None),
        P(("section", "dp"), None),
    )
    return jax.shard_map(local, mesh=mesh, in_specs=in_specs, out_specs=out_specs, check_vma=False)
```

```python
from functools import partial
from typing import Any, NamedTuple

import jax
import jax.numpy as jnp
import numpy as np
from jax import lax
from jax.experimental import pallas as pl
from jax.experimental.pallas import tpu as pltpu
from jax.sharding import PartitionSpec as P

HEADS = 12
HEAD_DIM = 64
PATCHES = 576
ROW_LEN = 64
SEGS = 3
IMG_MB = 2
ROWS_MB = 4
CORES = 2
RING = 8
BLOCK = ROWS_MB * ROW_LEN
PAIR = 2 * HEAD_DIM
PAIRS = HEADS // 2
TILE = 2 * ROW_LEN
MASKED_SCORE = -1000000000.0
NORM_EPS = 1e-05
SCALE = HEAD_DIM ** (-0.5)
VMEM_LIMIT = 56 * 1024 * 1024
SMALL_LIMIT = 12 * 1024 * 1024

F32 = jnp.float32
BF16 = jnp.bfloat16


def dot(a, b):
    return lax.dot_general(a, b, (((1,), (0,)), ((), ())), preferred_element_type=F32)


def dot_nt(a, b):
    return lax.dot_general(a, b, (((1,), (1,)), ((), ())), preferred_element_type=F32)


def dot_tn(a, b):
    return lax.dot_general(a, b, (((0,), (0,)), ((), ())), preferred_element_type=F32)


def norm_parts(x):
    mean = jnp.mean(x, axis=-1, keepdims=True)
    centred = x - mean
    inv = lax.rsqrt(jnp.mean(centred * centred, axis=-1, keepdims=True) + NORM_EPS)
    return centred * inv, inv


def norm_back(d_out, normed, inv, gain):
    d_normed = d_out * gain
    d_input = inv * (
        d_normed
        - jnp.mean(d_normed, axis=-1, keepdims=True)
        - normed * jnp.mean(d_normed * normed, axis=-1, keepdims=True)
    )
    sums = jnp.concatenate(
        [
            jnp.sum(d_out * normed, axis=0, keepdims=True),
            jnp.sum(d_out, axis=0, keepdims=True),
            jnp.zeros((6, d_out.shape[1]), F32),
        ],
        axis=0,
    )
    return d_input, sums


def lane_masks(dtype):
    lane = lax.broadcasted_iota(jnp.int32, (1, PAIR), 1)
    even = (lane < HEAD_DIM).astype(F32)
    return even.astype(dtype), (1.0 - even).astype(dtype)


def softmax(scores):
    top = jnp.max(scores, axis=-1, keepdims=True)
    e = jnp.exp(scores - top)
    return (e * (1.0 / jnp.sum(e, axis=-1, keepdims=True))).astype(BF16)


def stack_heads(part, even, odd):
    return jnp.concatenate([part * even, part * odd], axis=0)


def self_fwd_kernel(x_ref, vec_ref, code_ref, code_row_ref, w_ref, x1_ref, h_ref, qkv_ref, p_ref, o_ref):
    d = x_ref.shape[1]
    x = x_ref[...].astype(F32)
    normed, _ = norm_parts(x)
    h = (normed * vec_ref[0:1, :] + vec_ref[1:2, :]).astype(BF16)
    h_ref[...] = h
    qkv_ref[...] = dot(h, w_ref[:, : 3 * d]).astype(BF16)
    even, odd = lane_masks(BF16)
    for t in range(BLOCK // TILE):
        rows = slice(t * TILE, (t + 1) * TILE)
        causal = lax.broadcasted_iota(jnp.int32, (TILE, TILE), 1) <= lax.broadcasted_iota(
            jnp.int32, (TILE, TILE), 0
        )
        allowed = (code_ref[rows, 0:1] == code_row_ref[0, :, rows]) & causal
        for p in range(PAIRS):
            lanes = slice(p * PAIR, (p + 1) * PAIR)
            q = qkv_ref[rows, lanes] * jnp.asarray(SCALE, BF16)
            k2 = stack_heads(qkv_ref[rows, d + p * PAIR : d + (p + 1) * PAIR], even, odd)
            v2 = stack_heads(qkv_ref[rows, 2 * d + p * PAIR : 2 * d + (p + 1) * PAIR], even, odd)
            s = dot_nt(q, k2)
            probs = jnp.concatenate(
                [
                    softmax(jnp.where(allowed, s[:, :TILE], MASKED_SCORE)),
                    softmax(jnp.where(allowed, s[:, TILE:], MASKED_SCORE)),
                ],
                axis=1,
            )
            p_ref[rows, 2 * p * TILE : 2 * (p + 1) * TILE] = probs
            o_ref[rows, lanes] = dot(probs, v2).astype(BF16)
    x1_ref[...] = x + dot(o_ref[...], w_ref[:, 3 * d : 4 * d])


def self_bwd_kernel(x_ref, dy_ref, vec_ref, qkv_ref, p_ref, w_ref, dxb_ref, dx_ref, dyb_ref, dqkv_ref, sums_ref):
    d = x_ref.shape[1]
    dy = dy_ref[...]
    dyb = dy.astype(BF16)
    dyb_ref[...] = dyb
    d_mixed = dot_nt(dyb, w_ref[:, 3 * d : 4 * d]).astype(BF16)
    even, odd = lane_masks(BF16)
    for t in range(BLOCK // TILE):
        rows = slice(t * TILE, (t + 1) * TILE)
        for p in range(PAIRS):
            lanes = slice(p * PAIR, (p + 1) * PAIR)
            q2 = stack_heads(qkv_ref[rows, lanes] * jnp.asarray(SCALE, BF16), even, odd)
            k2 = stack_heads(qkv_ref[rows, d + p * PAIR : d + (p + 1) * PAIR], even, odd)
            v2 = stack_heads(qkv_ref[rows, 2 * d + p * PAIR : 2 * d + (p + 1) * PAIR], even, odd)
            do = d_mixed[rows, lanes]
            do2 = stack_heads(do, even, odd)
            dp = dot_nt(do, v2)
            probs_e = p_ref[rows, 2 * p * TILE : (2 * p + 1) * TILE]
            probs_o = p_ref[rows, (2 * p + 1) * TILE : (2 * p + 2) * TILE]
            ds = []
            for probs, part in ((probs_e, dp[:, :TILE]), (probs_o, dp[:, TILE:])):
                pf = probs.astype(F32)
                term = pf * part
                ds.append((term - pf * jnp.sum(term, axis=-1, keepdims=True)).astype(BF16))
            dq = dot(jnp.concatenate(ds, axis=1), k2) * SCALE
            dk = dot_tn(jnp.concatenate(ds, axis=0), q2)
            dv = dot_tn(jnp.concatenate([probs_e, probs_o], axis=0), do2)
            dqkv_ref[rows, lanes] = dq.astype(BF16)
            dqkv_ref[rows, d + p * PAIR : d + (p + 1) * PAIR] = dk.astype(BF16)
            dqkv_ref[rows, 2 * d + p * PAIR : 2 * d + (p + 1) * PAIR] = dv.astype(BF16)
    dh = dot_nt(dqkv_ref[...], w_ref[:, : 3 * d])
    normed, inv = norm_parts(x_ref[...].astype(F32))
    d_input, sums = norm_back(dh, normed, inv, vec_ref[0:1, :])
    dx = dy + d_input
    dx_ref[...] = dx
    dxb_ref[...] = dx.astype(BF16)
    sums_ref[0] = sums


def gelu_parts(u):
    phi = 0.5 + 0.5 * lax.erf(u * (0.5**0.5))
    slope = phi + u * (jnp.exp(-0.5 * (u * u)) * ((2.0 * np.pi) ** -0.5))
    return u * phi, slope


def ffn_fwd_kernel(x_ref, vec_ref, up_ref, down_ref, y_ref, m_ref, g_ref, slope_ref, ready=None):
    d = x_ref.shape[1]
    x = x_ref[...]
    normed, _ = norm_parts(x)
    m = (normed * vec_ref[0:1, :] + vec_ref[1:2, :]).astype(BF16)
    m_ref[...] = m
    acc = x
    for j in range(up_ref.shape[0]):
        cols = slice(j * d, (j + 1) * d)
        if ready is not None:
            ready(j)
        g, slope = gelu_parts(dot(m, up_ref[j]))
        g = g.astype(BF16)
        g_ref[:, cols] = g
        slope_ref[:, cols] = slope.astype(BF16)
        if ready is None:
            acc = acc + dot(g, down_ref[cols, :])
    if ready is not None:
        ready(up_ref.shape[0])
        acc = acc + dot(g_ref[...], down_ref[...])
    y_ref[...] = acc.astype(y_ref.dtype)


def ffn_bwd_kernel(x_ref, dy_ref, more_ref, vec_ref, slope_ref, up_ref, down_ref, dx_ref, dyb_ref, du_ref, sums_ref, ready=None):
    d = x_ref.shape[1]
    dy = dy_ref[...].astype(F32)
    if more_ref is not None:
        dy = dy + more_ref[...].astype(F32)
    dyb = dy.astype(BF16)
    dyb_ref[...] = dyb
    acc = None
    for j in range(up_ref.shape[0]):
        cols = slice(j * d, (j + 1) * d)
        du = (dot_nt(dyb, down_ref[cols, :]) * slope_ref[:, cols].astype(F32)).astype(BF16)
        du_ref[:, cols] = du
        if ready is not None:
            ready(j)
        part = dot_nt(du, up_ref[j])
        acc = part if acc is None else acc + part
    normed, inv = norm_parts(x_ref[...])
    d_input, sums = norm_back(acc, normed, inv, vec_ref[0:1, :])
    dx_ref[...] = dy + d_input
    sums_ref[0] = sums


def tied(part, first, second):
    return jnp.concatenate([part * first, part * second], axis=1)


def cross_fwd_kernel(x_ref, vec_ref, image_ref, kv_ref, w_ref, x2_ref, h_ref, q_ref, p_ref, o_ref):
    d = x_ref.shape[1]
    n = PATCHES
    x = x_ref[...]
    normed, _ = norm_parts(x)
    h = (normed * vec_ref[0:1, :] + vec_ref[1:2, :]).astype(BF16)
    h_ref[...] = h
    q_ref[...] = dot(h, w_ref[:, :d]).astype(BF16)
    even, odd = lane_masks(BF16)
    image = image_ref[:, 1:2].astype(F32)
    second = image.astype(BF16)
    first = (1.0 - image).astype(BF16)
    lane_even = lax.broadcasted_iota(jnp.int32, (BLOCK, PAIR), 1) < HEAD_DIM
    is_first = jnp.broadcast_to(image, (BLOCK, PAIR)) < 0.5
    for p in range(PAIRS):
        lanes = slice(p * PAIR, (p + 1) * PAIR)
        vlanes = slice(d + p * PAIR, d + (p + 1) * PAIR)
        k2 = jnp.concatenate([kv_ref[:n, lanes], kv_ref[n:, lanes]], axis=1)
        v2 = jnp.concatenate([kv_ref[:n, vlanes], kv_ref[n:, vlanes]], axis=1)
        q = q_ref[:, lanes] * jnp.asarray(SCALE, BF16)
        out = []
        for half, mask in enumerate((even, odd)):
            probs = softmax(dot_nt(tied(q * mask, first, second), k2))
            p_ref[2 * p + half, :, :n] = probs
            both = dot(probs, v2)
            out.append(jnp.where(is_first, both[:, :PAIR], both[:, PAIR:]))
        o_ref[:, lanes] = jnp.where(lane_even, out[0], out[1]).astype(BF16)
    x2_ref[...] = x + dot(o_ref[...], w_ref[:, 3 * d : 4 * d])


def cross_bwd_kernel(
    x_ref, dy_ref, vec_ref, image_ref, q_ref, p_ref, kv_ref, w_ref, dx_ref, dyb_ref, dq_ref, dkv_ref, sums_ref
):
    d = x_ref.shape[1]
    n = PATCHES
    dy = dy_ref[...]
    dyb = dy.astype(BF16)
    dyb_ref[...] = dyb
    d_mixed = dot_nt(dyb, w_ref[:, 3 * d : 4 * d]).astype(BF16)
    even, odd = lane_masks(BF16)
    image = image_ref[:, 1:2].astype(F32)
    second = image.astype(BF16)
    first = (1.0 - image).astype(BF16)
    lane_even = lax.broadcasted_iota(jnp.int32, (BLOCK, PAIR), 1) < HEAD_DIM
    is_first = jnp.broadcast_to(image, (BLOCK, PAIR)) < 0.5
    for p in range(PAIRS):
        lanes = slice(p * PAIR, (p + 1) * PAIR)
        vlanes = slice(d + p * PAIR, d + (p + 1) * PAIR)
        k2 = jnp.concatenate([kv_ref[:n, lanes], kv_ref[n:, lanes]], axis=1)
        v2 = jnp.concatenate([kv_ref[:n, vlanes], kv_ref[n:, vlanes]], axis=1)
        q = q_ref[:, lanes] * jnp.asarray(SCALE, BF16)
        do = d_mixed[:, lanes]
        ds, qq, dd, dq = [], [], [], []
        for half, mask in enumerate((even, odd)):
            qq.append(tied(q * mask, first, second))
            dd.append(tied(do * mask, first, second))
            dp = dot_nt(dd[half], v2)
            pf = p_ref[2 * p + half, :, :n].astype(F32)
            term = pf * dp
            ds.append((term - pf * jnp.sum(term, axis=-1, keepdims=True)).astype(BF16))
            both = dot(ds[half], k2)
            dq.append(jnp.where(is_first, both[:, :PAIR], both[:, PAIR:]))
        dq_ref[:, lanes] = (jnp.where(lane_even, dq[0], dq[1]) * SCALE).astype(BF16)
        dk = dot_tn(jnp.concatenate(ds, axis=0), jnp.concatenate(qq, axis=0)).astype(BF16)
        dv = dot_tn(
            jnp.concatenate([p_ref[2 * p, :, :n], p_ref[2 * p + 1, :, :n]], axis=0), jnp.concatenate(dd, axis=0)
        ).astype(BF16)
        dkv_ref[:n, lanes] = dk[:, :PAIR]
        dkv_ref[n:, lanes] = dk[:, PAIR:]
        dkv_ref[:n, vlanes] = dv[:, :PAIR]
        dkv_ref[n:, vlanes] = dv[:, PAIR:]
    dh = dot_nt(dq_ref[...], w_ref[:, :d])
    normed, inv = norm_parts(x_ref[...])
    d_input, sums = norm_back(dh, normed, inv, vec_ref[0:1, :])
    dx_ref[...] = dy + d_input
    sums_ref[0] = sums


def kv_kernel(x_ref, w_ref, out_ref):
    out_ref[...] = dot(x_ref[...], w_ref[...]).astype(BF16)


def image_back_kernel(dkv_ref, w_ref, theirs_ref, mine_ref):
    half = theirs_ref.shape[1]
    both = dot_nt(dkv_ref[...], w_ref[...])
    theirs_ref[...] = both[:, :half].astype(BF16)
    mine_ref[...] = both[:, half:]


def vec_columns(sums, width):
    rows = sums.shape[0]
    full = jnp.concatenate([sums, jnp.zeros((width - rows, sums.shape[1]), F32)], axis=0)
    return full.T.astype(BF16)


def by_section(tab_ref, first, second, kernel):
    @pl.when(tab_ref[0] == 0)
    def _():
        kernel(*first)

    @pl.when(tab_ref[0] == 1)
    def _():
        kernel(*second)


def store_halves(tab_ref, mine_ref, theirs_ref, rows, cols, value):
    chips = mine_ref.shape[0]
    count = value.shape[0] // (2 * chips)
    pairs = value.reshape(chips, 2, count, value.shape[1])
    here = tab_ref[1] == 0
    mine_ref[:, rows, cols] = jnp.where(here, pairs[:, 0], pairs[:, 1]).astype(BF16)
    theirs_ref[:, rows, cols] = jnp.where(here, pairs[:, 1], pairs[:, 0]).astype(BF16)


def ffn_grads_kernel(tab_ref, io, m_ref, du_ref, g_ref, dyb_ref, mine_ref, theirs_ref):
    d = dyb_ref.shape[1]
    blocks = du_ref.shape[1] // d
    store = partial(store_halves, tab_ref, mine_ref, theirs_ref)
    io.need(m_ref, du_ref)
    m = m_ref[...]
    up_rows = m.shape[1] // (2 * mine_ref.shape[0])
    for k in range(blocks):
        part = dot_tn(m, du_ref[:, k * d : (k + 1) * d]).astype(BF16)
        store(slice(k * up_rows, (k + 1) * up_rows), slice(None), part)
    io.flush(theirs_ref, mine_ref, part=0)
    io.need(g_ref, dyb_ref)
    down = dot_tn(g_ref[...], dyb_ref[...]).astype(BF16)
    store(slice(blocks * up_rows, None), slice(None), down)
    io.flush(theirs_ref, mine_ref)


def attn_grads_kernel(tab_ref, io, h_ref, dqkv_ref, o_ref, dyb_ref, asum_ref, fsum_ref, mine_ref, theirs_ref):
    d = dyb_ref.shape[1]
    store = partial(store_halves, tab_ref, mine_ref, theirs_ref, slice(None))
    io.need(h_ref, dqkv_ref)
    store(slice(0, 3 * d), dot_tn(h_ref[...], dqkv_ref[...]).astype(BF16))
    io.flush(theirs_ref, mine_ref, part=0)
    io.need(o_ref, dyb_ref, asum_ref, fsum_ref)
    store(slice(3 * d, 4 * d), dot_tn(o_ref[...], dyb_ref[...]).astype(BF16))
    sums = jnp.concatenate([jnp.sum(asum_ref[...], axis=0)[:2], jnp.sum(fsum_ref[...], axis=0)[:2]])
    store(slice(4 * d, None), vec_columns(sums, PAIR))
    io.flush(theirs_ref, mine_ref)


def cross_grads_kernel(
    tab_ref, io, h_ref, dq_ref, o_ref, dyb_ref, sum_ref, image_ref, dkv_ref, mine_ref, theirs_ref
):
    d = dyb_ref.shape[1]
    io.need(h_ref, dq_ref, o_ref, dyb_ref, sum_ref)

    def store(cols, value):
        half = value.shape[0] // 2
        for s in range(2):
            chips = pl.ds(s * RING, RING)
            store_halves(
                tab_ref, mine_ref.at[chips], theirs_ref.at[chips], slice(None), cols, value[s * half : (s + 1) * half]
            )

    store(slice(0, d), dot_tn(h_ref[...], dq_ref[...]))
    store(slice(3 * d, 4 * d), dot_tn(o_ref[...], dyb_ref[...]))
    store(slice(4 * d, None), vec_columns(jnp.sum(sum_ref[...], axis=0)[:2], PAIR).astype(F32))
    io.need(image_ref, dkv_ref)
    store(slice(d, 3 * d), dot_tn(image_ref[...], dkv_ref[...]))


def sds(shape, dtype):
    return jax.ShapeDtypeStruct(shape, dtype)


def rows_at(base, rows, cols):
    return pl.BlockSpec((rows, cols), lambda i, tab: (i + base, 0))


def whole_spec(shape):
    return pl.BlockSpec(shape, lambda i, tab: (0,) * len(shape), pipeline_mode=pl.Buffered(1))


ANY_SPEC = pl.BlockSpec(memory_space=pl.ANY)


class Unit(NamedTuple):
    arrays: Any
    moves: Any


def begin(unit, tab_ref, refs, targets, sems):
    copies = []
    for j, (array, start, rows, cols, target, lead, place) in enumerate(unit.moves):
        source = refs[array].at[pl.ds(start, rows)]
        if cols is not None:
            source = refs[array].at[pl.ds(start, rows), pl.ds(*cols)]
        row = 0
        if place is not None:
            offset, other, by_core = place
            chip = at_offset(tab_ref, offset)
            core = 1 - tab_ref[1] if other else tab_ref[1]
            at = core * RING + chip if by_core else chip * CORES + core
            row = pl.multiple_of(at * rows, rows)
        to = targets[target]
        to = to.at[pl.ds(row, rows)] if lead is None else to.at[lead, pl.ds(row, rows)]
        copy = pltpu.make_async_copy(source, to, sems.at[j])
        copy.start()
        copies.append(copy)
    return copies


def finish(copies):
    for copy in copies:
        copy.wait()


def vector_rows(table_ref, *vec_refs):
    rows = table_ref[...].astype(F32).T
    for j, vec_ref in enumerate(vec_refs):
        vec_ref[0:2, :] = rows[2 * j : 2 * j + 2, :]


class Stage(NamedTuple):
    kernel: Any
    only: Any
    steps: int
    ins: Any
    outs: Any
    cost: Any
    units: Any = ()
    scratch: Any = ()
    carried: Any = ()
    manual: bool = False
    lazy: bool = False
    cuts: Any = None


class Transfers:
    def __init__(self, incoming, outgoing):
        self.incoming, self.outgoing, self.sent, self.begun = list(incoming), list(outgoing), [], []

    def fetch(self, *refs):
        for copy, ref in self.incoming:
            if any(ref is one for one in refs) and not any(ref is one for one in self.begun):
                copy.start()
                self.begun.append(ref)

    def fetch_all(self):
        self.fetch(*[ref for _, ref in self.incoming])

    def need(self, *refs):
        self.fetch(*refs)
        left = []
        for copy, ref in self.incoming:
            if any(ref is one for one in refs):
                copy.wait()
            else:
                left.append((copy, ref))
        self.incoming = left

    def flush(self, *refs, part=None):
        left = []
        for copy, ref, own in self.outgoing:
            if any(ref is one for one in refs) and (part is None or part == own):
                copy.start()
                self.sent.append(copy)
            else:
                left.append((copy, ref, own))
        self.outgoing = left

    def close(self):
        self.need(*[ref for _, ref in self.incoming])
        self.flush(*[ref for _, ref, _ in self.outgoing])
        for copy in self.sent:
            copy.wait()


def window(spec):
    return tuple(pl.ds(at * size, size) for at, size in zip(spec.index_map(0, None), spec.block_shape))


def pinned(spec, stage, steps):
    index = spec.index_map

    def at(i, tab):
        if stage.steps < steps:
            i = jnp.minimum(i, stage.steps - 1)
        if stage.only is not None:
            i = jnp.where(tab[0] == stage.only, i, 0)
        return index(i, tab)

    return pl.BlockSpec(spec.block_shape, at, pipeline_mode=spec.pipeline_mode)


def taken(refs, count):
    return refs[:count], refs[count:]


def run(tab, stages, after=(), vmem_limit=VMEM_LIMIT):
    steps = max(stage.steps for stage in stages)
    ins, loaded, outs, scratch = [], [], [], []
    for stage in stages:
        if stage.manual:
            loaded += [array for array, _ in stage.ins]
            outs += [(sds(shape, dtype), ANY_SPEC) for shape, dtype, _ in stage.outs]
            scratch += [pltpu.VMEM(spec.block_shape, array.dtype) for array, spec in stage.ins]
            scratch += [pltpu.VMEM(spec.block_shape, dtype) for _, dtype, spec in stage.outs]
            parts = len(stage.cuts[1]) if stage.cuts else 1
            scratch.append(pltpu.SemaphoreType.DMA((len(stage.ins) + parts * len(stage.outs),)))
        else:
            ins += [(array, pinned(spec, stage, steps)) for array, spec in stage.ins]
            outs += [(sds(shape, dtype), pinned(spec, stage, steps)) for shape, dtype, spec in stage.outs]
        loaded += [array for unit in stage.units for array in unit.arrays]
        scratch += list(stage.scratch)
    carried = [buffer for stage in stages for buffer in stage.carried]
    n_skip = len(carried) + len(after)
    aliases, out_base = {}, 0
    for stage in stages:
        out_base += len(stage.outs)
        for j in range(len(stage.carried)):
            aliases[1 + len(ins) + len(loaded) + len(aliases)] = out_base - len(stage.carried) + j

    def manual_part(stage, tab_ref, in_any, unit_any, out_any, own):
        own_in, own = taken(own, len(stage.ins))
        own_out, own = taken(own, len(stage.outs))
        sems, own = own[0], own[1:]
        incoming = [
            (pltpu.make_async_copy(ref.at[window(spec)], to, sems.at[j]), to)
            for j, (ref, (_, spec), to) in enumerate(zip(in_any, stage.ins, own_in))
        ]
        outgoing = []
        for ref, (_, _, spec), source in zip(out_any, stage.outs, own_out):
            to = ref.at[window(spec)]
            start = 0
            for part, end in enumerate(stage.cuts[1] if stage.cuts else (None,)):
                at = (slice(None),) * (stage.cuts[0] if stage.cuts else 0) + (slice(start, end),)
                piece = (source.at[at], to.at[at]) if stage.cuts else (source, to)
                copy = pltpu.make_async_copy(*piece, sems.at[len(stage.ins) + len(outgoing)])
                outgoing.append((copy, source, part))
                start = end
        transfers = Transfers(incoming, outgoing)
        if not stage.lazy:
            transfers.fetch_all()
        stage.kernel(tab_ref, transfers, *own_in, *unit_any, *own_out, *own)
        transfers.close()

    def body(tab_ref, *refs):
        in_refs, refs = taken(refs, len(ins))
        any_refs, refs = taken(refs, len(loaded))
        out_refs, scratch_refs = taken(refs[n_skip:], len(outs))
        for stage in stages:
            own_in, in_refs = taken(in_refs, 0 if stage.manual else len(stage.ins))
            in_any, any_refs = taken(any_refs, len(stage.ins) if stage.manual else 0)
            unit_any, any_refs = taken(any_refs, sum(len(unit.arrays) for unit in stage.units))
            own_out, out_refs = taken(out_refs, len(stage.outs))
            extra = len(stage.ins) + len(stage.outs) + 1 if stage.manual else 0
            own_scratch, scratch_refs = taken(scratch_refs, extra + len(stage.scratch))
            if stage.manual:
                part = partial(manual_part, stage, tab_ref, in_any, unit_any, own_out, own_scratch)
            else:
                part = partial(stage.kernel, tab_ref, *own_in, *unit_any, *own_out, *own_scratch)
            wanted = []
            if stage.only is not None:
                wanted.append(tab_ref[0] == stage.only)
            if stage.steps < steps:
                wanted.append(pl.program_id(0) < stage.steps)
            if wanted:
                pl.when(wanted[0] if len(wanted) == 1 else wanted[0] & wanted[1])(part)
            else:
                part()

    results = pl.pallas_call(
        body,
        grid_spec=pltpu.PrefetchScalarGridSpec(
            num_scalar_prefetch=1,
            grid=(steps,),
            in_specs=[spec for _, spec in ins] + [ANY_SPEC] * (len(loaded) + n_skip),
            out_specs=[spec for _, spec in outs],
            scratch_shapes=scratch,
        ),
        out_shape=[shape for shape, _ in outs],
        input_output_aliases=aliases,
        compiler_params=pltpu.CompilerParams(vmem_limit_bytes=vmem_limit),
        cost_estimate=pl.CostEstimate(
            flops=max(stage.cost[0] for stage in stages),
            bytes_accessed=max(stage.cost[1] for stage in stages),
            transcendentals=0,
        ),
    )(tab, *[array for array, _ in ins], *loaded, *carried, *after)
    split, start = [], 0
    for stage in stages:
        split.append(list(results[start : start + len(stage.outs)]))
        start += len(stage.outs)
    return split


def call(kernel, on, steps, ins, outs, flops, moved, trans=0, carried=(), after=(), vmem_limit=VMEM_LIMIT):
    own = kernel if on[1] is None else lambda tab_ref, *refs: kernel(*refs)
    stage = Stage(own, on[1], steps, ins, outs, (flops, moved), carried=carried)
    if len(on) > 2:
        return stage
    return run(on[0], [stage], after, vmem_limit)[0]


def sums_at(base, d):
    return pl.BlockSpec((1, 8, d), lambda i, tab: (i + base, 0, 0))


def code_at(base):
    return pl.BlockSpec((1, 1, BLOCK), lambda i, tab: (i + base, 0, 0))


def dma(unit):
    return pltpu.SemaphoreType.DMA((len(unit.moves),))


def vmem(shape, dtype=BF16):
    return pltpu.VMEM(shape, dtype)


def first_attention(base, x, code, code_row, attn, carried):
    t, d = x.shape
    n = len(attn.arrays)

    def kernel(tab_ref, io, x_ref, code_ref, code_row_ref, *refs):
        pieces, refs = taken(refs, n)
        outs, (w_ref, vec_ref, sems) = taken(refs, 5)
        finish(begin(attn, tab_ref, pieces, (w_ref,), sems))
        vector_rows(w_ref.at[:, 4 * d : 4 * d + PAIR], vec_ref)
        io.need(x_ref, code_ref, code_row_ref)
        self_fwd_kernel(x_ref, vec_ref, code_ref, code_row_ref, w_ref, *outs)

    widths = ((d, F32), (d, BF16), (3 * d, BF16), (HEADS * TILE, BF16), (d, BF16))
    return Stage(
        kernel,
        0,
        1,
        [(x, rows_at(base, BLOCK, d)), (code, rows_at(base, BLOCK, 2)), (code_row, code_at(base))],
        [((t, wide), dtype, rows_at(base, BLOCK, wide)) for wide, dtype in widths],
        (t * d * 8 * d, d * d * 8 + t * d * 24),
        (attn,),
        (vmem((d, 4 * d + PAIR)), vmem((8, d), F32), dma(attn)),
        carried,
        manual=True,
    )


def first_feed(base, x, ffn, vecs, up_shape, down_shape, carried):
    t, d = x.shape
    ff = down_shape[0]
    n = len(ffn.arrays)

    def kernel(tab_ref, io, x_ref, *refs):
        pieces, refs = taken(refs, n)
        tables, refs = taken(refs, len(vecs.arrays))
        outs, (up_ref, down_ref, table_ref, unused_ref, vec_ref, sems, vec_sems) = taken(refs, 4)
        finish(begin(vecs, tab_ref, tables, (table_ref,), vec_sems))
        copies = begin(ffn, tab_ref, pieces, (up_ref, down_ref), sems)
        vector_rows(table_ref, unused_ref, vec_ref)
        io.need(x_ref)
        each = len(copies) // (up_shape[0] + 1)

        def ready(j):
            finish(copies[j * each : (j + 1) * each])
            if j == up_shape[0]:
                io.flush(*outs[1:])

        ffn_fwd_kernel(x_ref, vec_ref, up_ref, down_ref, *outs, ready=ready)

    return Stage(
        kernel,
        0,
        1,
        [(x, rows_at(base, BLOCK, d))],
        [((BLOCK, d), BF16, rows_at(0, BLOCK, d))]
        + [((t, wide), BF16, rows_at(base, BLOCK, wide)) for wide in (d, ff, ff)],
        (BLOCK * d * 4 * ff, d * ff * 4),
        (ffn, vecs),
        (
            vmem(up_shape),
            vmem(down_shape),
            vmem((d, PAIR)),
            vmem((8, d), F32),
            vmem((8, d), F32),
            dma(ffn),
            dma(vecs),
        ),
        carried,
        manual=True,
    )


def second_layer(base, t, x, code, code_row, kv, cot, attn, cross, ffn, up_shape, down_shape, carried):
    d = x.shape[1]
    ff = down_shape[0]
    n = IMG_MB * PATCHES
    nb = t // BLOCK
    counts = [len(unit.arrays) for unit in (attn, cross, ffn)]

    def kernel(tab_ref, io, x_ref, code_ref, code_row_ref, kv_ref, cot_ref, *refs):
        attn_refs, refs = taken(refs, counts[0])
        cross_refs, refs = taken(refs, counts[1])
        ffn_refs, refs = taken(refs, counts[2])
        outs, scratch = taken(refs, 19)
        (y, dxb, h, o, m, g, dy, du, fsum, ch, co, cdy, cdq, cdkv, csum, dx0, dy1, dqkv, asum) = outs
        (wa, wc, up, down, va, vf, vc, x1, qkv, p, cq, cp, x2, slope, dx2, dx1, sa, sc, sf) = scratch
        io.fetch(x_ref, code_ref, code_row_ref)
        finish(begin(attn, tab_ref, attn_refs, (wa,), sa))
        cross_copies = begin(cross, tab_ref, cross_refs, (wc,), sc)
        io.fetch(kv_ref)
        vector_rows(wa.at[:, 4 * d : 4 * d + PAIR], va, vf)
        io.need(x_ref, code_ref, code_row_ref)
        self_fwd_kernel(x_ref, va, code_ref, code_row_ref, wa, x1, h, qkv, p, o)
        ffn_copies = begin(ffn, tab_ref, ffn_refs, (up, down), sf)
        io.fetch(cot_ref)
        io.flush(h, o)
        io.need(kv_ref)
        finish(cross_copies)
        vector_rows(wc.at[:, 4 * d : 4 * d + PAIR], vc)
        cross_fwd_kernel(x1, vc, code_ref, kv_ref, wc, x2, ch, cq, cp, co)
        io.flush(ch, co)
        finish(ffn_copies)
        ffn_fwd_kernel(x2, vf, up, down, y, m, g, slope)
        io.flush(y, m, g)
        io.need(cot_ref)
        ffn_bwd_kernel(x2, cot_ref, None, vf, slope, up, down, dx2, dy, du, fsum)
        io.flush(dy, du, fsum)
        cross_bwd_kernel(x1, dx2, vc, code_ref, cq, cp, kv_ref, wc, dx1, cdy, cdq, cdkv, csum)
        io.flush(cdy, cdq, cdkv, csum)
        self_bwd_kernel(x_ref, dx1, va, qkv, p, wa, dxb, dx0, dy1, dqkv, asum)

    def rows(wide, dtype=BF16):
        return ((t, wide), dtype, rows_at(base, BLOCK, wide))

    sums = ((nb, 8, d), F32, sums_at(base, d))
    own = ((BLOCK, d), BF16, rows_at(0, BLOCK, d))
    return Stage(
        kernel,
        1,
        1,
        [
            (x, rows_at(0, BLOCK, d)),
            (code, rows_at(base, BLOCK, 2)),
            (code_row, code_at(base)),
            (kv, rows_at(base, n, 2 * d)),
            (cot, rows_at(base, BLOCK, d)),
        ],
        [own, own, rows(d), rows(d), rows(d), rows(ff), rows(d), rows(ff), sums]
        + [rows(d), rows(d), rows(d), rows(d), ((nb * n, 2 * d), BF16, rows_at(base, n, 2 * d)), sums]
        + [rows(d, F32), rows(d), rows(3 * d), sums],
        (BLOCK * d * 24 * d, d * d * 40),
        (attn, cross, ffn),
        (
            vmem((d, 4 * d + PAIR)),
            vmem((d, 4 * d + PAIR)),
            vmem(up_shape),
            vmem(down_shape),
            vmem((8, d), F32),
            vmem((8, d), F32),
            vmem((8, d), F32),
            vmem((BLOCK, d), F32),
            vmem((BLOCK, 3 * d)),
            vmem((BLOCK, HEADS * TILE)),
            vmem((BLOCK, d)),
            vmem((HEADS, BLOCK, -(-PATCHES // PAIR) * PAIR)),
            vmem((BLOCK, d), F32),
            vmem((BLOCK, ff)),
            vmem((BLOCK, d), F32),
            vmem((BLOCK, d), F32),
            dma(attn),
            dma(cross),
            dma(ffn),
        ),
        carried,
        manual=True,
        lazy=True,
    )


def first_back(base, x1, cot, more, slope, x, qkv, probs, attn, ffn, up_shape, down_shape, carried):
    t, d = x.shape
    ff = down_shape[0]
    nb = t // BLOCK
    counts = [len(unit.arrays) for unit in (attn, ffn)]

    def kernel(tab_ref, io, x1_ref, cot_ref, more_ref, slope_ref, x_ref, qkv_ref, p_ref, *refs):
        attn_refs, refs = taken(refs, counts[0])
        ffn_refs, refs = taken(refs, counts[1])
        (dy, du, fsum, dx0, dy1, dqkv, asum), scratch = taken(refs, 7)
        wa, up, down, va, vf, dx1, dxb, sa, sf = scratch
        ffn_copies = begin(ffn, tab_ref, ffn_refs, (up, down), sf)
        finish(begin(attn, tab_ref, attn_refs, (wa,), sa))
        vector_rows(wa.at[:, 4 * d : 4 * d + PAIR], va, vf)
        finish(ffn_copies)
        io.need(x1_ref, cot_ref, more_ref, slope_ref)
        ffn_bwd_kernel(x1_ref, cot_ref, more_ref, vf, slope_ref, up, down, dx1, dy, du, fsum)
        io.flush(dy, du, fsum)
        io.need(x_ref, qkv_ref, p_ref)
        self_bwd_kernel(x_ref, dx1, va, qkv_ref, p_ref, wa, dxb, dx0, dy1, dqkv, asum)

    def rows(wide, dtype=BF16):
        return ((t, wide), dtype, rows_at(base, BLOCK, wide))

    sums = ((nb, 8, d), F32, sums_at(base, d))
    here = rows_at(base, BLOCK, d)
    return Stage(
        kernel,
        0,
        1,
        [
            (x1, here),
            (cot, here),
            (more, rows_at(0, BLOCK, d)),
            (slope, rows_at(base, BLOCK, ff)),
            (x, here),
            (qkv, rows_at(base, BLOCK, 3 * d)),
            (probs, rows_at(base, BLOCK, HEADS * TILE)),
        ],
        [rows(d), rows(ff), sums, rows(d, F32), rows(d), rows(3 * d), sums],
        (BLOCK * d * 12 * d, d * d * 24),
        (attn, ffn),
        (
            vmem((d, 4 * d + PAIR)),
            vmem(up_shape),
            vmem(down_shape),
            vmem((8, d), F32),
            vmem((8, d), F32),
            vmem((BLOCK, d), F32),
            vmem((BLOCK, d)),
            dma(attn),
            dma(ffn),
        ),
        carried,
        manual=True,
    )


def first_feed_back(base, x1, cot, more, slope, ffn, vecs, up_shape, down_shape, carried):
    t, d = x1.shape
    ff = down_shape[0]
    nb = t // BLOCK

    def kernel(tab_ref, io, x1_ref, cot_ref, more_ref, slope_ref, *refs):
        pieces, refs = taken(refs, len(ffn.arrays))
        tables, refs = taken(refs, len(vecs.arrays))
        (dx1, dy, du, fsum), (up, down, table, va, vf, sf, sv) = taken(refs, 4)
        each = len(ffn.moves) // (up_shape[0] + 1)
        turned = Unit(ffn.arrays, list(ffn.moves[-each:]) + list(ffn.moves[:-each]))
        finish(begin(vecs, tab_ref, tables, (table,), sv))
        copies = begin(turned, tab_ref, pieces, (up, down), sf)
        vector_rows(table, va, vf)
        io.need(x1_ref, cot_ref, more_ref, slope_ref)
        finish(copies[:each])

        def ready(j):
            finish(copies[(j + 1) * each : (j + 2) * each])

        ffn_bwd_kernel(x1_ref, cot_ref, more_ref, vf, slope_ref, up, down, dx1, dy, du, fsum, ready=ready)

    here = rows_at(base, BLOCK, d)
    return Stage(
        kernel,
        0,
        1,
        [(x1, here), (cot, here), (more, rows_at(0, BLOCK, d)), (slope, rows_at(base, BLOCK, ff))],
        [
            ((BLOCK, d), F32, rows_at(0, BLOCK, d)),
            ((t, d), BF16, here),
            ((t, ff), BF16, rows_at(base, BLOCK, ff)),
            ((nb, 8, d), F32, sums_at(base, d)),
        ],
        (BLOCK * d * 4 * ff, d * d * 16),
        (ffn, vecs),
        (
            vmem(up_shape),
            vmem(down_shape),
            vmem((d, PAIR)),
            vmem((8, d), F32),
            vmem((8, d), F32),
            dma(ffn),
            dma(vecs),
        ),
        carried,
        manual=True,
    )


def first_attention_back(base, x, dx1, qkv, probs, attn, carried):
    t, d = x.shape
    nb = t // BLOCK

    def kernel(tab_ref, io, x_ref, dx1_ref, qkv_ref, p_ref, *refs):
        pieces, refs = taken(refs, len(attn.arrays))
        (dx0, dy1, dqkv, asum), (wa, va, dxb, sa) = taken(refs, 4)
        finish(begin(attn, tab_ref, pieces, (wa,), sa))
        vector_rows(wa.at[:, 4 * d : 4 * d + PAIR], va)
        io.need(x_ref, dx1_ref, qkv_ref, p_ref)
        self_bwd_kernel(x_ref, dx1_ref, va, qkv_ref, p_ref, wa, dxb, dx0, dy1, dqkv, asum)

    here = rows_at(base, BLOCK, d)
    return Stage(
        kernel,
        0,
        1,
        [
            (x, here),
            (dx1, rows_at(0, BLOCK, d)),
            (qkv, rows_at(base, BLOCK, 3 * d)),
            (probs, rows_at(base, BLOCK, HEADS * TILE)),
        ],
        [
            ((t, d), F32, here),
            ((t, d), BF16, here),
            ((t, 3 * d), BF16, rows_at(base, BLOCK, 3 * d)),
            ((nb, 8, d), F32, sums_at(base, d)),
        ],
        (BLOCK * d * 8 * d, d * d * 8),
        (attn,),
        (vmem((d, 4 * d + PAIR)), vmem((8, d), F32), vmem((BLOCK, d)), dma(attn)),
        carried,
        manual=True,
    )


def with_unit(kernel, unit, outs):
    def own(tab_ref, io, x_ref, *refs):
        pieces, refs = taken(refs, len(unit.arrays))
        out_refs, (w_ref, sems) = taken(refs, outs)
        finish(begin(unit, tab_ref, pieces, (w_ref,), sems))
        io.need(x_ref)
        for j in range(x_ref.shape[0] // PATCHES):
            rows = pl.ds(j * PATCHES, PATCHES)
            kernel(x_ref.at[rows], w_ref, *[ref.at[rows] for ref in out_refs])

    return own


def image_kv(patches, unit):
    n, d = patches.shape
    return Stage(
        with_unit(kv_kernel, unit, 1),
        1,
        1,
        [(patches, rows_at(0, n, d))],
        [((n, 2 * d), BF16, rows_at(0, n, 2 * d))],
        (n * d * d * 4, n * d * 6 + d * d * 4),
        (unit,),
        (vmem((d, 2 * d)), dma(unit)),
        manual=True,
    )


def image_back(dkv, unit):
    n, d = dkv.shape[0], dkv.shape[1] // 2
    return Stage(
        with_unit(image_back_kernel, unit, 2),
        1,
        1,
        [(dkv, rows_at(0, n, 2 * d))],
        [
            ((n, d // 2), BF16, rows_at(0, n, d // 2)),
            ((n, d // 2), F32, rows_at(0, n, d // 2)),
        ],
        (n * d * d * 4, n * d * 7 + d * d * 4),
        (unit,),
        (vmem((d, 2 * d)), dma(unit)),
        manual=True,
    )


def columns_of(section, rows, cols):
    def index(i, tab):
        return (0, i * (tab[0] if section else 1 - tab[0]))

    return pl.BlockSpec((rows, cols), index)


def sums_of(section, shape):
    def index(i, tab):
        return (0, 0, i * (tab[0] if section else 1 - tab[0]))

    return pl.BlockSpec(shape, index)


def either(kernel, sets, specs, outs, cost, cuts):
    n = len(specs)

    def own(tab_ref, io, *refs):
        first, refs = taken(refs, n)
        second, refs = taken(refs, n)
        out_refs, refs = taken(refs, len(outs))
        to, sems = refs[:n], refs[n]

        def fetched(source):
            return [pltpu.make_async_copy(ref, one, sems.at[j]) for j, (ref, one) in enumerate(zip(source, to))]

        for section, source in enumerate((first, second)):

            @pl.when(tab_ref[0] == section)
            def _(source=source):
                for copy in fetched(source):
                    copy.start()

        waiting = Transfers(list(zip(fetched(first), to)), io.outgoing)
        waiting.begun = list(to)
        kernel(tab_ref, waiting, *to, *out_refs)
        waiting.need(*[ref for _, ref in waiting.incoming])
        io.outgoing, io.sent = waiting.outgoing, waiting.sent

    return Stage(
        own,
        None,
        1,
        [],
        outs,
        cost,
        (Unit(list(sets[0]), ()), Unit(list(sets[1]), ())),
        tuple(pltpu.VMEM(array.shape, array.dtype) for array in sets[0]) + (pltpu.SemaphoreType.DMA((n,)),),
        manual=True,
        cuts=cuts,
    )


def ffn_grads(tab, sets, after=()):
    t, d = sets[0][0].shape
    ff = sets[0][2].shape[1]
    shape = (RING, (ff + 4 * d) // (RING * CORES), d)
    stage = either(
        ffn_grads_kernel,
        sets,
        sets[0],
        [(shape, BF16, whole_spec(shape))] * 2,
        (t * d * ff * 4, t * (ff + d) * 4 + d * ff * 4),
        (1, (ff // d * d // (RING * CORES), shape[1])),
    )
    return run(tab, [stage], after)[0]


def attn_grads(tab, sets, after=()):
    t, d = sets[0][0].shape
    shape = (RING, d // (RING * CORES), 4 * d + PAIR)
    stage = either(
        attn_grads_kernel,
        sets,
        sets[0],
        [(shape, BF16, whole_spec(shape))] * 2,
        (t * d * d * 8, t * d * 12 + d * d * 8),
        (2, (3 * d, shape[2])),
    )
    return run(tab, [stage], after)[0]


def cross_grads(h, dq, patches, dkv, o, dyb, sums):
    t, d = h.shape
    n = patches.shape[0]
    wide = 4 * d + PAIR
    shape = (2 * RING, d // (2 * RING * CORES), wide)
    return Stage(
        cross_grads_kernel,
        1,
        1,
        [
            (h, rows_at(0, t, d)),
            (dq, rows_at(0, t, d)),
            (o, rows_at(0, t, d)),
            (dyb, rows_at(0, t, d)),
            (sums, whole_spec(sums.shape)),
            (patches, rows_at(0, n, d)),
            (dkv, rows_at(0, n, 2 * d)),
        ],
        [(shape, BF16, whole_spec(shape))] * 2,
        (t * d * d * 4 + n * d * d * 4, t * d * 8 + n * d * 6 + d * d * 8),
        manual=True,
    )


def at_offset(tab, offset):
    return tab[2 + RING // 2 + offset]


def join_kernel(tab_ref, *refs, extra, moving, cuts):
    mine_ref, theirs_ref = refs[:2]
    moving_refs, out_refs = taken(refs[2 + extra :], moving)
    rows = mine_ref.shape[1]
    parts = [(0, mine_ref[0].astype(F32) + theirs_ref[0].astype(F32))]
    if extra:
        parts.append((rows, jnp.where(tab_ref[0] == 0, refs[2][0], refs[3][0]).astype(F32)))
    for start, value in parts:
        for ref in moving_refs:
            value = value + ref[start : start + value.shape[0], :].astype(F32)
        for out, row, at, first, count, column, columns in cuts:
            if start <= first < start + value.shape[0]:
                piece = value[first - start : first - start + count, column : column + columns]
                out_refs[out][row : row + count, at : at + columns] = piece.astype(out_refs[out].dtype)


def join(tab, offset, mine, theirs, extra, moving, dtype, after=(), cuts=None):
    cols = mine.shape[2]
    rows = mine.shape[1] + (extra[0].shape[1] if extra else 0)

    def part(array):
        return (array, pl.BlockSpec((1,) + array.shape[1:], lambda i, tab: (at_offset(tab, offset), 0, 0)))

    if cuts is None:
        cuts = [(0, 0, 0, 0, mine.shape[1], 0, cols)]
        if extra:
            cuts.append((0, mine.shape[1], 0, mine.shape[1], extra[0].shape[1], 0, cols))
    shapes = {}
    for out, row, at, _, count, _, columns in cuts:
        have = shapes.get(out, (0, 0))
        shapes[out] = (max(row + count, have[0]), max(at + columns, have[1]))
    shapes = [shapes[out] for out in range(len(shapes))]
    results = call(
        partial(join_kernel, extra=len(extra), moving=len(moving), cuts=cuts),
        (tab, None),
        1,
        [part(array) for array in (mine, theirs) + tuple(extra)]
        + [(array, pl.BlockSpec((rows, cols), lambda i, tab: (0, 0))) for array in moving],
        [(shape, dtype, pl.BlockSpec(shape, lambda i, tab: (0, 0))) for shape in shapes],
        rows * cols * 3,
        rows * cols * 2 * (3 + len(moving)),
        after=after,
        vmem_limit=SMALL_LIMIT,
    )
    return results[0] if len(shapes) == 1 else results


def cross_join_kernel(tab_ref, io, mine_ref, theirs_ref, first_ref, second_ref):
    io.need(mine_ref, theirs_ref)
    first_ref[...] = (mine_ref[:RING].astype(F32) + theirs_ref[:RING].astype(F32)).astype(BF16)
    io.flush(first_ref)
    second_ref[...] = (mine_ref[RING:].astype(F32) + theirs_ref[RING:].astype(F32)).astype(BF16)


def cross_join(mine, theirs):
    shape = (RING,) + mine.shape[1:]
    return Stage(
        cross_join_kernel,
        1,
        1,
        [(mine, whole_spec(mine.shape)), (theirs, whole_spec(theirs.shape))],
        [(shape, BF16, whole_spec(shape))] * 2,
        (mine.size, mine.size * 6),
        manual=True,
    )


def widen_kernel(tab_ref, io, x_ref, out_ref):
    io.need(x_ref)
    out_ref[...] = x_ref[...].astype(F32)


def widen(x, buffer):
    block = whole_spec(x.shape)
    return Stage(
        widen_kernel, 0, 1, [(x, block)], [(x.shape, F32, block)], (0, x.size * 6), carried=(buffer,), manual=True
    )


def relay_kernel(tab_ref, x_ref, out_ref):
    out_ref[...] = x_ref[...]


def relay(x):
    spec = pl.BlockSpec(x.shape, lambda i, tab: (0, 0))
    return Stage(relay_kernel, 1, 1, [(x, spec)], [(x.shape, x.dtype, spec)], (0, x.size * 4))


def pack_kernel(tab_ref, *refs):
    pieces, out_ref = refs[:-1], refs[-1]
    rows = pieces[0].shape[0]
    for j, ref in enumerate(pieces):
        out_ref[j * rows : (j + 1) * rows, :] = ref[...]


def pack(pieces):
    rows, cols = pieces[0].shape
    shape = (len(pieces) * rows, cols)
    return Stage(
        pack_kernel,
        1,
        1,
        [(piece, pl.BlockSpec((rows, cols), lambda i, tab: (0, 0))) for piece in pieces],
        [(shape, BF16, pl.BlockSpec(shape, lambda i, tab: (0, 0)))],
        (0, rows * cols * len(pieces) * 4),
    )


def ring_tables():
    half = RING // 2
    return [2 * z for z in range(half)] + [2 * z + 1 for z in range(half - 1, -1, -1)]


CHIP_AT = ring_tables()


def flat(section, chip, core):
    return section * RING * CORES + chip * CORES + core


def ring_pairs(sections, step):
    return [
        (flat(s, CHIP_AT[i], c), flat(s, CHIP_AT[(i + step) % RING], c))
        for s in sections
        for i in range(RING)
        for c in range(CORES)
    ]


def core_pairs(sections):
    return [
        (flat(s, chip, c), flat(s, chip, 1 - c))
        for s in sections
        for chip in range(RING)
        for c in range(CORES)
    ]


def send(x, pairs):
    return lax.ppermute(x, ("section", "dp"), pairs)


def device_table():
    rank = lax.axis_index("dp")
    chip = rank // CORES % RING
    half = RING // 2
    pos = jnp.where(chip % 2 == 0, chip // 2, RING - 1 - chip // 2)
    slot = lax.iota(jnp.int32, RING + 3)
    at = (pos + slot - 2 - half + RING) % RING
    chips = jnp.where(at < half, 2 * at, 2 * (RING - 1 - at) + 1)
    return jnp.where(slot == 0, lax.axis_index("section"), jnp.where(slot == 1, rank % CORES, chips)).astype(jnp.int32)


class Gather:
    def __init__(self, chunk, sections, long_way, by_core):
        self.chunk, self.sections, self.long_way, self.by_core = chunk, sections, long_way, by_core
        self.arrived = {1: [], -1: []}

    def step(self):
        done = len(self.arrived[self.long_way])
        ways = [way for way in (1, -1) if done < RING // 2 - 1 or way == self.long_way]
        held = {way: self.arrived[way][-1] if done else self.chunk for way in ways}
        for way in ways:
            self.arrived[way].append(send(held[way], ring_pairs(self.sections, way)))

    def last_step(self, held):
        self.arrived[self.long_way].append(send(held, ring_pairs(self.sections, self.long_way)))

    def own_pieces(self):
        held = [(0, self.chunk)]
        for step in range(1, RING // 2 + 1):
            held += [
                (-way * step, self.arrived[way][step - 1]) for way in (1, -1) if step <= len(self.arrived[way])
            ]
        return held

    def pieces(self):
        pieces, places = [], []
        for offset, piece in self.own_pieces():
            pieces += [piece, send(piece, core_pairs(self.sections))]
            places += [(offset, False, self.by_core), (offset, True, self.by_core)]
        return pieces, tuple(places)


class Order:
    def __init__(self):
        self.last = ()

    def mark(self, *outputs):
        self.last = outputs
        return outputs[0]


class Scatter:
    def __init__(self, tab, order, mine, out, sections, long_way, extra=()):
        self.tab, self.order, self.mine = tab, order, mine
        self.sections, self.long_way, self.extra = sections, long_way, extra
        self.theirs = send(out, core_pairs(sections))
        self.moving = {1: [], -1: []}
        self.done = 0

    def step(self):
        for way in (1, -1):
            hops = RING // 2 if way == self.long_way else RING // 2 - 1
            if self.done < hops:
                piece = join(
                    self.tab,
                    way * (hops - self.done),
                    self.mine,
                    self.theirs,
                    self.extra,
                    self.moving[way],
                    BF16,
                    self.order.last,
                )
                self.order.mark(piece)
                self.moving[way] = [send(piece, ring_pairs(self.sections, way))]
        self.done += 1

    def finish(self, cuts):
        moving = self.moving[1] + self.moving[-1]
        results = join(self.tab, 0, self.mine, self.theirs, self.extra, moving, F32, self.order.last, cuts)
        self.order.mark(results[0])
        return results


def lanes_of(vectors, width):
    table = jnp.stack(vectors, axis=1)
    return jnp.pad(table, ((0, 0), (0, width - table.shape[1])))


def local(
    tokens,
    images,
    segments,
    image_ids,
    cotangent,
    norm_gain,
    norm_bias,
    qkv_weight,
    out_weight,
    up_weight,
    down_weight,
    cross_gain,
    cross_bias,
    cross_query,
    cross_kv,
    cross_out,
):
    section = lax.axis_index("section")
    multimodal = section == 1
    tab = device_table()
    t, d = tokens.shape
    ff = up_weight.shape[2]
    nb = t // BLOCK
    members = lax.axis_size("dp")
    ringed = members == RING * CORES and lax.axis_size("section") == 2
    up_rows, down_rows = up_weight.shape[1], down_weight.shape[1]
    split = ff // d

    attn_piece = jnp.concatenate(
        [
            qkv_weight[0],
            out_weight[0],
            lanes_of([norm_gain[0, 0], norm_bias[0, 0], norm_gain[0, 1], norm_bias[0, 1]], PAIR),
        ],
        axis=1,
    ).astype(BF16)
    ffn_piece = jnp.concatenate(
        [up_weight[0, :, j * d : (j + 1) * d] for j in range(split)] + [down_weight[0]], axis=0
    ).astype(BF16)
    cross_piece = jnp.concatenate(
        [cross_query, cross_kv, cross_out, lanes_of([cross_gain, cross_bias], PAIR)], axis=1
    ).astype(BF16)

    row_in_tile = lax.broadcasted_iota(jnp.int32, segments.shape, 0) % (TILE // ROW_LEN)
    code = row_in_tile * (SEGS + 1) + segments
    code_row = code.reshape(nb, 1, BLOCK)
    slots = lax.broadcasted_iota(jnp.int32, (1, 1, SEGS), 2)
    token_image = jnp.sum(
        jnp.where(segments[:, :, None] == slots, image_ids[:, None, :], 0), axis=-1
    )
    codes = jnp.stack([code, token_image], axis=-1).reshape(-1, 2)
    patches = images.reshape(-1, d)

    up_shape, down_shape = (split, d, d), (ff, d)
    cot = cotangent[0]
    order = Order()
    if ringed:
        both, s1 = (0, 1), (1,)
        attn_ring = Gather(attn_piece, both, 1, False)
        ffn_ring = Gather(ffn_piece, both, -1, False)
        for _ in range(RING // 2):
            attn_ring.step()
            ffn_ring.step()
        w_cross = lax.all_gather(cross_piece, ("section", "dp"), axis=0, tiled=True)

        def unit_of(ring, layout):
            pieces, places = ring.pieces()
            moves = [
                (j, start, rows, cols, target, lead, place)
                for start, rows, cols, target, lead in layout
                for j, place in enumerate(places)
            ]
            return Unit(pieces, moves)

        def columns_of_unit(unit, cols):
            return Unit(unit.arrays, [move[:3] + (cols,) + move[4:] for move in unit.moves])

        attn = unit_of(attn_ring, [(0, up_rows, None, 0, None)])
        ffn = unit_of(
            ffn_ring,
            [(j * up_rows, up_rows, None, 0, j) for j in range(split)]
            + [(split * up_rows, down_rows, None, 1, None)],
        )
        cross = Unit([w_cross], [(0, 0, d, None, 0, None, None)])
    else:
        w_attn = lax.all_gather(attn_piece, "dp", axis=0, tiled=True)
        w_ffn = lax.all_gather(ffn_piece, "dp", axis=0, tiled=False)
        w_up = w_ffn[:, : split * up_rows].reshape(members, split, up_rows, d).swapaxes(0, 1).reshape(up_shape)
        w_down = w_ffn[:, split * up_rows :].reshape(down_shape)
        w_cross = lax.all_gather(cross_piece, ("section", "dp"), axis=0, tiled=True)

        def columns_of_unit(unit, cols):
            return Unit(unit.arrays, [move[:3] + (cols,) + move[4:] for move in unit.moves])

        attn = Unit([w_attn], [(0, 0, d, None, 0, None, None)])
        cross = Unit([w_cross], [(0, 0, d, None, 0, None, None)])
        ffn = Unit(
            [w_up.reshape(split * d, d), w_down],
            [(0, j * d, d, None, 0, j, None) for j in range(split)] + [(1, 0, ff, None, 1, None, None)],
        )
    vecs = columns_of_unit(attn, (4 * d, PAIR))
    kv_unit = columns_of_unit(cross, (d, 2 * d))
    a_y, kept, held = [], (), ()
    for b in range(nb):
        (held,) = run(tab, [first_attention(b, tokens, codes, code_row, attn, held)], a_y)
        a_x1 = held[0]
        stages = [first_feed(b, a_x1, ffn, vecs, up_shape, down_shape, kept)]
        if b == nb - 1:
            stages.append(image_kv(patches, kv_unit))
        (y, *kept), *more = run(tab, stages, a_y)
        a_y.append(y)
    a_x1, a_h, a_qkv, a_p, a_o = held
    a_m, a_g, a_slope = kept
    ((kv,),) = more
    arrived = [lax.ppermute(y, "section", [(0, 1)]) for y in a_y]

    b_y, leaving, kept = [], [], ()
    for b in range(nb):
        ((y, low, *kept),) = run(
            tab,
            [
                second_layer(
                    b, t, arrived[b], codes, code_row, kv, cot, attn, cross, ffn, up_shape, down_shape, kept
                )
            ],
        )
        b_y.append(y)
        leaving.append(low)
    (b_h, b_o, b_m, b_g, b_dy, b_du, b_fsum, c_h, c_o, c_dy, c_dq, c_dkv, c_sum) = kept[:13]
    b_dx0, b_dy1, b_dqkv, b_asum = kept[13:]
    returning = [lax.ppermute(low, "section", [(1, 0)]) for low in leaving]

    def layer_zero_back(b, kept):
        return first_back(
            b, a_x1, cot, returning[b], a_slope, tokens, a_qkv, a_p, attn, ffn, up_shape, down_shape, kept
        )

    def cross_terms():
        return jnp.concatenate(
            [dot_tn(c_h, c_dq), dot_tn(patches, c_dkv), dot_tn(c_o, c_dy), columns(c_sum)], axis=1
        )

    def columns(*sums):
        table = jnp.concatenate([jnp.sum(part, axis=0)[:2] for part in sums]).T
        return jnp.pad(table, ((0, 0), (0, PAIR - table.shape[1])))

    if ringed:
        (kept,) = run(tab, [layer_zero_back(0, ())], leaving)
        feed_kept, attn_kept = kept[:3], kept[3:]
        ((c_mine, c_out),) = run(
            tab, [cross_grads(c_h, c_dq, patches, c_dkv, c_o, c_dy, c_sum)], [kept[2]]
        )
        ((a_dx1, a_dy, a_du, a_fsum),) = run(
            tab,
            [first_feed_back(1, a_x1, cot, returning[1], a_slope, ffn, vecs, up_shape, down_shape, feed_kept)],
            [c_mine],
        )
        order.mark(a_dx1)
        c_theirs = send(c_out, core_pairs(s1))
        ffn_mine, ffn_out = ffn_grads(
            tab, ((a_m, a_du, a_g, a_dy), (b_m, b_du, b_g, b_dy)), order.last
        )
        order.mark(ffn_mine)
        ffn_sum = Scatter(tab, order, ffn_mine, ffn_out, both, 1)
        ((c_first, c_second),) = run(tab, [cross_join(c_mine, c_theirs)], order.last)
        order.mark(c_first)
        c_first = lax.ppermute(c_first, "section", [(1, 0)])
        ((a_dx0, a_dy1, a_dqkv, a_asum),) = run(
            tab, [first_attention_back(1, tokens, a_dx1, a_qkv, a_p, attn, attn_kept)], order.last
        )
        order.mark(a_asum)
        attn_mine, attn_out = attn_grads(
            tab,
            (
                (a_h, a_dqkv, a_o, a_dy1, a_asum, a_fsum),
                (b_h, b_dqkv, b_o, b_dy1, b_asum, b_fsum),
            ),
            order.last,
        )
        order.mark(attn_mine)
        ffn_sum.step()
        ((image_theirs, image_mine),) = run(tab, [image_back(c_dkv, kv_unit)], order.last)
        order.mark(image_theirs)
        image_theirs = lax.ppermute(image_theirs, "section", [(1, 0)])
        attn_sum = Scatter(tab, order, attn_mine, attn_out, both, -1, (c_first, c_second))
        while ffn_sum.done < RING // 2:
            ffn_sum.step()
            attn_sum.step()
        ((image_shard,),) = run(tab, [widen(image_theirs, image_mine)], order.last)
        order.mark(image_shard)
        up_g, down_g = ffn_sum.finish(
            [(0, 0, j * d, j * up_rows, up_rows, 0, d) for j in range(split)]
            + [(1, 0, 0, split * up_rows, down_rows, 0, d)]
        )
        attn_sum.step()
        below, few = up_rows, up_rows // 2
        qkv_g, out_g, vec_g, query_g, kv_g, cross_out_g, cross_vec_g = attn_sum.finish(
            [
                (0, 0, 0, 0, up_rows, 0, 3 * d),
                (1, 0, 0, 0, up_rows, 3 * d, d),
                (2, 0, 0, 0, up_rows, 4 * d, PAIR),
                (3, 0, 0, below, few, 0, d),
                (4, 0, 0, below, few, d, 2 * d),
                (5, 0, 0, below, few, 3 * d, d),
                (6, 0, 0, below, few, 4 * d, PAIR),
            ]
        )
    else:

        def summed(first, second):
            grads = jnp.where(multimodal, second, first)
            return lax.psum_scatter(grads, "dp", scatter_dimension=0, tiled=True)

        def ffn_terms(m, du, g, dyb):
            up = dot_tn(m, du).reshape(members, up_rows, split, d).swapaxes(1, 2)
            down = dot_tn(g, dyb).reshape(members, down_rows, d)
            return jnp.concatenate([up.reshape(members, split * up_rows, d), down], axis=1)

        def attn_terms(h, dqkv, o, dyb, asum, fsum):
            return jnp.concatenate([dot_tn(h, dqkv), dot_tn(o, dyb), columns(asum, fsum)], axis=1)

        kept = ()
        for b in range(nb):
            (kept,) = run(tab, [layer_zero_back(b, kept)])
        a_dy, a_du, a_fsum, a_dx0, a_dy1, a_dqkv, a_asum = kept
        ((image_theirs, image_mine),) = run(tab, [image_back(c_dkv, kv_unit)])
        image_theirs = lax.ppermute(image_theirs, "section", [(1, 0)])
        image_shard = jnp.where(multimodal, image_mine, image_theirs.astype(F32))
        ffn_g = summed(ffn_terms(a_m, a_du, a_g, a_dy), ffn_terms(b_m, b_du, b_g, b_dy))[0]
        attn_g = summed(
            attn_terms(a_h, a_dqkv, a_o, a_dy1, a_asum, a_fsum),
            attn_terms(b_h, b_dqkv, b_o, b_dy1, b_asum, b_fsum),
        )
        cross_g = lax.psum_scatter(
            jnp.where(multimodal, cross_terms(), 0.0),
            ("section", "dp"),
            scatter_dimension=0,
            tiled=True,
        )
        qkv_g, out_g, vec_g = attn_g[:, : 3 * d], attn_g[:, 3 * d : 4 * d], attn_g[:, 4 * d :]
        query_g, kv_g, cross_out_g = cross_g[:, :d], cross_g[:, d : 3 * d], cross_g[:, 3 * d : 4 * d]
        cross_vec_g = cross_g[:, 4 * d :]
        up_g = jnp.concatenate([ffn_g[j * up_rows : (j + 1) * up_rows] for j in range(split)], axis=1)
        down_g = ffn_g[split * up_rows :]

    return (
        jnp.where(multimodal, jnp.concatenate(b_y), jnp.concatenate(a_y))[None],
        jnp.where(multimodal, b_dx0, a_dx0)[None],
        image_shard.reshape(images.shape[0], images.shape[1], d // 2),
        vec_g[:, 0:4:2].T[None],
        vec_g[:, 1:4:2].T[None],
        qkv_g[None],
        out_g[None],
        up_g[None],
        down_g[None],
        cross_vec_g[:, 0],
        cross_vec_g[:, 1],
        query_g,
        kv_g,
        cross_out_g,
    )


def solution(mesh):
    in_specs = (
        P("dp", None),
        P("dp", None, None),
        P("dp", None),
        P("dp", None),
        P("section", "dp", None),
        P("section", None, "dp"),
        P("section", None, "dp"),
        P("section", "dp", None),
        P("section", "dp", None),
        P("section", "dp", None),
        P("section", "dp", None),
        P(("section", "dp")),
        P(("section", "dp")),
        P(("section", "dp"), None),
        P(("section", "dp"), None),
        P(("section", "dp"), None),
    )
    out_specs = (
        P("section", "dp", None),
        P("section", "dp", None),
        P("dp", None, "section"),
        P("section", None, "dp"),
        P("section", None, "dp"),
        P("section", "dp", None),
        P("section", "dp", None),
        P("section", "dp", None),
        P("section", "dp", None),
        P(("section", "dp")),
        P(("section", "dp")),
        P(("section", "dp"), None),
        P(("section", "dp"), None),
        P(("section", "dp"), None),
    )
    return jax.shard_map(local, mesh=mesh, in_specs=in_specs, out_specs=out_specs, check_vma=False)
```
